32 devices in a mesh: face: 4 (over z), dom: 8 (over y, x, core).
Axes of the slice: x: 2, y: 2, z: 4, core: 2. Of those that a mesh axis runs over, the one named last changes fastest.
Arguments:
- prognostic: float32 [2, 64, 384, 1024], P(None, None, 'face', 'dom'), may hold values from -6 to 6
- velocity: bfloat16 [2, 64, 384, 1024], P(None, None, 'face', 'dom'), may hold values from -4 to 4
- jacobian: float32 [96, 256], P('face', 'dom'), may hold values from 0.5 to 2
- element_span: int32 [96, 256], P('face', 'dom'), may hold values from 0 to 31, as said below
- sunlit: int32 [96, 256], P('face', 'dom'), may hold values from 0 to 1, as said below
- first_weight: bfloat16 [128, 512], replicated, may hold values from -0.5 to 0.5
- first_bias: float32 [512], replicated, may hold values from -3 to 3
- second_weight: bfloat16 [512, 512], replicated, may hold values from -0.25 to 0.25
- second_bias: float32 [512], replicated, may hold values from -3 to 3
- third_weight: bfloat16 [512, 512], replicated, may hold values from -0.25 to 0.25
- third_bias: float32 [512], replicated, may hold values from -3 to 3
- output_weight: bfloat16 [512, 128], replicated, may hold values from -0.25 to 0.25
- output_bias: float32 [128], replicated, may hold values from -3 to 3
- solar_inner: bfloat16 [128, 512], replicated, may hold values from -0.5 to 0.5
- solar_inner_bias: float32 [512], replicated, may hold values from -3 to 3
- solar_middle: bfloat16 [512, 512], replicated, may hold values from -0.25 to 0.25
- solar_middle_bias: float32 [512], replicated, may hold values from -3 to 3
- solar_outer: bfloat16 [512, 128], replicated, may hold values from -0.25 to 0.25
- solar_outer_bias: float32 [128], replicated, may hold values from -3 to 3
Outputs:
- new_state: float32 [2, 64, 384, 1024], P(None, None, 'face', 'dom')
- span_state: bfloat16 [98304, 128], P(('face', 'dom'))
The draws below stay inside these ranges and needn't reach their ends.
Inputs may be any that keep to these rules, and one draw needn't show every extreme that they name: `element_span`: span c lives on device c (face index slowest). Every span receives exactly 768 elements, half of them sunlit; one device sends at most 48 elements to one span, and 48 is reached. sunlit is the same for all elements of one device, and is 1 on half of the devices.
All inputs are finite; a program needn't handle non-finite values.
Results may differ from the reference program's by a relative error of at most 0.0025.
Values may be sent and summed in bfloat16 or wider, within the bound.
No kernel may reach another device: no remote copies, remote signals or barrier semaphores. Data moves between devices by JAX's collectives and lax.ppermute only.
A program may use at most 128 MiB of HBM per device.

```python
import math
import jax
import jax.numpy as jnp
import numpy as np
from jax import lax

NV = 2
LEV = 64
HIDDEN_SIZE = 512
EX = 24
EY = 32
FEAT = 128
CAP = 48
N_FACE = 4
N_DOM = 8


def spread_counts(key, groups, total, limit):
    first_key, second_key = jax.random.split(key)
    slots = (groups - 1) * limit
    ordering = jax.random.permutation(first_key, slots)
    extra = (ordering < total - limit).astype(jnp.int32).reshape(groups - 1, limit).sum(axis=1)
    counts = jnp.concatenate([jnp.full((1,), limit, jnp.int32), extra])
    return jnp.roll(counts, jax.random.randint(second_key, (), 0, groups))


def grid_layout(values):
    return values.reshape(N_FACE, N_DOM, EX, EY).transpose(0, 2, 1, 3).reshape(N_FACE * EX, N_DOM * EY)


def joint_assignment(key):
    devices = N_FACE * N_DOM
    elements = EX * EY
    subkeys = jax.random.split(key, 5)
    even_counts = spread_counts(subkeys[0], devices // 2, elements // 2, CAP)
    odd_counts = spread_counts(subkeys[1], devices // 2, elements // 2, CAP)
    counts = jnp.stack([even_counts, odd_counts], axis=1).reshape(devices)
    boundary = jnp.cumsum(counts)
    run_index = jnp.sum((boundary[None, :] <= jnp.arange(elements)[:, None]).astype(jnp.int32), axis=1)
    shifted = jax.random.permutation(subkeys[2], devices)
    renamed = jax.random.permutation(subkeys[3], devices)
    orders = jax.vmap(lambda k: jax.random.permutation(k, elements))(jax.random.split(subkeys[4], devices))
    runs = run_index[orders]
    target = renamed[(shifted[:, None] + runs) % devices]
    sunlit_flags = jnp.broadcast_to((shifted % 2 == 0).astype(jnp.int32)[:, None], (devices, elements))
    return (grid_layout(target.astype(jnp.int32)), grid_layout(sunlit_flags))


def draw_element_span(key, part):
    target, sunlit_flags = joint_assignment(key)
    return target


def draw_sunlit(key, part):
    target, sunlit_flags = joint_assignment(key)
    return sunlit_flags


def block_scale(own_key, dims, cuts, smallest, top_value):
    loudness = 1.0
    for axis_at, shards_of in cuts:
        heights = jax.random.uniform(jax.random.fold_in(jax.random.fold_in(own_key, 6), axis_at), (shards_of,), jnp.float32, smallest / len(cuts), top_value / len(cuts))
        loudness = loudness * jnp.repeat(jnp.exp(heights), dims[axis_at] // shards_of).reshape((-1,) + (1,) * (len(dims) - 1 - axis_at))
    return loudness


def normal_values(own_key, extent, scale, most, cuts=(), dtype=jnp.bfloat16):
    values = jax.random.normal(own_key, extent, jnp.float32) * scale
    if len(cuts) > 0:
        values = block_scale(own_key, extent, cuts, -0.22, 0.18) * values
    return jnp.clip(values, min=-most, max=most).astype(dtype)


def setup_inputs(seed: int = 0) -> dict:
    arg_keys = jax.random.split(jax.random.key(seed), 20)
    prognostic = normal_values(arg_keys[0], (NV, LEV, 4 * EX * N_FACE, 4 * EY * N_DOM), 1.0, 6.0, ((2, 4), (3, 8)), jnp.float32)
    velocity = normal_values(arg_keys[1], (2, LEV, 4 * EX * N_FACE, 4 * EY * N_DOM), 1.0, 4.0, ((2, 4), (3, 8)))
    jacobian = jnp.clip(jnp.exp(math.log(2.0) - 1.3862944 * jax.random.uniform(arg_keys[2], (EX * N_FACE, EY * N_DOM), jnp.float32) ** block_scale(arg_keys[2], (EX * N_FACE, EY * N_DOM), ((0, 4), (1, 8)), -0.2, 0.2)), 0.5, 2.0)
    element_span = draw_element_span(jax.random.fold_in(arg_keys[19], 71), 0)
    sunlit = draw_sunlit(jax.random.fold_in(arg_keys[19], 71), 0)
    first_weight = normal_values(arg_keys[5], (FEAT, HIDDEN_SIZE), FEAT ** -0.5, 0.5)
    first_bias = normal_values(arg_keys[6], (HIDDEN_SIZE,), 0.5, 3.0, (), jnp.float32)
    second_weight = normal_values(arg_keys[7], (HIDDEN_SIZE, HIDDEN_SIZE), HIDDEN_SIZE ** -0.5, 0.25)
    second_bias = normal_values(arg_keys[8], (HIDDEN_SIZE,), 0.5, 3.0, (), jnp.float32)
    third_weight = normal_values(arg_keys[9], (HIDDEN_SIZE, HIDDEN_SIZE), HIDDEN_SIZE ** -0.5, 0.25)
    third_bias = normal_values(arg_keys[10], (HIDDEN_SIZE,), 0.5, 3.0, (), jnp.float32)
    output_weight = normal_values(arg_keys[11], (HIDDEN_SIZE, FEAT), HIDDEN_SIZE ** -0.5, 0.25)
    output_bias = normal_values(arg_keys[12], (FEAT,), 0.5, 3.0, (), jnp.float32)
    solar_inner = normal_values(arg_keys[13], (FEAT, HIDDEN_SIZE), FEAT ** -0.5, 0.5)
    solar_inner_bias = normal_values(arg_keys[14], (HIDDEN_SIZE,), 0.5, 3.0, (), jnp.float32)
    solar_middle = normal_values(arg_keys[15], (HIDDEN_SIZE, HIDDEN_SIZE), HIDDEN_SIZE ** -0.5, 0.25)
    solar_middle_bias = normal_values(arg_keys[16], (HIDDEN_SIZE,), 0.5, 3.0, (), jnp.float32)
    solar_outer = normal_values(arg_keys[17], (HIDDEN_SIZE, FEAT), HIDDEN_SIZE ** -0.5, 0.25)
    solar_outer_bias = normal_values(arg_keys[18], (FEAT,), 0.5, 3.0, (), jnp.float32)
    return {"prognostic": prognostic, "velocity": velocity, "jacobian": jacobian, "element_span": element_span, "sunlit": sunlit, "first_weight": first_weight, "first_bias": first_bias, "second_weight": second_weight, "second_bias": second_bias, "third_weight": third_weight, "third_bias": third_bias, "output_weight": output_weight, "output_bias": output_bias, "solar_inner": solar_inner, "solar_inner_bias": solar_inner_bias, "solar_middle": solar_middle, "solar_middle_bias": solar_middle_bias, "solar_outer": solar_outer, "solar_outer_bias": solar_outer_bias}


TIME_STEP = 0.1
LEAK_SLOPE = 0.15

def gll_tables():
    points = np.array([-1.0, -1.0 / np.sqrt(5.0), 1.0 / np.sqrt(5.0), 1.0])
    legendre = (5.0 * points ** 3 - 3.0 * points) / 2.0
    derivative = np.zeros((4, 4))
    for i in range(4):
        for k in range(4):
            if i != k:
                derivative[i, k] = legendre[i] / (legendre[k] * (points[i] - points[k]))
    derivative[0, 0] = -3.0
    derivative[3, 3] = 3.0
    weights = np.array([1.0 / 6.0, 5.0 / 6.0, 5.0 / 6.0, 1.0 / 6.0])
    return (derivative.astype(np.float32), weights.astype(np.float32))

def sum_copies(node_field):
    full_shape = node_field.shape
    leading = full_shape[:-2]
    width_x, width_y = (full_shape[-2], full_shape[-1])
    blocks = node_field.reshape(leading + (width_x // 4, 4, width_y))
    joined = blocks[..., 3, :] + jnp.roll(blocks[..., 0, :], -1, axis=-2)
    blocks = blocks.at[..., 3, :].set(joined).at[..., 0, :].set(jnp.roll(joined, 1, axis=-2))
    node_field = blocks.reshape(full_shape)
    blocks = node_field.reshape(leading + (width_x, width_y // 4, 4))
    joined = blocks[..., 3] + jnp.roll(blocks[..., 0], -1, axis=-1)
    blocks = blocks.at[..., 3].set(joined).at[..., 0].set(jnp.roll(joined, 1, axis=-1))
    return blocks.reshape(full_shape)

def assemble(values, node_mass):
    return sum_copies(values * node_mass) / sum_copies(node_mass)

def slopes(node_field, derivative, metric):
    fields, levels, width_x, width_y = node_field.shape
    blocks = node_field.reshape(fields, levels, width_x // 4, 4, width_y)
    along_x = jnp.einsum('ik,vlekz->vleiz', derivative, blocks, precision=lax.Precision.HIGHEST).reshape(node_field.shape)
    blocks = node_field.reshape(fields, levels, width_x, width_y // 4, 4)
    along_y = jnp.einsum('jk,vlxek->vlxej', derivative, blocks, precision=lax.Precision.HIGHEST).reshape(node_field.shape)
    return (along_x / metric, along_y / metric)

def to_cells(node_field):
    fields, levels, width_x, width_y = node_field.shape
    blocks = node_field.reshape(fields, levels, width_x // 4, 2, 2, width_y // 4, 2, 2)
    quarter = jnp.array([[1.0 / 6.0, 5.0 / 6.0], [5.0 / 6.0, 1.0 / 6.0]], jnp.float32)
    cells = jnp.einsum('vlxaiybj,ai,bj->xyabvl', blocks, quarter, quarter, precision=lax.Precision.HIGHEST)
    return cells.reshape(width_x // 4, width_y // 4, 4, fields * levels)

def to_nodes(cells, fields, levels):
    elements_x, elements_y = (cells.shape[0], cells.shape[1])
    spread = cells.reshape(elements_x, elements_y, 2, 2, fields, levels).transpose(4, 5, 0, 2, 1, 3)
    spread = jnp.broadcast_to(spread[:, :, :, :, None, :, :, None], (fields, levels, elements_x, 2, 2, elements_y, 2, 2))
    return spread.reshape(fields, levels, 4 * elements_x, 4 * elements_y)

def leaky_relu(values):
    return jnp.where(values > 0, values, LEAK_SLOPE * values)

def layer(inputs, weight, bias):
    return leaky_relu(jnp.dot(inputs, weight, preferred_element_type=jnp.float32) + bias).astype(jnp.bfloat16)

def primary(row_data, params):
    first = layer(row_data, params[0], params[1])
    second = layer(first, params[2], params[3])
    third = layer(second, params[4], params[5])
    return jnp.dot(third, params[6], preferred_element_type=jnp.float32) + params[7]

def solar_net(row_data, params):
    inner = layer(row_data, params[0], params[1])
    middle = layer(inner, params[2], params[3])
    return jnp.dot(middle, params[4], preferred_element_type=jnp.float32) + params[5]

def reference(prognostic, velocity, jacobian, element_span, sunlit, first_weight, first_bias, second_weight, second_bias, third_weight, third_bias, output_weight, output_bias, solar_inner, solar_inner_bias, solar_middle, solar_middle_bias, solar_outer, solar_outer_bias):
    derivative, weights = gll_tables()
    derivative = jnp.asarray(derivative, jnp.float32)
    weights = jnp.asarray(weights, jnp.float32)
    fields, levels = (prognostic.shape[0], prognostic.shape[1])
    node_mass = (jacobian[:, None, :, None] * weights[None, :, None, None] * weights[None, None, None, :]).reshape(prognostic.shape[2:])
    metric = jnp.sqrt(jnp.repeat(jnp.repeat(jacobian, 4, axis=0), 4, axis=1))
    along_x, along_y = slopes(prognostic, derivative, metric)
    motion = velocity.astype(jnp.float32)
    dynamics = -(motion[0][None] * along_x + motion[1][None] * along_y)
    advanced = prognostic + TIME_STEP * assemble(dynamics, node_mass)
    columns = to_cells(advanced).astype(jnp.bfloat16)
    grid_x, grid_y = jacobian.shape
    features = columns.shape[-1]
    per_block = 4 * EX * EY
    row_data = columns.reshape(-1, per_block, features)
    flags = jnp.repeat(sunlit.reshape(-1).astype(jnp.float32), 4).reshape(-1, per_block)
    main_params = (first_weight, first_bias, second_weight, second_bias, third_weight, third_bias, output_weight, output_bias)
    solar_params = (solar_inner, solar_inner_bias, solar_middle, solar_middle_bias, solar_outer, solar_outer_bias)

    def one_block(pair):
        block_rows, block_flags = pair
        primary_out = primary(block_rows, main_params)
        solar_out = solar_net(block_rows, solar_params)
        return (primary_out + block_flags[:, None] * solar_out).astype(jnp.bfloat16)
    increment = lax.map(one_block, (row_data, flags)).reshape(grid_x, grid_y, 4, features)
    new_state = advanced + assemble(to_nodes(increment.astype(jnp.float32), fields, levels), node_mass)
    ordered = columns.reshape(N_FACE, EX, N_DOM, EY, 4, features).transpose(0, 2, 1, 3, 4, 5).reshape(-1, 4, features)
    owners = element_span.reshape(N_FACE, EX, N_DOM, EY).transpose(0, 2, 1, 3).reshape(-1)
    ordering = jnp.argsort(owners, stable=True)
    span_state = ordered[ordering].reshape(-1, features)
    return (new_state, span_state)
```

```python
import jax
import jax.numpy as jnp
import numpy as np
from jax import lax
from jax.experimental import pallas as pl
from jax.experimental.pallas import tpu as pltpu
from jax.sharding import PartitionSpec as P

TIME_STEP = 0.1
LEAK_SLOPE = 0.15
F32 = jnp.float32
BF16 = jnp.bfloat16
HIGHEST = lax.Precision.HIGHEST
CELL_WEIGHTS = (1.0 / 6.0, 5.0 / 6.0, 5.0 / 6.0, 1.0 / 6.0)
MIB = 1024 * 1024
EMPTY = 1e30


def derivative_matrix():
    points = np.array([-1.0, -1.0 / np.sqrt(5.0), 1.0 / np.sqrt(5.0), 1.0])
    legendre = (5.0 * points**3 - 3.0 * points) / 2.0
    derivative = np.zeros((4, 4))
    for i in range(4):
        for k in range(4):
            if i != k:
                derivative[i, k] = legendre[i] / (legendre[k] * (points[i] - points[k]))
    derivative[0, 0] = -3.0
    derivative[3, 3] = 3.0
    return derivative


D = derivative_matrix()


def y_derivative_operand(width):
    full = np.kron(np.eye(width // 4), D.T).astype(np.float32)
    high = full.astype(jnp.bfloat16)
    low = (full - high.astype(np.float32)).astype(jnp.bfloat16)
    return np.concatenate([high, high, low], axis=0)


def iota(shape, dim):
    return lax.broadcasted_iota(jnp.int32, shape, dim)


def split(values):
    high = values.astype(BF16)
    return high, (values - high.astype(F32)).astype(BF16)


def copies_along_y(values):
    width = values.shape[-1]
    lane = iota((1, width), 1)
    up = ((lane & 3) == 3) & (lane < width - 1)
    down = ((lane & 3) == 0) & (lane > 0)
    return jnp.where(
        up, pltpu.roll(values, width - 1, 1), jnp.where(down, pltpu.roll(values, 1, 1), 0.0)
    )


def along_lanes(jac, width):
    expand = (iota((jac.shape[1], width), 1) >> 2) == iota((jac.shape[1], width), 0)
    return jnp.dot(jac, expand.astype(F32), precision=HIGHEST, preferred_element_type=F32)


def inner_reciprocals(mass):
    width = mass.shape[1]
    lane = iota(mass.shape, 1)
    row = iota(mass.shape, 0)
    inner = (lane > 0) & (lane < width - 1)
    inside = jnp.where(inner, 1.0 / mass, 0.0)
    shared = jnp.where(inner & (row > 0), 1.0 / (mass + pltpu.roll(mass, 1, 0)), 0.0)
    return inside, shared


def dynamics_kernel(
    prog_ref, vel_ref, jac_ref, dcat_ref, adv_ref, xlo_ref, xhi_ref, ylo_ref, yhi_ref,
    sy3_ref, vf3_ref, pf3_ref, scale_ref, inside_ref, shared_ref, zlo_ref, zhi_ref,
):
    step = pl.program_id(0)
    _, tile, width_x, width = prog_ref.shape
    elements_x, elements_y = jac_ref.shape
    features = zlo_ref.shape[0]
    levels = features // 2
    planes = 2 * tile
    pitch = sy3_ref.shape[1]
    sy_ref = sy3_ref.reshape(planes * pitch, width)
    vf_ref = vf3_ref.reshape(planes * pitch, width)
    pf_ref = pf3_ref.reshape(planes * pitch, width)

    @pl.when(step == 0)
    def _():
        mass = along_lanes(jac_ref[...], width)
        scale_ref[...] = -TIME_STEP * jnp.sqrt(mass)
        inside, shared = inner_reciprocals(mass + copies_along_y(mass))
        inside_ref[...] = inside
        shared_ref[...] = shared

    vf3_ref[:, 0:width_x, :] = vel_ref[...].astype(F32).reshape(planes, width_x, width)
    piece = planes // 4
    for at in range(4):
        first = at * piece
        values = prog_ref[first // tile, first % tile : first % tile + piece]
        pf3_ref[first : first + piece, 0:width_x, :] = values
        high, low = split(values.reshape(piece * width_x, width))
        sy3_ref[first : first + piece, 0:width_x, :] = jnp.dot(
            jnp.concatenate([high, low, high], axis=1), dcat_ref[...], preferred_element_type=F32
        ).reshape(piece, width_x, width)

    lane = iota((tile, width), 1)
    p0, p1 = (D[0, 0] - D[0, 3]) / 2, (D[0, 1] - D[0, 2]) / 2
    q0 = (D[0, 1] + D[0, 2]) / 2
    r0, r1 = (D[1, 0] - D[1, 3]) / 2, -D[1, 2] / 2
    t0 = D[1, 2] / 2

    def rims(lines):
        first, second, third = lines
        a = pltpu.roll(first, 1, 1)
        b = pltpu.roll(second, 2, 1)
        c = pltpu.roll(third, 3, 1)

        def pick(base):
            return jnp.where(
                lane == base, first,
                jnp.where(
                    lane == (base + 1) % width, a,
                    jnp.where(
                        lane == (base + 2) % width, b, jnp.where(lane == (base + 3) % width, c, 0.0)
                    ),
                ),
            )

        return pick(0), pick(width - 1)

    def element(p, carry):
        scale = scale_ref[p : p + 1, :]
        inside = inside_ref[p : p + 1, :]
        shared = shared_ref[p : p + 1, :]
        shift = (4 * p + width - 1) % width
        vx = [vf_ref[pl.ds(4 * p + k, tile, stride=pitch), :] for k in range(4)]
        vy = [
            vf_ref[pl.ds(tile * pitch + 4 * p + k, tile, stride=pitch), :] for k in range(4)
        ]
        out = []
        for v in range(2):
            last_e, last_f, z_low, z_high = carry[4 * v : 4 * v + 4]
            base = v * tile * pitch + 4 * p
            f = [pf_ref[pl.ds(base + k, tile, stride=pitch), :] for k in range(4)]
            sy = [sy_ref[pl.ds(base + k, tile, stride=pitch), :] for k in range(4)]
            outer_gap, inner_gap = f[0] - f[3], f[1] - f[2]
            bend = (f[1] + f[2]) - (f[0] + f[3])
            odd = p0 * outer_gap + p1 * inner_gap
            even = q0 * bend
            odd_in = r0 * outer_gap + r1 * inner_gap
            even_in = t0 * bend
            sx = [odd + even, odd_in + even_in, odd_in - even_in, odd - even]
            e = []
            for k in range(4):
                moved = (vx[k] * sx[k] + vy[k] * sy[k]) * scale
                e.append(moved + copies_along_y(moved))
            joined = last_e + e[0]
            gain = joined * shared
            adv_ref[4 * p, v] = f[0] + gain
            adv_ref[4 * p + 1, v] = f[1] + e[1] * inside
            adv_ref[4 * p + 2, v] = f[2] + e[2] * inside

            if p == 0:
                xlo_ref[pl.ds(pl.multiple_of(v * levels + tile * step, tile), tile), :] = joined
            else:
                adv_ref[4 * p - 1, v] = last_f + gain

            low, high = rims((joined, e[1], e[2]))
            out += [
                e[3], f[3],
                z_low + pltpu.roll(low, shift, 1), z_high + pltpu.roll(high, shift, 1),
            ]
        return tuple(out)

    zero = jnp.zeros((tile, width), F32)
    final = (zero,) * 8
    for p in range(elements_x):
        final = element(p, final)
    for v in range(2):
        last_e, last_f, z_low, z_high = final[4 * v : 4 * v + 4]
        at = pl.ds(pl.multiple_of(v * levels + tile * step, tile), tile)
        adv_ref[width_x - 1, v] = last_f
        xhi_ref[at, :] = last_e
        zlo_ref[at, :] = jnp.where(
            lane == width_x - 1, pltpu.roll(last_e, width_x - 1, 1), z_low
        )
        zhi_ref[at, :] = pltpu.roll(
            jnp.where(lane == width_x - 2, pltpu.roll(last_e, width_x - 1, 1), z_high), 1, 1
        )

    @pl.when(step == pl.num_programs(0) - 1)
    def _():
        jac = jac_ref[...]
        mass = along_lanes(jac, width)
        mass = mass + copies_along_y(mass)
        ylo_ref[...] = zlo_ref[...].T
        yhi_ref[...] = zhi_ref[...].T
        for ref, q in ((ylo_ref, 0), (yhi_ref, elements_y - 1)):
            ref[width_x : width_x + elements_x, :] = jnp.broadcast_to(
                jac[:, q : q + 1], (elements_x, features)
            )
        for ref, x, p in ((xlo_ref, 0, 0), (xhi_ref, width_x - 1, elements_x - 1)):
            ref[features : features + 8, :] = jnp.concatenate(
                [
                    ylo_ref[x : x + 1, :],
                    yhi_ref[x : x + 1, :],
                    mass[p : p + 1, :],
                    ylo_ref[width_x + p : width_x + p + 1, :],
                    yhi_ref[width_x + p : width_x + p + 1, :],
                    jnp.zeros((3, width), F32),
                ],
                axis=0,
            )


def cells_kernel(capacity, devices, adv_ref, span_ref, col_ref, slot_ref):
    group = adv_ref.shape[0] // 4
    width = adv_ref.shape[3]
    features = adv_ref.shape[1] * adv_ref.shape[2]
    elements_x, elements_y = span_ref.shape
    elements = elements_x * elements_y

    @pl.when(pl.program_id(0) == 0)
    def _():
        lane = iota((elements_y, elements), 1)
        tiled = lax.rem(lane, elements_y) == iota((elements_y, elements), 0)
        spread = jnp.dot(
            span_ref[...].astype(F32).astype(BF16), tiled.astype(BF16), preferred_element_type=F32
        )
        start = iota((elements_x, elements), 0) * elements_y
        at = iota((elements_x, elements), 1)
        own = (at >= start) & (at < start + elements_y)
        target = jnp.sum(jnp.where(own, spread, 0.0), axis=0, keepdims=True)
        chosen = jnp.where(
            target == iota((devices, elements), 0).astype(F32), 1.0, 0.0
        )
        before = iota((elements, elements), 0) < iota((elements, elements), 1)
        earlier = jnp.dot(
            chosen.astype(BF16), before.astype(BF16), preferred_element_type=F32
        )
        rank = jnp.sum(chosen * earlier, axis=0, keepdims=True)
        slot_ref[...] = (target * capacity + rank).astype(jnp.int32)

    select = select_cells(elements_y, width)
    for p in range(group):
        for a in range(2):
            line = adv_ref[4 * p + 2 * a] * CELL_WEIGHTS[2 * a]
            line += adv_ref[4 * p + 2 * a + 1] * CELL_WEIGHTS[2 * a + 1]
            low, high = cells_of_line(line.reshape(features, width), select)
            at = slice(p * elements_y, (p + 1) * elements_y)
            col_ref[2 * a, at, :] = low
            col_ref[2 * a + 1, at, :] = high


def select_cells(elements_y, width):
    shape = (2 * elements_y, width)
    row, lane = iota(shape, 0), iota(shape, 1)
    wanted = jnp.where(row < elements_y, 4 * row, 4 * (row - elements_y) + 2)
    return (lane == wanted).astype(BF16)


def cells_of_line(line, select):
    features, width = line.shape
    inner = (iota((1, width), 1) & 3)
    line = line * jnp.where((inner == 0) | (inner == 3), 1.0 / 6.0, 5.0 / 6.0)
    line = line + pltpu.roll(line, width - 1, 1)
    high, low = split(line)
    both = lax.dot_general(
        select, jnp.concatenate([high, low], axis=0), (((1,), (1,)), ((), ())),
        preferred_element_type=F32,
    )
    cells = both[:, :features] + both[:, features:]
    half = select.shape[0] // 2
    return cells[:half], cells[half:]


def corners_kernel(width_x, elements_x, ylo_ref, yhi_ref, prev_ref, next_ref, ylo_out, yhi_out):
    features = prev_ref.shape[0] - 8
    spare = width_x + elements_x
    for side, (ref, out) in enumerate(((ylo_ref, ylo_out), (yhi_ref, yhi_out))):
        row = iota(ref.shape, 0)
        values = ref[...]
        prev = prev_ref[features + side : features + side + 1, :]
        later = next_ref[features + side : features + side + 1, :]
        prev_mass = prev_ref[features + 3 + side : features + 4 + side, :]
        later_mass = next_ref[features + 3 + side : features + 4 + side, :]
        values = values + jnp.where(row == 0, prev, 0.0)
        values = values + jnp.where(row == width_x - 1, later, 0.0)
        values = jnp.where(row == spare, prev_mass, values)
        out[...] = jnp.where(row == spare + 1, later_mass, values)


def send_kernel(
    width_x, elements_x,
    col_ref, slot_ref, xlo_ref, xhi_ref, prev_ref, next_ref, ylo_ref, yhi_ref, yprev_ref,
    ynext_ref, colbf_ref, out_ref, fy_ref, ry_ref, fx_ref, rx_ref, work_ref,
):
    _, elements, features = col_ref.shape
    elements_y = elements // elements_x
    width = xlo_ref.shape[1]
    work_ref[...] = col_ref[...]
    select = select_cells(elements_y, width)
    lane = iota((1, width), 1)
    inner = (lane > 0) & (lane < width - 1)
    for side, (own, other) in enumerate(((ylo_ref, yprev_ref), (yhi_ref, ynext_ref))):
        total = own[...] + other[...]
        mass = total[width_x : width_x + elements_x]
        row = iota(mass.shape, 0)
        spare = width_x + elements_x
        before = jnp.where(row == 0, total[spare : spare + 1], pltpu.roll(mass, 1, 0))
        after = jnp.where(
            row == elements_x - 1, total[spare + 1 : spare + 2], pltpu.roll(mass, elements_x - 1, 0)
        )
        inside = 1.0 / mass
        ry_ref[side, pl.ds(0, elements_x, stride=4), :] = 1.0 / (mass + before)
        ry_ref[side, pl.ds(1, elements_x, stride=4), :] = inside
        ry_ref[side, pl.ds(2, elements_x, stride=4), :] = inside
        ry_ref[side, pl.ds(3, elements_x, stride=4), :] = 1.0 / (mass + after)
        fy_ref[side] = total[:width_x] * ry_ref[side]
        fixes = [fy_ref[side, pl.ds(k, elements_x, stride=4), :] for k in range(4)]
        at = pl.ds(side * (elements_y - 1), elements_x, stride=elements_y)
        for a in range(2):
            added = CELL_WEIGHTS[2 * a] * fixes[2 * a] + CELL_WEIGHTS[2 * a + 1] * fixes[2 * a + 1]
            k = 2 * a + side
            work_ref[k, at, :] = work_ref[k, at, :] + CELL_WEIGHTS[0] * added
    for side, (own, other) in enumerate(((xlo_ref, prev_ref), (xhi_ref, next_ref))):
        mass = own[features + 2 : features + 3, :] + other[features + 2 : features + 3, :]
        reciprocal = jnp.where(inner, 1.0 / mass, 0.0)
        rx_ref[side] = jnp.broadcast_to(reciprocal, (8, width))
        fix = (own[:features] + other[:features]) * reciprocal
        fx_ref[side] = fix
        low, high = cells_of_line(CELL_WEIGHTS[0] * fix, select)
        at = slice(side * (elements_x - 1) * elements_y, (side * (elements_x - 1) + 1) * elements_y)
        work_ref[2 * side, at, :] = work_ref[2 * side, at, :] + low
        work_ref[2 * side + 1, at, :] = work_ref[2 * side + 1, at, :] + high
    for k in range(4):
        colbf_ref[:, k * features : (k + 1) * features] = work_ref[k].astype(BF16)
    slots = out_ref.shape[0]
    piece = slots // 4
    for part in range(4):
        chosen = (iota((piece, elements), 0) + part * piece) == slot_ref[...]
        chosen = jnp.where(chosen, 1.0, 0.0)
        filled = jnp.max(chosen, axis=1, keepdims=True)
        moved = jnp.dot(chosen.astype(BF16), colbf_ref[...], preferred_element_type=F32)
        out_ref[pl.ds(part * piece, piece), :] = jnp.where(filled > 0.0, moved, EMPTY).astype(BF16)


def dense(inputs, weight_ref, bias_ref):
    return jnp.dot(inputs, weight_ref[...], preferred_element_type=F32) + bias_ref[...]


def leaky(values):
    return jnp.maximum(values, LEAK_SLOPE * values).astype(BF16)


def network_kernel(
    lit_ref, col_ref, w1, b1, w2, b2, w3, b3, w4, b4, s1, c1, s2, c2, s3, c3, inc_ref, total_ref
):
    rows = col_ref.shape[0]
    features = col_ref.shape[1] // 4
    inputs = jnp.concatenate(
        [col_ref[:, k * features : (k + 1) * features] for k in range(4)], axis=0
    )
    hidden = leaky(dense(inputs, w1, b1))
    hidden = leaky(dense(hidden, w2, b2))
    hidden = leaky(dense(hidden, w3, b3))
    total_ref[...] = dense(hidden, w4, b4)

    @pl.when(lit_ref[0, 0] != 0)
    def _():
        solar = leaky(dense(inputs, s1, c1))
        solar = leaky(dense(solar, s2, c2))
        total_ref[...] += lit_ref[0, 0].astype(F32) * dense(solar, s3, c3)

    for k in range(4):
        inc_ref[:, k * features : (k + 1) * features] = total_ref[
            k * rows : (k + 1) * rows, :
        ].astype(BF16)


def spread_operand(mass_line, elements_y):
    width = mass_line.shape[1]
    shape = (2 * elements_y, width)
    row, lane = iota(shape, 0), iota(shape, 1)
    upper = row >= elements_y
    q = jnp.where(upper, row - elements_y, row)
    b = jnp.where(upper, 1, 0)
    own = (lane >> 1) == 2 * q + b
    copy = lane == jnp.where(upper, 4 * q + 4, 4 * q - 1)
    weights = jnp.where(
        own, mass_line, jnp.where(copy, copies_along_y(mass_line), 0.0)
    )
    high, low = split(weights)
    return jnp.concatenate([high, low], axis=0)


def spread_line(inc_ref, p, a, operand, elements_y):
    features = inc_ref.shape[1] // 4
    at = pl.ds(pl.multiple_of(p * elements_y, elements_y), elements_y)
    cells = [
        inc_ref[at, (2 * a + b) * features : (2 * a + b + 1) * features] for b in range(2)
    ]
    return lax.dot_general(
        jnp.concatenate(cells + cells, axis=0), operand, (((0,), (0,)), ((), ())),
        preferred_element_type=F32,
    )


def rims_kernel(inc_ref, jac_ref, xlo_ref, xhi_ref, ylo_ref, yhi_ref, wide_ref):
    elements_x, elements_y = jac_ref.shape
    features = inc_ref.shape[1] // 4
    width = xlo_ref.shape[1]
    width_x = 4 * elements_x
    for k in range(4):
        wide_ref[k] = inc_ref[:, k * features : (k + 1) * features].astype(F32)
    mass = along_lanes(jac_ref[...], width)
    for side, ref in enumerate((ylo_ref, yhi_ref)):
        q = side * (elements_y - 1)
        column = jac_ref[:, q : q + 1]
        at = pl.ds(q, elements_x, stride=elements_y)
        first = column * wide_ref[side, at, :]
        second = column * wide_ref[2 + side, at, :]
        row = iota(first.shape, 0)
        ref[pl.ds(0, elements_x, stride=4), :] = first + jnp.where(
            row == 0, 0.0, pltpu.roll(second, 1, 0)
        )
        ref[pl.ds(1, elements_x, stride=4), :] = first
        ref[pl.ds(2, elements_x, stride=4), :] = second
        ref[pl.ds(3, elements_x, stride=4), :] = second + jnp.where(
            row == elements_x - 1, 0.0, pltpu.roll(first, elements_x - 1, 0)
        )
        ref[width_x:, :] = jnp.zeros((ref.shape[0] - width_x, features), F32)
    for side, ref in enumerate((xlo_ref, xhi_ref)):
        p = side * (elements_x - 1)
        x = side * (width_x - 1)
        operand = spread_operand(mass[p : p + 1], elements_y)
        ref[0:features, :] = spread_line(inc_ref, p, side, operand, elements_y)
        ref[features : features + 8, :] = jnp.concatenate(
            [ylo_ref[x : x + 1, :], yhi_ref[x : x + 1, :], jnp.zeros((6, width), F32)], axis=0
        )


def final_kernel(
    adv_ref, inc_ref, jac_ref, xlo_ref, xhi_ref, prev_ref, next_ref, ylo_ref, yhi_ref, yprev_ref,
    ynext_ref, fy_ref, ry_ref, fx_ref, rx_ref, out_ref, mass_ref, inside_ref, shared_ref,
    rim_ref, edge_ref,
):
    step = pl.program_id(0)
    elements_x, elements_y = jac_ref.shape
    width_x = 4 * elements_x
    lines = adv_ref.shape[0]
    group = lines // 4
    width = adv_ref.shape[3]
    features = adv_ref.shape[1] * adv_ref.shape[2]

    @pl.when(step == 0)
    def _():
        mass = along_lanes(jac_ref[...], width)
        mass_ref[...] = mass
        inside, shared = inner_reciprocals(mass + copies_along_y(mass))
        inside_ref[...] = inside
        shared_ref[0:elements_x, :] = shared
        shared_ref[elements_x:, :] = jnp.zeros((8, width), F32)
        for side, (own, other) in enumerate(((ylo_ref, yprev_ref), (yhi_ref, ynext_ref))):
            rim_ref[side] = fy_ref[side] + (own[0:width_x, :] + other[0:width_x, :]) * ry_ref[side]
        for side, (own, other) in enumerate(((xlo_ref, prev_ref), (xhi_ref, next_ref))):
            edge_ref[side] = (
                fx_ref[side] + (own[0:features, :] + other[0:features, :]) * rx_ref[side, 0:1, :]
            )

    out = out_ref.reshape(features * lines, width)
    row = iota((16, width), 0)
    lane = iota((16, width), 1)
    place = (((row < 2) & (lane == 0)) | ((row >= 2) & (row < 4) & (lane == width - 1))).astype(BF16)

    def rim_of(x):
        low = rim_ref[0, pl.ds(x, 1), :]
        high = rim_ref[1, pl.ds(x, 1), :]
        parts = jnp.where(row < 2, low, high)
        rough = parts.astype(BF16).astype(F32)
        rest = parts - rough
        stacked = jnp.where((row == 0) | (row == 2), rough, jnp.where(row < 4, rest, 0.0))
        return lax.dot_general(
            stacked.astype(BF16), place, (((0,), (0,)), ((), ())), preferred_element_type=F32
        )

    def line_of(p, a):
        operand = spread_operand(mass_ref[pl.ds(p, 1), :], elements_y)
        return spread_line(inc_ref, p, a, operand, elements_y)

    def store(at, values):
        out[pl.ds(at, features, stride=lines), :] = adv_ref[at].reshape(features, width) + values

    first = step * group
    before = line_of(jnp.maximum(first - 1, 0), 1)
    here = line_of(first, 0)
    joint = (before + here) * shared_ref[pl.ds(first, 1), :] + rim_of(4 * first)
    for k in range(group):
        p = first + k
        inside = inside_ref[pl.ds(p, 1), :]
        store(4 * k, joint)
        store(4 * k + 1, here * inside + rim_of(4 * p + 1))
        there = line_of(p, 1)
        store(4 * k + 2, there * inside + rim_of(4 * p + 2))
        here = line_of(jnp.minimum(p + 1, elements_x - 1), 0)
        joint = (there + here) * shared_ref[pl.ds(p + 1, 1), :] + rim_of(4 * p + 3)
        store(4 * k + 3, joint)

    @pl.when(step == 0)
    def _():
        at = pl.ds(0, features, stride=lines)
        out[at, :] = out[at, :] + edge_ref[0]

    @pl.when(step == pl.num_programs(0) - 1)
    def _():
        at = pl.ds(lines - 1, features, stride=lines)
        out[at, :] = out[at, :] + edge_ref[1]


def arrange_kernel(capacity, data_ref, out_ref, wide_ref, rows_ref, vector_ref, start_ref, sem):
    devices = vector_ref.shape[0]
    slots = data_ref.shape[0]
    features = data_ref.shape[1] // 4
    elements = out_ref.shape[0] // 4
    filled = jnp.where(data_ref[:, 0:features].astype(F32) < 0.5 * EMPTY, 1.0, 0.0).astype(BF16)
    before = iota((devices, slots), 1) < iota((devices, slots), 0) * capacity
    starts = jnp.dot(
        jnp.where(before, 1.0, 0.0).astype(BF16), filled, preferred_element_type=F32
    )
    vector_ref[...] = jnp.clip(starts, 0.0, float(elements)).astype(jnp.int32)
    copy = pltpu.make_async_copy(vector_ref, start_ref, sem)
    copy.start()
    for k in range(4):
        wide_ref[k] = data_ref[:, k * features : (k + 1) * features].astype(F32)
    copy.wait()

    def one(s, carry):
        start = start_ref[s, 0]
        for k in range(4):
            rows_ref[pl.ds(4 * start + k, capacity, stride=4), :] = wide_ref[
                k, pl.ds(s * capacity, capacity), :
            ]
        return carry

    lax.fori_loop(0, devices, one, 0)
    out_ref[...] = rows_ref[0 : out_ref.shape[0], :].astype(BF16)


def params(mib):
    return pltpu.CompilerParams(vmem_limit_bytes=mib * MIB)


def whole(shape):
    return pl.BlockSpec(shape, lambda *_: (0,) * len(shape))


def cost(flops, bytes_accessed):
    return pl.CostEstimate(flops=flops, bytes_accessed=bytes_accessed, transcendentals=0)


def shape_of(shape, dtype=F32):
    return jax.ShapeDtypeStruct(shape, dtype)


def shifted(axis, by):
    count = lax.axis_size(axis)
    return [(i, (i + by) % count) for i in range(count)]


def dynamics_call(prognostic, velocity, jacobian):
    fields, levels, width_x, width = prognostic.shape
    elements_x, elements_y = jacobian.shape
    features = fields * levels
    tile = 8
    packet = features + 8
    dcat = jnp.asarray(y_derivative_operand(width))
    return pl.pallas_call(
        dynamics_kernel,
        grid=(levels // tile,),
        in_specs=[
            pl.BlockSpec((2, tile, width_x, width), lambda t: (0, t, 0, 0)),
            pl.BlockSpec((2, tile, width_x, width), lambda t: (0, t, 0, 0)),
            whole((elements_x, elements_y)),
            whole((3 * width, width)),
        ],
        out_specs=[
            pl.BlockSpec((width_x, 2, tile, width), lambda t: (0, 0, t, 0)),
            whole((packet, width)),
            whole((packet, width)),
            whole((width, features)),
            whole((width, features)),
        ],
        out_shape=[
            shape_of((width_x, fields, levels, width)),
            shape_of((packet, width)),
            shape_of((packet, width)),
            shape_of((width, features)),
            shape_of((width, features)),
        ],
        scratch_shapes=[
            pltpu.VMEM((2 * tile, width_x + 8, width), F32),
            pltpu.VMEM((2 * tile, width_x + 8, width), F32),
            pltpu.VMEM((2 * tile, width_x + 8, width), F32),
            pltpu.VMEM((elements_x, width), F32),
            pltpu.VMEM((elements_x, width), F32),
            pltpu.VMEM((elements_x, width), F32),
            pltpu.VMEM((features, width), F32),
            pltpu.VMEM((features, width), F32),
        ],
        compiler_params=params(58),
        cost_estimate=cost(2_000_000_000, 16_000_000),
        name="dynamics",
    )(prognostic, velocity, jacobian, dcat)


def on_device(
    prognostic,
    velocity,
    jacobian,
    element_span,
    sunlit,
    *weights,
):
    fields, levels, width_x, width = prognostic.shape
    elements_x, elements_y = jacobian.shape
    features = fields * levels
    elements = elements_x * elements_y
    devices = lax.axis_size("face") * lax.axis_size("dom")
    capacity = max(2, 2 * elements // devices)
    slots = devices * capacity
    packet = features + 8
    vmem = pl.BlockSpec(memory_space=pltpu.VMEM)
    smem = pl.BlockSpec(memory_space=pltpu.SMEM)

    adv, xlo, xhi, ylo, yhi = dynamics_call(prognostic, velocity, jacobian)

    group = 4
    col, slot_ids = pl.pallas_call(
        lambda *refs: cells_kernel(capacity, devices, *refs),
        grid=(elements_x // group,),
        in_specs=[
            pl.BlockSpec((4 * group, fields, levels, width), lambda g: (g, 0, 0, 0)),
            whole((elements_x, elements_y)),
        ],
        out_specs=[
            pl.BlockSpec((4, group * elements_y, features), lambda g: (0, g, 0)),
            whole((1, elements)),
        ],
        out_shape=[
            shape_of((4, elements, features)),
            shape_of((1, elements), jnp.int32),
        ],
        compiler_params=params(58),
        cost_estimate=cost(1_000_000_000, 8_000_000),
        name="cells",
    )(adv, element_span)

    def exchange(xlo, xhi, ylo, yhi):
        prev = lax.ppermute(xhi, "face", shifted("face", 1))
        later = lax.ppermute(xlo, "face", shifted("face", -1))
        ylo, yhi = pl.pallas_call(
            lambda *refs: corners_kernel(width_x, elements_x, *refs),
            in_specs=[vmem] * 4,
            out_specs=[vmem] * 2,
            out_shape=[shape_of((width, features))] * 2,
            compiler_params=params(16),
            name="corners",
        )(ylo, yhi, prev, later)
        yprev = lax.ppermute(yhi, "dom", shifted("dom", 1))
        ynext = lax.ppermute(ylo, "dom", shifted("dom", -1))
        return prev, later, ylo, yhi, yprev, ynext

    prev, later, ylo, yhi, yprev, ynext = exchange(xlo, xhi, ylo, yhi)

    colbf, outgoing, fy, ry, fx, rx = pl.pallas_call(
        lambda *refs: send_kernel(width_x, elements_x, *refs),
        in_specs=[vmem] * 10,
        out_specs=[vmem] * 6,
        out_shape=[
            shape_of((elements, 4 * features), BF16),
            shape_of((slots, 4 * features), BF16),
            shape_of((2, width_x, features)),
            shape_of((2, width_x, features)),
            shape_of((2, features, width)),
            shape_of((2, 8, width)),
        ],
        scratch_shapes=[pltpu.VMEM((4, elements, features), F32)],
        compiler_params=params(24),
        cost_estimate=cost(2_000_000_000, 5_000_000),
        name="send",
    )(col, slot_ids, xlo, xhi, prev, later, ylo, yhi, yprev, ynext)

    arrived = lax.all_to_all(
        outgoing.reshape(devices, capacity, 4 * features), ("face", "dom"),
        split_axis=0, concat_axis=0, tiled=True,
    ).reshape(slots, 4 * features)

    chunk = elements // 3
    hidden = weights[0].shape[1]
    operands, operand_specs = [], []
    for item in weights:
        item = item if item.ndim == 2 else item.reshape(1, -1)
        operands.append(item)
        operand_specs.append(whole(item.shape))
    inc = pl.pallas_call(
        network_kernel,
        grid=(3,),
        in_specs=[smem, pl.BlockSpec((chunk, 4 * features), lambda g: (g, 0))] + operand_specs,
        out_specs=pl.BlockSpec((chunk, 4 * features), lambda g: (g, 0)),
        out_shape=shape_of((elements, 4 * features), BF16),
        scratch_shapes=[pltpu.VMEM((4 * chunk, features), F32)],
        compiler_params=params(58),
        cost_estimate=cost(8 * elements * (4 * features * hidden + 3 * hidden * hidden), 4_000_000),
        name="network",
    )(sunlit, colbf, *operands)

    xlo2, xhi2, ylo2, yhi2 = pl.pallas_call(
        rims_kernel,
        in_specs=[vmem] * 2,
        out_specs=[vmem] * 4,
        out_shape=[
            shape_of((packet, width)),
            shape_of((packet, width)),
            shape_of((width, features)),
            shape_of((width, features)),
        ],
        scratch_shapes=[pltpu.VMEM((4, elements, features), F32)],
        compiler_params=params(16),
        cost_estimate=cost(10_000_000, 2_000_000),
        name="rims",
    )(inc, jacobian)

    prev2, later2, ylo2, yhi2, yprev2, ynext2 = exchange(xlo2, xhi2, ylo2, yhi2)

    new_state = pl.pallas_call(
        final_kernel,
        grid=(elements_x // group,),
        in_specs=[
            pl.BlockSpec((4 * group, fields, levels, width), lambda g: (g, 0, 0, 0)),
            whole((elements, 4 * features)),
            whole((elements_x, elements_y)),
            whole((packet, width)),
            whole((packet, width)),
            whole((packet, width)),
            whole((packet, width)),
            whole((width, features)),
            whole((width, features)),
            whole((width, features)),
            whole((width, features)),
            whole((2, width_x, features)),
            whole((2, width_x, features)),
            whole((2, features, width)),
            whole((2, 8, width)),
        ],
        out_specs=pl.BlockSpec((fields, levels, 4 * group, width), lambda g: (0, 0, g, 0)),
        out_shape=shape_of((fields, levels, width_x, width)),
        scratch_shapes=[
            pltpu.VMEM((elements_x, width), F32),
            pltpu.VMEM((elements_x, width), F32),
            pltpu.VMEM((elements_x + 8, width), F32),
            pltpu.VMEM((2, width_x, features), F32),
            pltpu.VMEM((2, features, width), F32),
        ],
        compiler_params=params(58),
        cost_estimate=cost(1_000_000_000, 14_000_000),
        name="final",
    )(
        adv, inc, jacobian, xlo2, xhi2, prev2, later2, ylo2, yhi2, yprev2, ynext2, fy, ry, fx, rx
    )

    span_state = pl.pallas_call(
        lambda *refs: arrange_kernel(capacity, *refs),
        in_specs=[vmem],
        out_specs=vmem,
        out_shape=shape_of((4 * elements, features), BF16),
        scratch_shapes=[
            pltpu.VMEM((4, slots, features), F32),
            pltpu.VMEM((4 * (elements + capacity), features), F32),
            pltpu.VMEM((devices, features), jnp.int32),
            pltpu.SMEM((devices, features), jnp.int32),
            pltpu.SemaphoreType.DMA,
        ],
        compiler_params=params(24),
        cost_estimate=cost(1_000_000, 3_000_000),
        name="arrange",
    )(arrived)
    return (new_state, span_state)


def solution(mesh):
    return jax.shard_map(
        on_device,
        mesh=mesh,
        in_specs=(
            P(None, None, "face", "dom"),
            P(None, None, "face", "dom"),
            P("face", "dom"),
            P("face", "dom"),
            P("face", "dom"),
        )
        + (P(),) * 14,
        out_specs=(P(None, None, "face", "dom"), P(("face", "dom"), None)),
        check_vma=False,
    )
```

```python
import jax
import jax.numpy as jnp
import numpy as np
from jax import lax
from jax.experimental import pallas as pl
from jax.experimental.pallas import tpu as pltpu
from jax.sharding import PartitionSpec as P

TIME_STEP = 0.1
LEAK_SLOPE = 0.15
F32 = jnp.float32
BF16 = jnp.bfloat16
HIGHEST = lax.Precision.HIGHEST
CELL_WEIGHTS = (1.0 / 6.0, 5.0 / 6.0, 5.0 / 6.0, 1.0 / 6.0)
MIB = 1024 * 1024
EMPTY = 1e30


def derivative_matrix():
    points = np.array([-1.0, -1.0 / np.sqrt(5.0), 1.0 / np.sqrt(5.0), 1.0])
    legendre = (5.0 * points**3 - 3.0 * points) / 2.0
    derivative = np.zeros((4, 4))
    for i in range(4):
        for k in range(4):
            if i != k:
                derivative[i, k] = legendre[i] / (legendre[k] * (points[i] - points[k]))
    derivative[0, 0] = -3.0
    derivative[3, 3] = 3.0
    return derivative


D = derivative_matrix()


def y_derivative_operand(width):
    full = np.kron(np.eye(width // 4), D.T).astype(np.float32)
    high = full.astype(jnp.bfloat16)
    low = (full - high.astype(np.float32)).astype(jnp.bfloat16)
    return np.concatenate([high, high, low], axis=0)


def iota(shape, dim):
    return lax.broadcasted_iota(jnp.int32, shape, dim)


def split(values):
    high = values.astype(BF16)
    return high, (values - high.astype(F32)).astype(BF16)


def copies_along_y(values):
    width = values.shape[-1]
    lane = iota((1, width), 1)
    up = ((lane & 3) == 3) & (lane < width - 1)
    down = ((lane & 3) == 0) & (lane > 0)
    return jnp.where(
        up, pltpu.roll(values, width - 1, 1), jnp.where(down, pltpu.roll(values, 1, 1), 0.0)
    )


def along_lanes(jac, width):
    expand = (iota((jac.shape[1], width), 1) >> 2) == iota((jac.shape[1], width), 0)
    return jnp.dot(jac, expand.astype(F32), precision=HIGHEST, preferred_element_type=F32)


def inner_reciprocals(mass):
    width = mass.shape[1]
    lane = iota(mass.shape, 1)
    row = iota(mass.shape, 0)
    inner = (lane > 0) & (lane < width - 1)
    inside = jnp.where(inner, 1.0 / mass, 0.0)
    shared = jnp.where(inner & (row > 0), 1.0 / (mass + pltpu.roll(mass, 1, 0)), 0.0)
    return inside, shared


def element_slopes(f):
    outer_gap, inner_gap = f[0] - f[3], f[1] - f[2]
    bend = (f[1] + f[2]) - (f[0] + f[3])
    odd = (D[0, 0] - D[0, 3]) / 2 * outer_gap + (D[0, 1] - D[0, 2]) / 2 * inner_gap
    even = (D[0, 1] + D[0, 2]) / 2 * bend
    odd_in = (D[1, 0] - D[1, 3]) / 2 * outer_gap - D[1, 2] / 2 * inner_gap
    even_in = D[1, 2] / 2 * bend
    return [odd + even, odd_in + even_in, odd_in - even_in, odd - even]


def edges_kernel(
    lit_ref, proglo_ref, proghi_ref, vello_ref, velhi_ref, jac_ref, dcat_ref, xlo_ref, xhi_ref,
    vf_ref,
):
    elements_x, elements_y = jac_ref.shape
    fields, levels, _, width = proglo_ref.shape
    features = fields * levels
    jac = jac_ref[...]
    mass = along_lanes(jac, width)
    joined = mass + copies_along_y(mass)
    inside, _ = inner_reciprocals(joined)
    lit = lit_ref[0, 0].astype(F32)
    sides = ((proglo_ref, vello_ref, xlo_ref), (proghi_ref, velhi_ref, xhi_ref))
    for side, (prog_ref, vel_ref, out_ref) in enumerate(sides):
        p = side * (elements_x - 1)
        lines = prog_ref.shape[2]
        prog = prog_ref.reshape(features * lines, width)
        first = side * (lines - 4)
        f = [prog[pl.ds(first + k, features, stride=lines), :] for k in range(4)]
        vlines = vel_ref.shape[2]
        vf_ref[...] = vel_ref[...].astype(F32).reshape(2 * levels * vlines, width)
        slopes = element_slopes(f)
        turned, moved = [], []
        for node in (3 * side, 1 + side):
            row = node + side * (vlines - 4)
            vx = vf_ref[pl.ds(row, levels, stride=vlines), :]
            vy = vf_ref[pl.ds(levels * vlines + row, levels, stride=vlines), :]
            high, low = split(f[node])
            sy = jnp.dot(
                jnp.concatenate([high, low, high], axis=1), dcat_ref[...],
                preferred_element_type=F32,
            )
            vx = jnp.concatenate([vx] * fields, axis=0)
            vy = jnp.concatenate([vy] * fields, axis=0)
            line = (vx * slopes[node] + vy * sy) * (-TIME_STEP * jnp.sqrt(mass[p : p + 1]))
            line = line + copies_along_y(line)
            moved.append(line)
            turned.append(line.T)
        out_ref[0:features, :] = moved[0]
        out_ref[features : 2 * features, :] = CELL_WEIGHTS[0] * f[3 * side] + CELL_WEIGHTS[1] * (
            f[1 + side] + moved[1] * inside[p : p + 1]
        )
        out_ref[2 * features : 2 * features + 16, :] = jnp.concatenate(
            [
                turned[0][0:1],
                turned[0][width - 1 : width],
                joined[p : p + 1],
                jnp.broadcast_to(jac[p : p + 1, 0:1], (1, width)),
                jnp.broadcast_to(jac[p : p + 1, elements_y - 1 : elements_y], (1, width)),
                turned[1][0:1],
                turned[1][width - 1 : width],
                jnp.broadcast_to(lit, (1, width)),
                mass[p : p + 1],
                jnp.zeros((7, width), F32),
            ],
            axis=0,
        )


def dynamics_kernel(
    prog_ref, vel_ref, jac_ref, dcat_ref, adv_ref, ylo_ref, yhi_ref,
    sy3_ref, vf3_ref, pf3_ref, scale_ref, inside_ref, shared_ref, zlo_ref, zhi_ref,
):
    step = pl.program_id(0)
    _, tile, width_x, width = prog_ref.shape
    elements_x, elements_y = jac_ref.shape
    features = zlo_ref.shape[0]
    levels = features // 2
    planes = 2 * tile
    pitch = sy3_ref.shape[1]
    sy_ref = sy3_ref.reshape(planes * pitch, width)
    vf_ref = vf3_ref.reshape(planes * pitch, width)
    pf_ref = pf3_ref.reshape(planes * pitch, width)

    @pl.when(step == 0)
    def _():
        mass = along_lanes(jac_ref[...], width)
        scale_ref[...] = -TIME_STEP * jnp.sqrt(mass)
        inside, shared = inner_reciprocals(mass + copies_along_y(mass))
        inside_ref[...] = inside
        shared_ref[...] = shared

    vf3_ref[:, 0:width_x, :] = vel_ref[...].astype(F32).reshape(planes, width_x, width)
    piece = planes // 4
    for at in range(4):
        first = at * piece
        values = prog_ref[first // tile, first % tile : first % tile + piece]
        pf3_ref[first : first + piece, 0:width_x, :] = values
        high, low = split(values.reshape(piece * width_x, width))
        sy3_ref[first : first + piece, 0:width_x, :] = jnp.dot(
            jnp.concatenate([high, low, high], axis=1), dcat_ref[...], preferred_element_type=F32
        ).reshape(piece, width_x, width)

    lane = iota((tile, width), 1)

    def rims(lines):
        first, second, third = lines
        a = pltpu.roll(first, 1, 1)
        b = pltpu.roll(second, 2, 1)
        c = pltpu.roll(third, 3, 1)

        def pick(base):
            return jnp.where(
                lane == base, first,
                jnp.where(
                    lane == (base + 1) % width, a,
                    jnp.where(
                        lane == (base + 2) % width, b, jnp.where(lane == (base + 3) % width, c, 0.0)
                    ),
                ),
            )

        return pick(0), pick(width - 1)

    def element(p, carry):
        scale = scale_ref[p : p + 1, :]
        inside = inside_ref[p : p + 1, :]
        shared = shared_ref[p : p + 1, :]
        shift = (4 * p + width - 1) % width
        vx = [vf_ref[pl.ds(4 * p + k, tile, stride=pitch), :] for k in range(4)]
        vy = [
            vf_ref[pl.ds(tile * pitch + 4 * p + k, tile, stride=pitch), :] for k in range(4)
        ]
        out = []
        for v in range(2):
            last_e, last_f, z_low, z_high = carry[4 * v : 4 * v + 4]
            base = v * tile * pitch + 4 * p
            f = [pf_ref[pl.ds(base + k, tile, stride=pitch), :] for k in range(4)]
            sy = [sy_ref[pl.ds(base + k, tile, stride=pitch), :] for k in range(4)]
            sx = element_slopes(f)
            e = []
            for k in range(4):
                moved = (vx[k] * sx[k] + vy[k] * sy[k]) * scale
                e.append(moved + copies_along_y(moved))
            joined = last_e + e[0]
            gain = joined * shared
            adv_ref[4 * p, v] = f[0] + gain
            adv_ref[4 * p + 1, v] = f[1] + e[1] * inside
            adv_ref[4 * p + 2, v] = f[2] + e[2] * inside

            if p > 0:
                adv_ref[4 * p - 1, v] = last_f + gain

            low, high = rims((joined, e[1], e[2]))
            out += [
                e[3], f[3],
                z_low + pltpu.roll(low, shift, 1), z_high + pltpu.roll(high, shift, 1),
            ]
        return tuple(out)

    zero = jnp.zeros((tile, width), F32)
    final = (zero,) * 8
    for p in range(elements_x):
        final = element(p, final)
    for v in range(2):
        last_e, last_f, z_low, z_high = final[4 * v : 4 * v + 4]
        at = pl.ds(pl.multiple_of(v * levels + tile * step, tile), tile)
        adv_ref[width_x - 1, v] = last_f
        zlo_ref[at, :] = jnp.where(
            lane == width_x - 1, pltpu.roll(last_e, width_x - 1, 1), z_low
        )
        zhi_ref[at, :] = pltpu.roll(
            jnp.where(lane == width_x - 2, pltpu.roll(last_e, width_x - 1, 1), z_high), 1, 1
        )

    @pl.when(step == pl.num_programs(0) - 1)
    def _():
        jac = jac_ref[...]
        ylo_ref[...] = zlo_ref[...].T
        yhi_ref[...] = zhi_ref[...].T
        for ref, q in ((ylo_ref, 0), (yhi_ref, elements_y - 1)):
            ref[width_x : width_x + elements_x, :] = jnp.broadcast_to(
                jac[:, q : q + 1], (elements_x, features)
            )


def cells_kernel(capacity, devices, adv_ref, span_ref, col_ref, slot_ref):
    group = adv_ref.shape[0] // 4
    width = adv_ref.shape[3]
    features = adv_ref.shape[1] * adv_ref.shape[2]
    elements_x, elements_y = span_ref.shape
    elements = elements_x * elements_y

    @pl.when(pl.program_id(0) == 0)
    def _():
        lane = iota((elements_y, elements), 1)
        tiled = lax.rem(lane, elements_y) == iota((elements_y, elements), 0)
        spread = jnp.dot(
            span_ref[...].astype(F32).astype(BF16), tiled.astype(BF16), preferred_element_type=F32
        )
        start = iota((elements_x, elements), 0) * elements_y
        at = iota((elements_x, elements), 1)
        own = (at >= start) & (at < start + elements_y)
        target = jnp.sum(jnp.where(own, spread, 0.0), axis=0, keepdims=True)
        chosen = jnp.where(
            target == iota((devices, elements), 0).astype(F32), 1.0, 0.0
        )
        before = iota((elements, elements), 0) < iota((elements, elements), 1)
        earlier = jnp.dot(
            chosen.astype(BF16), before.astype(BF16), preferred_element_type=F32
        )
        rank = jnp.sum(chosen * earlier, axis=0, keepdims=True)
        slot_ref[...] = (target * capacity + rank).astype(jnp.int32)

    select = select_cells(elements_y, width)
    for p in range(group):
        for a in range(2):
            line = adv_ref[4 * p + 2 * a] * CELL_WEIGHTS[2 * a]
            line += adv_ref[4 * p + 2 * a + 1] * CELL_WEIGHTS[2 * a + 1]
            low, high = cells_of_line(line.reshape(features, width), select)
            at = slice(p * elements_y, (p + 1) * elements_y)
            col_ref[2 * a, at, :] = low
            col_ref[2 * a + 1, at, :] = high


def select_cells(elements_y, width):
    shape = (2 * elements_y, width)
    row, lane = iota(shape, 0), iota(shape, 1)
    wanted = jnp.where(row < elements_y, 4 * row, 4 * (row - elements_y) + 2)
    return (lane == wanted).astype(BF16)


def cells_of_line(line, select):
    features, width = line.shape
    inner = (iota((1, width), 1) & 3)
    line = line * jnp.where((inner == 0) | (inner == 3), 1.0 / 6.0, 5.0 / 6.0)
    line = line + pltpu.roll(line, width - 1, 1)
    high, low = split(line)
    both = lax.dot_general(
        select, jnp.concatenate([high, low], axis=0), (((1,), (1,)), ((), ())),
        preferred_element_type=F32,
    )
    cells = both[:, :features] + both[:, features:]
    half = select.shape[0] // 2
    return cells[:half], cells[half:]


def corners_kernel(width_x, elements_x, ylo_ref, yhi_ref, prev_ref, next_ref, ylo_out, yhi_out):
    tail = prev_ref.shape[0] - 16
    spare = width_x + elements_x
    for side, (ref, out) in enumerate(((ylo_ref, ylo_out), (yhi_ref, yhi_out))):
        row = iota(ref.shape, 0)
        values = ref[...]
        for k, (packet, x) in enumerate(((prev_ref, 0), (next_ref, width_x - 1))):
            rim = packet[tail + side : tail + side + 1, :]
            mass = packet[tail + 3 + side : tail + 4 + side, :]
            inner = packet[tail + 5 + side : tail + 6 + side, :]
            values = values + jnp.where(row == x, rim, 0.0)
            values = jnp.where(row == spare + k, mass, values)
            values = jnp.where(row == spare + 2 + k, inner, values)
        out[...] = values


def complete_kernel(
    width_x, elements_x,
    col_ref, xlo_ref, xhi_ref, prev_ref, next_ref, ylo_ref, yhi_ref, yprev_ref,
    ynext_ref, colbf_ref, fy_ref, ry_ref, fx_ref, rx_ref, ghost_ref, work_ref, cell_ref,
):
    _, elements, features = col_ref.shape
    tail = 2 * features
    ghost_fixes = []
    elements_y = elements // elements_x
    width = xlo_ref.shape[1]
    work_ref[...] = col_ref[...]
    select = select_cells(elements_y, width)
    lane = iota((1, width), 1)
    inner = (lane > 0) & (lane < width - 1)
    for side, (own, other) in enumerate(((ylo_ref, yprev_ref), (yhi_ref, ynext_ref))):
        total = own[...] + other[...]
        mass = total[width_x : width_x + elements_x]
        row = iota(mass.shape, 0)
        spare = width_x + elements_x
        before = jnp.where(row == 0, total[spare : spare + 1], pltpu.roll(mass, 1, 0))
        after = jnp.where(
            row == elements_x - 1, total[spare + 1 : spare + 2], pltpu.roll(mass, elements_x - 1, 0)
        )
        inside = 1.0 / mass
        ry_ref[side, pl.ds(0, elements_x, stride=4), :] = 1.0 / (mass + before)
        ry_ref[side, pl.ds(1, elements_x, stride=4), :] = inside
        ry_ref[side, pl.ds(2, elements_x, stride=4), :] = inside
        ry_ref[side, pl.ds(3, elements_x, stride=4), :] = 1.0 / (mass + after)
        fy_ref[side] = total[:width_x] * ry_ref[side]
        ghost_fixes.append(total[spare + 2 : spare + 4] / total[spare : spare + 2])
        fixes = [fy_ref[side, pl.ds(k, elements_x, stride=4), :] for k in range(4)]
        at = pl.ds(side * (elements_y - 1), elements_x, stride=elements_y)
        for a in range(2):
            added = CELL_WEIGHTS[2 * a] * fixes[2 * a] + CELL_WEIGHTS[2 * a + 1] * fixes[2 * a + 1]
            k = 2 * a + side
            work_ref[k, at, :] = work_ref[k, at, :] + CELL_WEIGHTS[0] * added
    for side, (own, other) in enumerate(((xlo_ref, prev_ref), (xhi_ref, next_ref))):
        mass = own[tail + 2 : tail + 3, :] + other[tail + 2 : tail + 3, :]
        reciprocal = jnp.where(inner, 1.0 / mass, 0.0)
        rx_ref[side] = jnp.broadcast_to(reciprocal, (8, width))
        fix = (own[:features] + other[:features]) * reciprocal
        fx_ref[side] = fix
        low, high = cells_of_line(CELL_WEIGHTS[0] * fix, select)
        at = slice(side * (elements_x - 1) * elements_y, (side * (elements_x - 1) + 1) * elements_y)
        work_ref[2 * side, at, :] = work_ref[2 * side, at, :] + low
        work_ref[2 * side + 1, at, :] = work_ref[2 * side + 1, at, :] + high
        line = other[features : 2 * features] + CELL_WEIGHTS[0] * fix
        cell_ref[2 * side], cell_ref[2 * side + 1] = cells_of_line(line, select)
        for end in range(2):
            x = side * (width_x - 1)
            added = CELL_WEIGHTS[0] * fy_ref[end, x : x + 1, :]
            added = added + CELL_WEIGHTS[1] * ghost_fixes[end][side : side + 1]
            q = end * (elements_y - 1)
            cell_ref[2 * side + end, q : q + 1, :] = (
                cell_ref[2 * side + end, q : q + 1, :] + CELL_WEIGHTS[0] * added
            )
    for k in range(4):
        ghost_ref[k * elements_y : (k + 1) * elements_y, :] = cell_ref[k].astype(BF16)
    for k in range(4):
        colbf_ref[:, k * features : (k + 1) * features] = work_ref[k].astype(BF16)


def send_kernel(colbf_ref, slot_ref, out_ref):
    elements = colbf_ref.shape[0]
    slots = out_ref.shape[0]
    piece = slots // 4
    for part in range(4):
        chosen = (iota((piece, elements), 0) + part * piece) == slot_ref[...]
        chosen = jnp.where(chosen, 1.0, 0.0)
        filled = jnp.max(chosen, axis=1, keepdims=True)
        moved = jnp.dot(chosen.astype(BF16), colbf_ref[...], preferred_element_type=F32)
        out_ref[pl.ds(part * piece, piece), :] = jnp.where(filled > 0.0, moved, EMPTY).astype(BF16)


def dense(inputs, weight_ref, bias_ref):
    return jnp.dot(inputs, weight_ref[...], preferred_element_type=F32) + bias_ref[...]


def leaky(values):
    return jnp.maximum(values, LEAK_SLOPE * values).astype(BF16)


def network_kernel(
    lit_ref, col_ref, ghost_ref, prev_ref, next_ref, w1, b1, w2, b2, w3, b3, w4, b4, s1, c1, s2,
    c2, s3, c3, inc_ref, ghost_inc_ref, total_ref,
):
    rows = col_ref.shape[0]
    features = col_ref.shape[1] // 4
    inputs = jnp.concatenate(
        [col_ref[:, k * features : (k + 1) * features] for k in range(4)], axis=0
    )
    total_ref[...] = primary(inputs, w1, b1, w2, b2, w3, b3, w4, b4)

    @pl.when(lit_ref[0, 0] != 0)
    def _():
        total_ref[...] += lit_ref[0, 0].astype(F32) * solar(inputs, s1, c1, s2, c2, s3, c3)

    for k in range(4):
        inc_ref[:, k * features : (k + 1) * features] = total_ref[
            k * rows : (k + 1) * rows, :
        ].astype(BF16)

    @pl.when(pl.program_id(0) == 0)
    def _():
        near = ghost_ref[...]
        tail = 2 * features + 7
        row = iota(near.shape, 0)
        lit = jnp.where(
            row < near.shape[0] // 2, prev_ref[tail : tail + 1, :], next_ref[tail : tail + 1, :]
        )
        near_inc = primary(near, w1, b1, w2, b2, w3, b3, w4, b4)
        near_inc = near_inc + lit * solar(near, s1, c1, s2, c2, s3, c3)
        ghost_inc_ref[...] = near_inc.astype(BF16)


def primary(inputs, w1, b1, w2, b2, w3, b3, w4, b4):
    hidden = leaky(dense(inputs, w1, b1))
    hidden = leaky(dense(hidden, w2, b2))
    hidden = leaky(dense(hidden, w3, b3))
    return dense(hidden, w4, b4)


def solar(inputs, s1, c1, s2, c2, s3, c3):
    hidden = leaky(dense(inputs, s1, c1))
    hidden = leaky(dense(hidden, s2, c2))
    return dense(hidden, s3, c3)


def spread_operand(mass_line, elements_y):
    width = mass_line.shape[1]
    shape = (2 * elements_y, width)
    row, lane = iota(shape, 0), iota(shape, 1)
    upper = row >= elements_y
    q = jnp.where(upper, row - elements_y, row)
    b = jnp.where(upper, 1, 0)
    own = (lane >> 1) == 2 * q + b
    copy = lane == jnp.where(upper, 4 * q + 4, 4 * q - 1)
    weights = jnp.where(
        own, mass_line, jnp.where(copy, copies_along_y(mass_line), 0.0)
    )
    high, low = split(weights)
    return jnp.concatenate([high, low], axis=0)


def spread_line(inc_ref, p, a, operand, elements_y):
    features = inc_ref.shape[1] // 4
    start = p * elements_y
    if not isinstance(p, int):
        start = pl.multiple_of(start, elements_y)
    at = pl.ds(start, elements_y)
    cells = [
        inc_ref[at, (2 * a + b) * features : (2 * a + b + 1) * features] for b in range(2)
    ]
    return spread_cells(cells, operand)


def spread_cells(cells, operand):
    return lax.dot_general(
        jnp.concatenate(cells + cells, axis=0), operand, (((0,), (0,)), ((), ())),
        preferred_element_type=F32,
    )


def rims_kernel(inc_ref, near_ref, jac_ref, prev_ref, next_ref, ylo_ref, yhi_ref, wide_ref):
    elements_x, elements_y = jac_ref.shape
    features = near_ref.shape[1]
    width_x = 4 * elements_x
    tail = 2 * features
    for k in range(4):
        wide_ref[k] = inc_ref[:, k * features : (k + 1) * features].astype(F32)
    near = near_ref[...].astype(F32)
    for side, ref in enumerate((ylo_ref, yhi_ref)):
        q = side * (elements_y - 1)
        column = jac_ref[:, q : q + 1]
        at = pl.ds(q, elements_x, stride=elements_y)
        first = column * wide_ref[side, at, :]
        second = column * wide_ref[2 + side, at, :]
        ghosts = []
        for k, packet in enumerate((prev_ref, next_ref)):
            cell = (2 * k + side) * elements_y + q
            mass = packet[tail + 3 + side : tail + 4 + side, :]
            ghosts.append(mass * near[cell : cell + 1])
        row = iota(first.shape, 0)
        ref[pl.ds(0, elements_x, stride=4), :] = first + jnp.where(
            row == 0, ghosts[0], pltpu.roll(second, 1, 0)
        )
        ref[pl.ds(1, elements_x, stride=4), :] = first
        ref[pl.ds(2, elements_x, stride=4), :] = second
        ref[pl.ds(3, elements_x, stride=4), :] = second + jnp.where(
            row == elements_x - 1, ghosts[1], pltpu.roll(first, elements_x - 1, 0)
        )
        ref[width_x:, :] = jnp.zeros((ref.shape[0] - width_x, features), F32)


def final_kernel(
    adv_ref, inc_ref, near_ref, jac_ref, prev_ref, next_ref, ylo_ref, yhi_ref, yprev_ref,
    ynext_ref, fy_ref, ry_ref, fx_ref, rx_ref, out_ref, mass_ref, inside_ref, shared_ref,
    rim_ref, edge_ref,
):
    step = pl.program_id(0)
    elements_x, elements_y = jac_ref.shape
    width_x = 4 * elements_x
    lines = adv_ref.shape[0]
    group = lines // 4
    width = adv_ref.shape[3]
    features = adv_ref.shape[1] * adv_ref.shape[2]

    @pl.when(step == 0)
    def _():
        mass = along_lanes(jac_ref[...], width)
        mass_ref[...] = mass
        inside, shared = inner_reciprocals(mass + copies_along_y(mass))
        inside_ref[...] = inside
        shared_ref[0:elements_x, :] = shared
        shared_ref[elements_x:, :] = jnp.zeros((8, width), F32)
        for side, (own, other) in enumerate(((ylo_ref, yprev_ref), (yhi_ref, ynext_ref))):
            rim_ref[side] = fy_ref[side] + (own[0:width_x, :] + other[0:width_x, :]) * ry_ref[side]
        for side, packet in enumerate((prev_ref, next_ref)):
            p = side * (elements_x - 1)
            own = spread_line(
                inc_ref, p, side, spread_operand(mass[p : p + 1], elements_y), elements_y
            )
            tail = 2 * features + 8
            at = 2 * side * elements_y
            other = spread_cells(
                [near_ref[at : at + 2 * elements_y, :]],
                spread_operand(packet[tail : tail + 1, :], elements_y),
            )
            edge_ref[side] = fx_ref[side] + (own + other) * rx_ref[side, 0:1, :]

    out = out_ref.reshape(features * lines, width)
    row = iota((16, width), 0)
    lane = iota((16, width), 1)
    place = (((row < 2) & (lane == 0)) | ((row >= 2) & (row < 4) & (lane == width - 1))).astype(BF16)

    def rim_of(x):
        low = rim_ref[0, pl.ds(x, 1), :]
        high = rim_ref[1, pl.ds(x, 1), :]
        parts = jnp.where(row < 2, low, high)
        rough = parts.astype(BF16).astype(F32)
        rest = parts - rough
        stacked = jnp.where((row == 0) | (row == 2), rough, jnp.where(row < 4, rest, 0.0))
        return lax.dot_general(
            stacked.astype(BF16), place, (((0,), (0,)), ((), ())), preferred_element_type=F32
        )

    def line_of(p, a):
        operand = spread_operand(mass_ref[pl.ds(p, 1), :], elements_y)
        return spread_line(inc_ref, p, a, operand, elements_y)

    def store(at, values):
        out[pl.ds(at, features, stride=lines), :] = adv_ref[at].reshape(features, width) + values

    first = step * group
    before = line_of(jnp.maximum(first - 1, 0), 1)
    here = line_of(first, 0)
    joint = (before + here) * shared_ref[pl.ds(first, 1), :] + rim_of(4 * first)
    for k in range(group):
        p = first + k
        inside = inside_ref[pl.ds(p, 1), :]
        store(4 * k, joint)
        store(4 * k + 1, here * inside + rim_of(4 * p + 1))
        there = line_of(p, 1)
        store(4 * k + 2, there * inside + rim_of(4 * p + 2))
        here = line_of(jnp.minimum(p + 1, elements_x - 1), 0)
        joint = (there + here) * shared_ref[pl.ds(p + 1, 1), :] + rim_of(4 * p + 3)
        store(4 * k + 3, joint)

    @pl.when(step == 0)
    def _():
        at = pl.ds(0, features, stride=lines)
        out[at, :] = out[at, :] + edge_ref[0]

    @pl.when(step == pl.num_programs(0) - 1)
    def _():
        at = pl.ds(lines - 1, features, stride=lines)
        out[at, :] = out[at, :] + edge_ref[1]


def arrange_kernel(capacity, data_ref, out_ref, wide_ref, rows_ref, vector_ref, start_ref, sem):
    devices = vector_ref.shape[0]
    slots = data_ref.shape[0]
    features = data_ref.shape[1] // 4
    elements = out_ref.shape[0] // 4
    filled = jnp.where(data_ref[:, 0:features].astype(F32) < 0.5 * EMPTY, 1.0, 0.0).astype(BF16)
    before = iota((devices, slots), 1) < iota((devices, slots), 0) * capacity
    starts = jnp.dot(
        jnp.where(before, 1.0, 0.0).astype(BF16), filled, preferred_element_type=F32
    )
    vector_ref[...] = jnp.clip(starts, 0.0, float(elements)).astype(jnp.int32)
    copy = pltpu.make_async_copy(vector_ref, start_ref, sem)
    copy.start()
    for k in range(4):
        wide_ref[k] = data_ref[:, k * features : (k + 1) * features].astype(F32)
    copy.wait()

    def one(s, carry):
        start = start_ref[s, 0]
        for k in range(4):
            rows_ref[pl.ds(4 * start + k, capacity, stride=4), :] = wide_ref[
                k, pl.ds(s * capacity, capacity), :
            ]
        return carry

    lax.fori_loop(0, devices, one, 0)
    out_ref[...] = rows_ref[0 : out_ref.shape[0], :].astype(BF16)


def params(mib):
    return pltpu.CompilerParams(vmem_limit_bytes=mib * MIB)


def whole(shape):
    return pl.BlockSpec(shape, lambda *_: (0,) * len(shape))


def cost(flops, bytes_accessed):
    return pl.CostEstimate(flops=flops, bytes_accessed=bytes_accessed, transcendentals=0)


def shape_of(shape, dtype=F32):
    return jax.ShapeDtypeStruct(shape, dtype)


def shifted(axis, by):
    count = lax.axis_size(axis)
    return [(i, (i + by) % count) for i in range(count)]


def edges_call(sunlit, prognostic, velocity, jacobian):
    fields, levels, width_x, width = prognostic.shape
    features = fields * levels
    last = width_x // 8 - 1, width_x // 16 - 1
    dcat = jnp.asarray(y_derivative_operand(width))
    return pl.pallas_call(
        edges_kernel,
        grid=(1,),
        in_specs=[
            pl.BlockSpec(memory_space=pltpu.SMEM),
            pl.BlockSpec((fields, levels, 8, width), lambda g: (0, 0, 0, 0)),
            pl.BlockSpec((fields, levels, 8, width), lambda g: (0, 0, last[0], 0)),
            pl.BlockSpec((2, levels, 16, width), lambda g: (0, 0, 0, 0)),
            pl.BlockSpec((2, levels, 16, width), lambda g: (0, 0, last[1], 0)),
            whole(jacobian.shape),
            whole((3 * width, width)),
        ],
        out_specs=[whole((2 * features + 16, width))] * 2,
        out_shape=[shape_of((2 * features + 16, width))] * 2,
        scratch_shapes=[pltpu.VMEM((2 * levels * 16, width), F32)],
        compiler_params=params(58),
        cost_estimate=cost(50_000_000, 2_000_000),
        name="edges",
    )(sunlit, prognostic, prognostic, velocity, velocity, jacobian, dcat)


def dynamics_call(prognostic, velocity, jacobian):
    fields, levels, width_x, width = prognostic.shape
    elements_x, elements_y = jacobian.shape
    features = fields * levels
    tile = 8
    dcat = jnp.asarray(y_derivative_operand(width))
    return pl.pallas_call(
        dynamics_kernel,
        grid=(levels // tile,),
        in_specs=[
            pl.BlockSpec((2, tile, width_x, width), lambda t: (0, t, 0, 0)),
            pl.BlockSpec((2, tile, width_x, width), lambda t: (0, t, 0, 0)),
            whole((elements_x, elements_y)),
            whole((3 * width, width)),
        ],
        out_specs=[
            pl.BlockSpec((width_x, 2, tile, width), lambda t: (0, 0, t, 0)),
            whole((width, features)),
            whole((width, features)),
        ],
        out_shape=[
            shape_of((width_x, fields, levels, width)),
            shape_of((width, features)),
            shape_of((width, features)),
        ],
        scratch_shapes=[
            pltpu.VMEM((2 * tile, width_x + 8, width), F32),
            pltpu.VMEM((2 * tile, width_x + 8, width), F32),
            pltpu.VMEM((2 * tile, width_x + 8, width), F32),
            pltpu.VMEM((elements_x, width), F32),
            pltpu.VMEM((elements_x, width), F32),
            pltpu.VMEM((elements_x, width), F32),
            pltpu.VMEM((features, width), F32),
            pltpu.VMEM((features, width), F32),
        ],
        compiler_params=params(58),
        cost_estimate=cost(2_000_000_000, 16_000_000),
        name="dynamics",
    )(prognostic, velocity, jacobian, dcat)


def on_device(
    prognostic,
    velocity,
    jacobian,
    element_span,
    sunlit,
    *weights,
):
    fields, levels, width_x, width = prognostic.shape
    elements_x, elements_y = jacobian.shape
    features = fields * levels
    elements = elements_x * elements_y
    devices = lax.axis_size("face") * lax.axis_size("dom")
    capacity = max(2, 2 * elements // devices)
    slots = devices * capacity
    packet = 2 * features + 16
    vmem = pl.BlockSpec(memory_space=pltpu.VMEM)
    smem = pl.BlockSpec(memory_space=pltpu.SMEM)

    xlo, xhi = edges_call(sunlit, prognostic, velocity, jacobian)
    adv, ylo, yhi = dynamics_call(prognostic, velocity, jacobian)

    group = 4
    col, slot_ids = pl.pallas_call(
        lambda *refs: cells_kernel(capacity, devices, *refs),
        grid=(elements_x // group,),
        in_specs=[
            pl.BlockSpec((4 * group, fields, levels, width), lambda g: (g, 0, 0, 0)),
            whole((elements_x, elements_y)),
        ],
        out_specs=[
            pl.BlockSpec((4, group * elements_y, features), lambda g: (0, g, 0)),
            whole((1, elements)),
        ],
        out_shape=[
            shape_of((4, elements, features)),
            shape_of((1, elements), jnp.int32),
        ],
        compiler_params=params(20),
        cost_estimate=cost(1_000_000_000, 8_000_000),
        name="cells",
    )(adv, element_span)

    prev = lax.ppermute(xhi, "face", shifted("face", 1))
    later = lax.ppermute(xlo, "face", shifted("face", -1))
    ylo, yhi = pl.pallas_call(
        lambda *refs: corners_kernel(width_x, elements_x, *refs),
        in_specs=[vmem] * 4,
        out_specs=[vmem] * 2,
        out_shape=[shape_of((width, features))] * 2,
        compiler_params=params(12),
        name="corners",
    )(ylo, yhi, prev, later)
    yprev = lax.ppermute(yhi, "dom", shifted("dom", 1))
    ynext = lax.ppermute(ylo, "dom", shifted("dom", -1))

    colbf, fy, ry, fx, rx, ghosts = pl.pallas_call(
        lambda *refs: complete_kernel(width_x, elements_x, *refs),
        in_specs=[vmem] * 9,
        out_specs=[vmem] * 6,
        out_shape=[
            shape_of((elements, 4 * features), BF16),
            shape_of((2, width_x, features)),
            shape_of((2, width_x, features)),
            shape_of((2, features, width)),
            shape_of((2, 8, width)),
            shape_of((4 * elements_y, features), BF16),
        ],
        scratch_shapes=[
            pltpu.VMEM((4, elements, features), F32),
            pltpu.VMEM((4, elements_y, features), F32),
        ],
        compiler_params=params(16),
        cost_estimate=cost(10_000_000, 3_000_000),
        name="complete",
    )(col, xlo, xhi, prev, later, ylo, yhi, yprev, ynext)

    chunk = elements // 3
    hidden = weights[0].shape[1]
    operands, operand_specs = [], []
    for item in weights:
        item = item if item.ndim == 2 else item.reshape(1, -1)
        operands.append(item)
        operand_specs.append(whole(item.shape))
    outgoing = pl.pallas_call(
        send_kernel,
        in_specs=[vmem] * 2,
        out_specs=vmem,
        out_shape=shape_of((slots, 4 * features), BF16),
        compiler_params=params(16),
        cost_estimate=cost(2_000_000_000, 3_000_000),
        name="send",
    )(colbf, slot_ids)

    arrived = lax.all_to_all(
        outgoing.reshape(devices, capacity, 4 * features), ("face", "dom"),
        split_axis=0, concat_axis=0, tiled=True,
    ).reshape(slots, 4 * features)

    inc, near = pl.pallas_call(
        network_kernel,
        grid=(3,),
        in_specs=[
            smem,
            pl.BlockSpec((chunk, 4 * features), lambda g: (g, 0)),
            whole((4 * elements_y, features)),
            whole((packet, width)),
            whole((packet, width)),
        ]
        + operand_specs,
        out_specs=[
            pl.BlockSpec((chunk, 4 * features), lambda g: (g, 0)),
            whole((4 * elements_y, features)),
        ],
        out_shape=[
            shape_of((elements, 4 * features), BF16),
            shape_of((4 * elements_y, features), BF16),
        ],
        scratch_shapes=[pltpu.VMEM((4 * chunk, features), F32)],
        compiler_params=params(24),
        cost_estimate=cost(8 * elements * (4 * features * hidden + 3 * hidden * hidden), 4_000_000),
        name="network",
    )(sunlit, colbf, ghosts, prev, later, *operands)

    ylo2, yhi2 = pl.pallas_call(
        rims_kernel,
        in_specs=[vmem] * 5,
        out_specs=[vmem] * 2,
        out_shape=[shape_of((width, features))] * 2,
        scratch_shapes=[pltpu.VMEM((4, elements, features), F32)],
        compiler_params=params(16),
        cost_estimate=cost(10_000_000, 2_000_000),
        name="rims",
    )(inc, near, jacobian, prev, later)
    yprev2 = lax.ppermute(yhi2, "dom", shifted("dom", 1))
    ynext2 = lax.ppermute(ylo2, "dom", shifted("dom", -1))

    new_state = pl.pallas_call(
        final_kernel,
        grid=(elements_x // group,),
        in_specs=[
            pl.BlockSpec((4 * group, fields, levels, width), lambda g: (g, 0, 0, 0)),
            whole((elements, 4 * features)),
            whole((4 * elements_y, features)),
            whole((elements_x, elements_y)),
            whole((packet, width)),
            whole((packet, width)),
            whole((width, features)),
            whole((width, features)),
            whole((width, features)),
            whole((width, features)),
            whole((2, width_x, features)),
            whole((2, width_x, features)),
            whole((2, features, width)),
            whole((2, 8, width)),
        ],
        out_specs=pl.BlockSpec((fields, levels, 4 * group, width), lambda g: (0, 0, g, 0)),
        out_shape=shape_of((fields, levels, width_x, width)),
        scratch_shapes=[
            pltpu.VMEM((elements_x, width), F32),
            pltpu.VMEM((elements_x, width), F32),
            pltpu.VMEM((elements_x + 8, width), F32),
            pltpu.VMEM((2, width_x, features), F32),
            pltpu.VMEM((2, features, width), F32),
        ],
        compiler_params=params(20),
        cost_estimate=cost(1_000_000_000, 14_000_000),
        name="final",
    )(
        adv, inc, near, jacobian, prev, later, ylo2, yhi2, yprev2, ynext2, fy, ry, fx, rx
    )

    span_state = pl.pallas_call(
        lambda *refs: arrange_kernel(capacity, *refs),
        in_specs=[vmem],
        out_specs=vmem,
        out_shape=shape_of((4 * elements, features), BF16),
        scratch_shapes=[
            pltpu.VMEM((4, slots, features), F32),
            pltpu.VMEM((4 * (elements + capacity), features), F32),
            pltpu.VMEM((devices, features), jnp.int32),
            pltpu.SMEM((devices, features), jnp.int32),
            pltpu.SemaphoreType.DMA,
        ],
        compiler_params=params(24),
        cost_estimate=cost(1_000_000, 3_000_000),
        name="arrange",
    )(arrived)
    return (new_state, span_state)


def solution(mesh):
    return jax.shard_map(
        on_device,
        mesh=mesh,
        in_specs=(
            P(None, None, "face", "dom"),
            P(None, None, "face", "dom"),
            P("face", "dom"),
            P("face", "dom"),
            P("face", "dom"),
        )
        + (P(),) * 14,
        out_specs=(P(None, None, "face", "dom"), P(("face", "dom"), None)),
        check_vma=False,
    )
```

```python
import jax
import jax.numpy as jnp
import numpy as np
from jax import lax
from jax.experimental import pallas as pl
from jax.experimental.pallas import tpu as pltpu
from jax.sharding import PartitionSpec as P

TIME_STEP = 0.1
LEAK_SLOPE = 0.15
F32 = jnp.float32
BF16 = jnp.bfloat16
HIGHEST = lax.Precision.HIGHEST
CELL_WEIGHTS = (1.0 / 6.0, 5.0 / 6.0, 5.0 / 6.0, 1.0 / 6.0)
MIB = 1024 * 1024
EMPTY = 1e30


def derivative_matrix():
    points = np.array([-1.0, -1.0 / np.sqrt(5.0), 1.0 / np.sqrt(5.0), 1.0])
    legendre = (5.0 * points**3 - 3.0 * points) / 2.0
    derivative = np.zeros((4, 4))
    for i in range(4):
        for k in range(4):
            if i != k:
                derivative[i, k] = legendre[i] / (legendre[k] * (points[i] - points[k]))
    derivative[0, 0] = -3.0
    derivative[3, 3] = 3.0
    return derivative


D = derivative_matrix()


def y_derivative_operand(width):
    full = np.kron(np.eye(width // 4), D.T).astype(np.float32)
    high = full.astype(jnp.bfloat16)
    low = (full - high.astype(np.float32)).astype(jnp.bfloat16)
    return np.concatenate([high, high, low], axis=0)


def iota(shape, dim):
    return lax.broadcasted_iota(jnp.int32, shape, dim)


def split(values):
    high = values.astype(BF16)
    return high, (values - high.astype(F32)).astype(BF16)


def copies_along_y(values):
    width = values.shape[-1]
    lane = iota((1, width), 1)
    up = ((lane & 3) == 3) & (lane < width - 1)
    down = ((lane & 3) == 0) & (lane > 0)
    return jnp.where(
        up, pltpu.roll(values, width - 1, 1), jnp.where(down, pltpu.roll(values, 1, 1), 0.0)
    )


def along_lanes(jac, width):
    expand = (iota((jac.shape[1], width), 1) >> 2) == iota((jac.shape[1], width), 0)
    return jnp.dot(jac, expand.astype(F32), precision=HIGHEST, preferred_element_type=F32)


def inner_reciprocals(mass):
    width = mass.shape[1]
    lane = iota(mass.shape, 1)
    row = iota(mass.shape, 0)
    inner = (lane > 0) & (lane < width - 1)
    inside = jnp.where(inner, 1.0 / mass, 0.0)
    shared = jnp.where(inner & (row > 0), 1.0 / (mass + pltpu.roll(mass, 1, 0)), 0.0)
    return inside, shared


def element_slopes(f):
    outer_gap, inner_gap = f[0] - f[3], f[1] - f[2]
    bend = (f[1] + f[2]) - (f[0] + f[3])
    odd = (D[0, 0] - D[0, 3]) / 2 * outer_gap + (D[0, 1] - D[0, 2]) / 2 * inner_gap
    even = (D[0, 1] + D[0, 2]) / 2 * bend
    odd_in = (D[1, 0] - D[1, 3]) / 2 * outer_gap - D[1, 2] / 2 * inner_gap
    even_in = D[1, 2] / 2 * bend
    return [odd + even, odd_in + even_in, odd_in - even_in, odd - even]


def edges_kernel(
    lit_ref, proglo_ref, proghi_ref, vello_ref, velhi_ref, jac_ref, dcat_ref, xlo_ref, xhi_ref,
    vf_ref,
):
    elements_x, elements_y = jac_ref.shape
    fields, levels, _, width = proglo_ref.shape
    features = fields * levels
    jac = jac_ref[...]
    mass = along_lanes(jac, width)
    joined = mass + copies_along_y(mass)
    inside, _ = inner_reciprocals(joined)
    lit = lit_ref[0, 0].astype(F32)
    sides = ((proglo_ref, vello_ref, xlo_ref), (proghi_ref, velhi_ref, xhi_ref))
    for side, (prog_ref, vel_ref, out_ref) in enumerate(sides):
        p = side * (elements_x - 1)
        lines = prog_ref.shape[2]
        prog = prog_ref.reshape(features * lines, width)
        first = side * (lines - 4)
        f = [prog[pl.ds(first + k, features, stride=lines), :] for k in range(4)]
        vlines = vel_ref.shape[2]
        vf_ref[...] = vel_ref[...].astype(F32).reshape(2 * levels * vlines, width)
        slopes = element_slopes(f)
        turned, moved = [], []
        for node in (3 * side, 1 + side):
            row = node + side * (vlines - 4)
            vx = vf_ref[pl.ds(row, levels, stride=vlines), :]
            vy = vf_ref[pl.ds(levels * vlines + row, levels, stride=vlines), :]
            high, low = split(f[node])
            sy = jnp.dot(
                jnp.concatenate([high, low, high], axis=1), dcat_ref[...],
                preferred_element_type=F32,
            )
            vx = jnp.concatenate([vx] * fields, axis=0)
            vy = jnp.concatenate([vy] * fields, axis=0)
            line = (vx * slopes[node] + vy * sy) * (-TIME_STEP * jnp.sqrt(mass[p : p + 1]))
            line = line + copies_along_y(line)
            moved.append(line)
            turned.append(line.T)
        out_ref[0:features, :] = moved[0]
        out_ref[features : 2 * features, :] = CELL_WEIGHTS[0] * f[3 * side] + CELL_WEIGHTS[1] * (
            f[1 + side] + moved[1] * inside[p : p + 1]
        )
        out_ref[2 * features : 2 * features + 16, :] = jnp.concatenate(
            [
                turned[0][0:1],
                turned[0][width - 1 : width],
                joined[p : p + 1],
                jnp.broadcast_to(jac[p : p + 1, 0:1], (1, width)),
                jnp.broadcast_to(jac[p : p + 1, elements_y - 1 : elements_y], (1, width)),
                turned[1][0:1],
                turned[1][width - 1 : width],
                jnp.broadcast_to(lit, (1, width)),
                mass[p : p + 1],
                jnp.zeros((7, width), F32),
            ],
            axis=0,
        )


def dynamics_kernel(
    prog_hbm, vel_hbm, jac_ref, dcat_ref, adv_ref, ylo_ref, yhi_ref, prog_ref, vel_ref,
    sy3_ref, vf3_ref, pf3_ref, scale_ref, inside_ref, shared_ref, zlo_ref, zhi_ref, sems,
):
    _, levels, width_x, width = prog_ref.shape
    tile = sy3_ref.shape[0] // 2
    steps = levels // tile
    elements_x, elements_y = jac_ref.shape
    features = zlo_ref.shape[0]
    planes = 2 * tile
    pitch = sy3_ref.shape[1]
    sy_ref = sy3_ref.reshape(planes * pitch, width)
    vf_ref = vf3_ref.reshape(planes * pitch, width)
    pf_ref = pf3_ref.reshape(planes * pitch, width)

    def copies(step):
        at = pl.ds(step * tile, tile)
        return (
            pltpu.make_async_copy(prog_hbm.at[:, at], prog_ref.at[:, at], sems.at[0, step]),
            pltpu.make_async_copy(vel_hbm.at[:, at], vel_ref.at[:, at], sems.at[1, step]),
        )

    for step in range(steps):
        for copy in copies(step):
            copy.start()

    mass = along_lanes(jac_ref[...], width)
    scale_ref[...] = -TIME_STEP * jnp.sqrt(mass)
    inside, shared = inner_reciprocals(mass + copies_along_y(mass))
    inside_ref[...] = inside
    shared_ref[...] = shared

    def one_tile(step):
        level = pl.ds(pl.multiple_of(step * tile, tile), tile)
        vf3_ref[:, 0:width_x, :] = vel_ref[:, pl.ds(step * tile, tile)].astype(F32).reshape(
            planes, width_x, width
        )
        piece = planes // 4
        for at in range(4):
            first = at * piece
            values = prog_ref[first // tile, pl.ds(step * tile + first % tile, piece)]
            pf3_ref[first : first + piece, 0:width_x, :] = values
            high, low = split(values.reshape(piece * width_x, width))
            sy3_ref[first : first + piece, 0:width_x, :] = jnp.dot(
                jnp.concatenate([high, low, high], axis=1), dcat_ref[...], preferred_element_type=F32
            ).reshape(piece, width_x, width)

        lane = iota((tile, width), 1)

        def rims(lines):
            first, second, third = lines
            a = pltpu.roll(first, 1, 1)
            b = pltpu.roll(second, 2, 1)
            c = pltpu.roll(third, 3, 1)

            def pick(base):
                return jnp.where(
                    lane == base, first,
                    jnp.where(
                        lane == (base + 1) % width, a,
                        jnp.where(
                            lane == (base + 2) % width, b, jnp.where(lane == (base + 3) % width, c, 0.0)
                        ),
                    ),
                )

            return pick(0), pick(width - 1)

        def element(p, carry):
            scale = scale_ref[p : p + 1, :]
            inside = inside_ref[p : p + 1, :]
            shared = shared_ref[p : p + 1, :]
            shift = (4 * p + width - 1) % width
            vx = [vf_ref[pl.ds(4 * p + k, tile, stride=pitch), :] for k in range(4)]
            vy = [
                vf_ref[pl.ds(tile * pitch + 4 * p + k, tile, stride=pitch), :] for k in range(4)
            ]
            out = []
            for v in range(2):
                last_e, last_f, z_low, z_high = carry[4 * v : 4 * v + 4]
                base = v * tile * pitch + 4 * p
                f = [pf_ref[pl.ds(base + k, tile, stride=pitch), :] for k in range(4)]
                sy = [sy_ref[pl.ds(base + k, tile, stride=pitch), :] for k in range(4)]
                sx = element_slopes(f)
                e = []
                for k in range(4):
                    moved = (vx[k] * sx[k] + vy[k] * sy[k]) * scale
                    e.append(moved + copies_along_y(moved))
                joined = last_e + e[0]
                gain = joined * shared
                adv_ref[4 * p, v, level, :] = f[0] + gain
                adv_ref[4 * p + 1, v, level, :] = f[1] + e[1] * inside
                adv_ref[4 * p + 2, v, level, :] = f[2] + e[2] * inside

                if p > 0:
                    adv_ref[4 * p - 1, v, level, :] = last_f + gain

                low, high = rims((joined, e[1], e[2]))
                out += [
                    e[3], f[3],
                    z_low + pltpu.roll(low, shift, 1), z_high + pltpu.roll(high, shift, 1),
                ]
            return tuple(out)

        zero = jnp.zeros((tile, width), F32)
        final = (zero,) * 8
        for p in range(elements_x):
            final = element(p, final)
        for v in range(2):
            last_e, last_f, z_low, z_high = final[4 * v : 4 * v + 4]
            at = pl.ds(pl.multiple_of(v * levels + tile * step, tile), tile)
            adv_ref[width_x - 1, v, level, :] = last_f
            zlo_ref[at, :] = jnp.where(
                lane == width_x - 1, pltpu.roll(last_e, width_x - 1, 1), z_low
            )
            zhi_ref[at, :] = pltpu.roll(
                jnp.where(lane == width_x - 2, pltpu.roll(last_e, width_x - 1, 1), z_high), 1, 1
            )

    @pl.loop(0, steps)
    def _(step):
        for copy in copies(step):
            copy.wait()
        one_tile(step)

    jac = jac_ref[...]
    ylo_ref[...] = zlo_ref[...].T
    yhi_ref[...] = zhi_ref[...].T
    for ref, q in ((ylo_ref, 0), (yhi_ref, elements_y - 1)):
        ref[width_x : width_x + elements_x, :] = jnp.broadcast_to(
            jac[:, q : q + 1], (elements_x, features)
        )


def cells_kernel(capacity, devices, adv_ref, span_ref, col_ref, slot_ref):
    group = adv_ref.shape[0] // 4
    width = adv_ref.shape[3]
    features = adv_ref.shape[1] * adv_ref.shape[2]
    elements_x, elements_y = span_ref.shape
    elements = elements_x * elements_y

    @pl.when(pl.program_id(0) == 0)
    def _():
        lane = iota((elements_y, elements), 1)
        tiled = lax.rem(lane, elements_y) == iota((elements_y, elements), 0)
        spread = jnp.dot(
            span_ref[...].astype(F32).astype(BF16), tiled.astype(BF16), preferred_element_type=F32
        )
        start = iota((elements_x, elements), 0) * elements_y
        at = iota((elements_x, elements), 1)
        own = (at >= start) & (at < start + elements_y)
        target = jnp.sum(jnp.where(own, spread, 0.0), axis=0, keepdims=True)
        chosen = jnp.where(
            target == iota((devices, elements), 0).astype(F32), 1.0, 0.0
        )
        before = iota((elements, elements), 0) < iota((elements, elements), 1)
        earlier = jnp.dot(
            chosen.astype(BF16), before.astype(BF16), preferred_element_type=F32
        )
        rank = jnp.sum(chosen * earlier, axis=0, keepdims=True)
        slot_ref[...] = (target * capacity + rank).astype(jnp.int32)

    select = select_cells(elements_y, width)
    for p in range(group):
        for a in range(2):
            line = adv_ref[4 * p + 2 * a] * CELL_WEIGHTS[2 * a]
            line += adv_ref[4 * p + 2 * a + 1] * CELL_WEIGHTS[2 * a + 1]
            low, high = cells_of_line(line.reshape(features, width), select)
            at = slice(p * elements_y, (p + 1) * elements_y)
            col_ref[2 * a, at, :] = low
            col_ref[2 * a + 1, at, :] = high


def select_cells(elements_y, width):
    shape = (2 * elements_y, width)
    row, lane = iota(shape, 0), iota(shape, 1)
    wanted = jnp.where(row < elements_y, 4 * row, 4 * (row - elements_y) + 2)
    return (lane == wanted).astype(BF16)


def cells_of_line(line, select):
    features, width = line.shape
    inner = (iota((1, width), 1) & 3)
    line = line * jnp.where((inner == 0) | (inner == 3), 1.0 / 6.0, 5.0 / 6.0)
    line = line + pltpu.roll(line, width - 1, 1)
    high, low = split(line)
    both = lax.dot_general(
        select, jnp.concatenate([high, low], axis=0), (((1,), (1,)), ((), ())),
        preferred_element_type=F32,
    )
    cells = both[:, :features] + both[:, features:]
    half = select.shape[0] // 2
    return cells[:half], cells[half:]


def corners_kernel(width_x, elements_x, ylo_ref, yhi_ref, prev_ref, next_ref, ylo_out, yhi_out):
    tail = prev_ref.shape[0] - 16
    spare = width_x + elements_x
    for side, (ref, out) in enumerate(((ylo_ref, ylo_out), (yhi_ref, yhi_out))):
        row = iota(ref.shape, 0)
        values = ref[...]
        for k, (packet, x) in enumerate(((prev_ref, 0), (next_ref, width_x - 1))):
            rim = packet[tail + side : tail + side + 1, :]
            mass = packet[tail + 3 + side : tail + 4 + side, :]
            inner = packet[tail + 5 + side : tail + 6 + side, :]
            values = values + jnp.where(row == x, rim, 0.0)
            values = jnp.where(row == spare + k, mass, values)
            values = jnp.where(row == spare + 2 + k, inner, values)
        out[...] = values


def complete_kernel(
    width_x, elements_x,
    col_ref, xlo_ref, xhi_ref, prev_ref, next_ref, ylo_ref, yhi_ref, yprev_ref,
    ynext_ref, colbf_ref, fy_ref, ry_ref, fx_ref, rx_ref, ghost_ref, work_ref, cell_ref,
):
    _, elements, features = col_ref.shape
    tail = 2 * features
    ghost_fixes = []
    elements_y = elements // elements_x
    width = xlo_ref.shape[1]
    work_ref[...] = col_ref[...]
    select = select_cells(elements_y, width)
    lane = iota((1, width), 1)
    inner = (lane > 0) & (lane < width - 1)
    for side, (own, other) in enumerate(((ylo_ref, yprev_ref), (yhi_ref, ynext_ref))):
        total = own[...] + other[...]
        mass = total[width_x : width_x + elements_x]
        row = iota(mass.shape, 0)
        spare = width_x + elements_x
        before = jnp.where(row == 0, total[spare : spare + 1], pltpu.roll(mass, 1, 0))
        after = jnp.where(
            row == elements_x - 1, total[spare + 1 : spare + 2], pltpu.roll(mass, elements_x - 1, 0)
        )
        inside = 1.0 / mass
        ry_ref[side, pl.ds(0, elements_x, stride=4), :] = 1.0 / (mass + before)
        ry_ref[side, pl.ds(1, elements_x, stride=4), :] = inside
        ry_ref[side, pl.ds(2, elements_x, stride=4), :] = inside
        ry_ref[side, pl.ds(3, elements_x, stride=4), :] = 1.0 / (mass + after)
        fy_ref[side] = total[:width_x] * ry_ref[side]
        ghost_fixes.append(total[spare + 2 : spare + 4] / total[spare : spare + 2])
        fixes = [fy_ref[side, pl.ds(k, elements_x, stride=4), :] for k in range(4)]
        at = pl.ds(side * (elements_y - 1), elements_x, stride=elements_y)
        for a in range(2):
            added = CELL_WEIGHTS[2 * a] * fixes[2 * a] + CELL_WEIGHTS[2 * a + 1] * fixes[2 * a + 1]
            k = 2 * a + side
            work_ref[k, at, :] = work_ref[k, at, :] + CELL_WEIGHTS[0] * added
    for side, (own, other) in enumerate(((xlo_ref, prev_ref), (xhi_ref, next_ref))):
        mass = own[tail + 2 : tail + 3, :] + other[tail + 2 : tail + 3, :]
        reciprocal = jnp.where(inner, 1.0 / mass, 0.0)
        rx_ref[side] = jnp.broadcast_to(reciprocal, (8, width))
        fix = (own[:features] + other[:features]) * reciprocal
        fx_ref[side] = fix
        low, high = cells_of_line(CELL_WEIGHTS[0] * fix, select)
        at = slice(side * (elements_x - 1) * elements_y, (side * (elements_x - 1) + 1) * elements_y)
        work_ref[2 * side, at, :] = work_ref[2 * side, at, :] + low
        work_ref[2 * side + 1, at, :] = work_ref[2 * side + 1, at, :] + high
        line = other[features : 2 * features] + CELL_WEIGHTS[0] * fix
        cell_ref[2 * side], cell_ref[2 * side + 1] = cells_of_line(line, select)
        for end in range(2):
            x = side * (width_x - 1)
            added = CELL_WEIGHTS[0] * fy_ref[end, x : x + 1, :]
            added = added + CELL_WEIGHTS[1] * ghost_fixes[end][side : side + 1]
            q = end * (elements_y - 1)
            cell_ref[2 * side + end, q : q + 1, :] = (
                cell_ref[2 * side + end, q : q + 1, :] + CELL_WEIGHTS[0] * added
            )
    for k in range(4):
        ghost_ref[k * elements_y : (k + 1) * elements_y, :] = cell_ref[k].astype(BF16)
    for k in range(4):
        colbf_ref[:, k * features : (k + 1) * features] = work_ref[k].astype(BF16)


def send_kernel(colbf_ref, slot_ref, out_ref):
    elements = colbf_ref.shape[0]
    slots = out_ref.shape[0]
    piece = slots // 4
    for part in range(4):
        chosen = (iota((piece, elements), 0) + part * piece) == slot_ref[...]
        chosen = jnp.where(chosen, 1.0, 0.0)
        filled = jnp.max(chosen, axis=1, keepdims=True)
        moved = jnp.dot(chosen.astype(BF16), colbf_ref[...], preferred_element_type=F32)
        out_ref[pl.ds(part * piece, piece), :] = jnp.where(filled > 0.0, moved, EMPTY).astype(BF16)


def dense(inputs, weight_ref, bias_ref):
    return jnp.dot(inputs, weight_ref[...], preferred_element_type=F32) + bias_ref[...]


def leaky(values):
    return jnp.maximum(values, LEAK_SLOPE * values).astype(BF16)


def network_kernel(
    lit_ref, col_ref, ghost_ref, prev_ref, next_ref, w1, b1, w2, b2, w3, b3, w4, b4, s1, c1, s2,
    c2, s3, c3, inc_ref, ghost_inc_ref, total_ref,
):
    rows = col_ref.shape[0]
    features = col_ref.shape[1] // 4
    inputs = jnp.concatenate(
        [col_ref[:, k * features : (k + 1) * features] for k in range(4)], axis=0
    )
    total_ref[...] = primary(inputs, w1, b1, w2, b2, w3, b3, w4, b4)

    @pl.when(lit_ref[0, 0] != 0)
    def _():
        total_ref[...] += lit_ref[0, 0].astype(F32) * solar(inputs, s1, c1, s2, c2, s3, c3)

    for k in range(4):
        inc_ref[:, k * features : (k + 1) * features] = total_ref[
            k * rows : (k + 1) * rows, :
        ].astype(BF16)

    @pl.when(pl.program_id(0) == 0)
    def _():
        near = ghost_ref[...]
        tail = 2 * features + 7
        row = iota(near.shape, 0)
        lit = jnp.where(
            row < near.shape[0] // 2, prev_ref[tail : tail + 1, :], next_ref[tail : tail + 1, :]
        )
        near_inc = primary(near, w1, b1, w2, b2, w3, b3, w4, b4)
        near_inc = near_inc + lit * solar(near, s1, c1, s2, c2, s3, c3)
        ghost_inc_ref[...] = near_inc.astype(BF16)


def primary(inputs, w1, b1, w2, b2, w3, b3, w4, b4):
    hidden = leaky(dense(inputs, w1, b1))
    hidden = leaky(dense(hidden, w2, b2))
    hidden = leaky(dense(hidden, w3, b3))
    return dense(hidden, w4, b4)


def solar(inputs, s1, c1, s2, c2, s3, c3):
    hidden = leaky(dense(inputs, s1, c1))
    hidden = leaky(dense(hidden, s2, c2))
    return dense(hidden, s3, c3)


def spread_operand(mass_line, elements_y):
    width = mass_line.shape[1]
    shape = (2 * elements_y, width)
    row, lane = iota(shape, 0), iota(shape, 1)
    upper = row >= elements_y
    q = jnp.where(upper, row - elements_y, row)
    b = jnp.where(upper, 1, 0)
    own = (lane >> 1) == 2 * q + b
    copy = lane == jnp.where(upper, 4 * q + 4, 4 * q - 1)
    weights = jnp.where(
        own, mass_line, jnp.where(copy, copies_along_y(mass_line), 0.0)
    )
    high, low = split(weights)
    return jnp.concatenate([high, low], axis=0)


def spread_line(inc_ref, p, a, operand, elements_y):
    features = inc_ref.shape[1] // 4
    start = p * elements_y
    if not isinstance(p, int):
        start = pl.multiple_of(start, elements_y)
    at = pl.ds(start, elements_y)
    cells = [
        inc_ref[at, (2 * a + b) * features : (2 * a + b + 1) * features] for b in range(2)
    ]
    return spread_cells(cells, operand)


def spread_cells(cells, operand):
    return lax.dot_general(
        jnp.concatenate(cells + cells, axis=0), operand, (((0,), (0,)), ((), ())),
        preferred_element_type=F32,
    )


def rims_kernel(inc_ref, near_ref, jac_ref, prev_ref, next_ref, ylo_ref, yhi_ref, wide_ref):
    elements_x, elements_y = jac_ref.shape
    features = near_ref.shape[1]
    width_x = 4 * elements_x
    tail = 2 * features
    for k in range(4):
        wide_ref[k] = inc_ref[:, k * features : (k + 1) * features].astype(F32)
    near = near_ref[...].astype(F32)
    for side, ref in enumerate((ylo_ref, yhi_ref)):
        q = side * (elements_y - 1)
        column = jac_ref[:, q : q + 1]
        at = pl.ds(q, elements_x, stride=elements_y)
        first = column * wide_ref[side, at, :]
        second = column * wide_ref[2 + side, at, :]
        ghosts = []
        for k, packet in enumerate((prev_ref, next_ref)):
            cell = (2 * k + side) * elements_y + q
            mass = packet[tail + 3 + side : tail + 4 + side, :]
            ghosts.append(mass * near[cell : cell + 1])
        row = iota(first.shape, 0)
        ref[pl.ds(0, elements_x, stride=4), :] = first + jnp.where(
            row == 0, ghosts[0], pltpu.roll(second, 1, 0)
        )
        ref[pl.ds(1, elements_x, stride=4), :] = first
        ref[pl.ds(2, elements_x, stride=4), :] = second
        ref[pl.ds(3, elements_x, stride=4), :] = second + jnp.where(
            row == elements_x - 1, ghosts[1], pltpu.roll(first, elements_x - 1, 0)
        )
        ref[width_x:, :] = jnp.zeros((ref.shape[0] - width_x, features), F32)


def final_kernel(
    adv_ref, inc_ref, near_ref, jac_ref, prev_ref, next_ref, ylo_ref, yhi_ref, yprev_ref,
    ynext_ref, fy_ref, ry_ref, fx_ref, rx_ref, out_ref, mass_ref, inside_ref, shared_ref,
    rim_ref, edge_ref,
):
    step = pl.program_id(0)
    elements_x, elements_y = jac_ref.shape
    width_x = 4 * elements_x
    lines = adv_ref.shape[0]
    group = lines // 4
    width = adv_ref.shape[3]
    features = adv_ref.shape[1] * adv_ref.shape[2]

    @pl.when(step == 0)
    def _():
        mass = along_lanes(jac_ref[...], width)
        mass_ref[...] = mass
        inside, shared = inner_reciprocals(mass + copies_along_y(mass))
        inside_ref[...] = inside
        shared_ref[0:elements_x, :] = shared
        shared_ref[elements_x:, :] = jnp.zeros((8, width), F32)
        for side, (own, other) in enumerate(((ylo_ref, yprev_ref), (yhi_ref, ynext_ref))):
            rim_ref[side] = fy_ref[side] + (own[0:width_x, :] + other[0:width_x, :]) * ry_ref[side]
        for side, packet in enumerate((prev_ref, next_ref)):
            p = side * (elements_x - 1)
            own = spread_line(
                inc_ref, p, side, spread_operand(mass[p : p + 1], elements_y), elements_y
            )
            tail = 2 * features + 8
            at = 2 * side * elements_y
            other = spread_cells(
                [near_ref[at : at + 2 * elements_y, :]],
                spread_operand(packet[tail : tail + 1, :], elements_y),
            )
            edge_ref[side] = fx_ref[side] + (own + other) * rx_ref[side, 0:1, :]

    out = out_ref.reshape(features * lines, width)
    row = iota((16, width), 0)
    lane = iota((16, width), 1)
    place = (((row < 2) & (lane == 0)) | ((row >= 2) & (row < 4) & (lane == width - 1))).astype(BF16)

    def rim_of(x):
        low = rim_ref[0, pl.ds(x, 1), :]
        high = rim_ref[1, pl.ds(x, 1), :]
        parts = jnp.where(row < 2, low, high)
        rough = parts.astype(BF16).astype(F32)
        rest = parts - rough
        stacked = jnp.where((row == 0) | (row == 2), rough, jnp.where(row < 4, rest, 0.0))
        return lax.dot_general(
            stacked.astype(BF16), place, (((0,), (0,)), ((), ())), preferred_element_type=F32
        )

    def line_of(p, a):
        operand = spread_operand(mass_ref[pl.ds(p, 1), :], elements_y)
        return spread_line(inc_ref, p, a, operand, elements_y)

    def store(at, values):
        out[pl.ds(at, features, stride=lines), :] = adv_ref[at].reshape(features, width) + values

    first = step * group
    before = line_of(jnp.maximum(first - 1, 0), 1)
    here = line_of(first, 0)
    joint = (before + here) * shared_ref[pl.ds(first, 1), :] + rim_of(4 * first)
    for k in range(group):
        p = first + k
        inside = inside_ref[pl.ds(p, 1), :]
        store(4 * k, joint)
        store(4 * k + 1, here * inside + rim_of(4 * p + 1))
        there = line_of(p, 1)
        store(4 * k + 2, there * inside + rim_of(4 * p + 2))
        here = line_of(jnp.minimum(p + 1, elements_x - 1), 0)
        joint = (there + here) * shared_ref[pl.ds(p + 1, 1), :] + rim_of(4 * p + 3)
        store(4 * k + 3, joint)

    @pl.when(step == 0)
    def _():
        at = pl.ds(0, features, stride=lines)
        out[at, :] = out[at, :] + edge_ref[0]

    @pl.when(step == pl.num_programs(0) - 1)
    def _():
        at = pl.ds(lines - 1, features, stride=lines)
        out[at, :] = out[at, :] + edge_ref[1]


def arrange_kernel(capacity, data_ref, out_ref, wide_ref, rows_ref, vector_ref, start_ref, sem):
    devices = vector_ref.shape[0]
    slots = data_ref.shape[0]
    features = data_ref.shape[1] // 4
    elements = out_ref.shape[0] // 4
    filled = jnp.where(data_ref[:, 0:features].astype(F32) < 0.5 * EMPTY, 1.0, 0.0).astype(BF16)
    before = iota((devices, slots), 1) < iota((devices, slots), 0) * capacity
    starts = jnp.dot(
        jnp.where(before, 1.0, 0.0).astype(BF16), filled, preferred_element_type=F32
    )
    vector_ref[...] = jnp.clip(starts, 0.0, float(elements)).astype(jnp.int32)
    copy = pltpu.make_async_copy(vector_ref, start_ref, sem)
    copy.start()
    for k in range(4):
        wide_ref[k] = data_ref[:, k * features : (k + 1) * features].astype(F32)
    copy.wait()

    def one(s, carry):
        start = start_ref[s, 0]
        for k in range(4):
            rows_ref[pl.ds(4 * start + k, capacity, stride=4), :] = wide_ref[
                k, pl.ds(s * capacity, capacity), :
            ]
        return carry

    lax.fori_loop(0, devices, one, 0)
    out_ref[...] = rows_ref[0 : out_ref.shape[0], :].astype(BF16)


def params(mib):
    return pltpu.CompilerParams(vmem_limit_bytes=mib * MIB)


def whole(shape):
    return pl.BlockSpec(shape, lambda *_: (0,) * len(shape))


def cost(flops, bytes_accessed):
    return pl.CostEstimate(flops=flops, bytes_accessed=bytes_accessed, transcendentals=0)


def shape_of(shape, dtype=F32):
    return jax.ShapeDtypeStruct(shape, dtype)


def shifted(axis, by):
    count = lax.axis_size(axis)
    return [(i, (i + by) % count) for i in range(count)]


def edges_call(sunlit, prognostic, velocity, jacobian):
    fields, levels, width_x, width = prognostic.shape
    features = fields * levels
    last = width_x // 8 - 1, width_x // 16 - 1
    dcat = jnp.asarray(y_derivative_operand(width))
    return pl.pallas_call(
        edges_kernel,
        grid=(1,),
        in_specs=[
            pl.BlockSpec(memory_space=pltpu.SMEM),
            pl.BlockSpec((fields, levels, 8, width), lambda g: (0, 0, 0, 0)),
            pl.BlockSpec((fields, levels, 8, width), lambda g: (0, 0, last[0], 0)),
            pl.BlockSpec((2, levels, 16, width), lambda g: (0, 0, 0, 0)),
            pl.BlockSpec((2, levels, 16, width), lambda g: (0, 0, last[1], 0)),
            whole(jacobian.shape),
            whole((3 * width, width)),
        ],
        out_specs=[whole((2 * features + 16, width))] * 2,
        out_shape=[shape_of((2 * features + 16, width))] * 2,
        scratch_shapes=[pltpu.VMEM((2 * levels * 16, width), F32)],
        compiler_params=params(58),
        cost_estimate=cost(50_000_000, 2_000_000),
        name="edges",
    )(sunlit, prognostic, prognostic, velocity, velocity, jacobian, dcat)


def dynamics_call(prognostic, velocity, jacobian):
    fields, levels, width_x, width = prognostic.shape
    elements_x, elements_y = jacobian.shape
    features = fields * levels
    tile = 8
    dcat = jnp.asarray(y_derivative_operand(width))
    hbm = pl.BlockSpec(memory_space=pltpu.HBM)
    vmem = pl.BlockSpec(memory_space=pltpu.VMEM)
    return pl.pallas_call(
        dynamics_kernel,
        in_specs=[hbm, hbm, vmem, vmem],
        out_specs=[vmem] * 3,
        out_shape=[
            shape_of((width_x, fields, levels, width)),
            shape_of((width, features)),
            shape_of((width, features)),
        ],
        scratch_shapes=[
            pltpu.VMEM(prognostic.shape, F32),
            pltpu.VMEM(velocity.shape, BF16),
            pltpu.VMEM((2 * tile, width_x + 8, width), F32),
            pltpu.VMEM((2 * tile, width_x + 8, width), F32),
            pltpu.VMEM((2 * tile, width_x + 8, width), F32),
            pltpu.VMEM((elements_x, width), F32),
            pltpu.VMEM((elements_x, width), F32),
            pltpu.VMEM((elements_x, width), F32),
            pltpu.VMEM((features, width), F32),
            pltpu.VMEM((features, width), F32),
            pltpu.SemaphoreType.DMA((2, levels // tile)),
        ],
        compiler_params=params(42),
        cost_estimate=cost(2_000_000_000, 16_000_000),
        name="dynamics",
    )(prognostic, velocity, jacobian, dcat)


def on_device(
    prognostic,
    velocity,
    jacobian,
    element_span,
    sunlit,
    *weights,
):
    fields, levels, width_x, width = prognostic.shape
    elements_x, elements_y = jacobian.shape
    features = fields * levels
    elements = elements_x * elements_y
    devices = lax.axis_size("face") * lax.axis_size("dom")
    capacity = max(2, 2 * elements // devices)
    slots = devices * capacity
    packet = 2 * features + 16
    vmem = pl.BlockSpec(memory_space=pltpu.VMEM)
    smem = pl.BlockSpec(memory_space=pltpu.SMEM)

    xlo, xhi = edges_call(sunlit, prognostic, velocity, jacobian)
    adv, ylo, yhi = dynamics_call(prognostic, velocity, jacobian)

    group = 4
    col, slot_ids = pl.pallas_call(
        lambda *refs: cells_kernel(capacity, devices, *refs),
        grid=(elements_x // group,),
        in_specs=[
            pl.BlockSpec((4 * group, fields, levels, width), lambda g: (g, 0, 0, 0)),
            whole((elements_x, elements_y)),
        ],
        out_specs=[
            pl.BlockSpec((4, group * elements_y, features), lambda g: (0, g, 0)),
            whole((1, elements)),
        ],
        out_shape=[
            shape_of((4, elements, features)),
            shape_of((1, elements), jnp.int32),
        ],
        compiler_params=params(20),
        cost_estimate=cost(1_000_000_000, 8_000_000),
        name="cells",
    )(adv, element_span)

    prev = lax.ppermute(xhi, "face", shifted("face", 1))
    later = lax.ppermute(xlo, "face", shifted("face", -1))
    ylo, yhi = pl.pallas_call(
        lambda *refs: corners_kernel(width_x, elements_x, *refs),
        in_specs=[vmem] * 4,
        out_specs=[vmem] * 2,
        out_shape=[shape_of((width, features))] * 2,
        compiler_params=params(12),
        name="corners",
    )(ylo, yhi, prev, later)
    yprev = lax.ppermute(yhi, "dom", shifted("dom", 1))
    ynext = lax.ppermute(ylo, "dom", shifted("dom", -1))

    colbf, fy, ry, fx, rx, ghosts = pl.pallas_call(
        lambda *refs: complete_kernel(width_x, elements_x, *refs),
        in_specs=[vmem] * 9,
        out_specs=[vmem] * 6,
        out_shape=[
            shape_of((elements, 4 * features), BF16),
            shape_of((2, width_x, features)),
            shape_of((2, width_x, features)),
            shape_of((2, features, width)),
            shape_of((2, 8, width)),
            shape_of((4 * elements_y, features), BF16),
        ],
        scratch_shapes=[
            pltpu.VMEM((4, elements, features), F32),
            pltpu.VMEM((4, elements_y, features), F32),
        ],
        compiler_params=params(16),
        cost_estimate=cost(10_000_000, 3_000_000),
        name="complete",
    )(col, xlo, xhi, prev, later, ylo, yhi, yprev, ynext)

    chunk = elements // 3
    hidden = weights[0].shape[1]
    operands, operand_specs = [], []
    for item in weights:
        item = item if item.ndim == 2 else item.reshape(1, -1)
        operands.append(item)
        operand_specs.append(whole(item.shape))
    outgoing = pl.pallas_call(
        send_kernel,
        in_specs=[vmem] * 2,
        out_specs=vmem,
        out_shape=shape_of((slots, 4 * features), BF16),
        compiler_params=params(16),
        cost_estimate=cost(2_000_000_000, 3_000_000),
        name="send",
    )(colbf, slot_ids)

    arrived = lax.all_to_all(
        outgoing.reshape(devices, capacity, 4 * features), ("face", "dom"),
        split_axis=0, concat_axis=0, tiled=True,
    ).reshape(slots, 4 * features)

    inc, near = pl.pallas_call(
        network_kernel,
        grid=(3,),
        in_specs=[
            smem,
            pl.BlockSpec((chunk, 4 * features), lambda g: (g, 0)),
            whole((4 * elements_y, features)),
            whole((packet, width)),
            whole((packet, width)),
        ]
        + operand_specs,
        out_specs=[
            pl.BlockSpec((chunk, 4 * features), lambda g: (g, 0)),
            whole((4 * elements_y, features)),
        ],
        out_shape=[
            shape_of((elements, 4 * features), BF16),
            shape_of((4 * elements_y, features), BF16),
        ],
        scratch_shapes=[pltpu.VMEM((4 * chunk, features), F32)],
        compiler_params=params(24),
        cost_estimate=cost(8 * elements * (4 * features * hidden + 3 * hidden * hidden), 4_000_000),
        name="network",
    )(sunlit, colbf, ghosts, prev, later, *operands)

    ylo2, yhi2 = pl.pallas_call(
        rims_kernel,
        in_specs=[vmem] * 5,
        out_specs=[vmem] * 2,
        out_shape=[shape_of((width, features))] * 2,
        scratch_shapes=[pltpu.VMEM((4, elements, features), F32)],
        compiler_params=params(16),
        cost_estimate=cost(10_000_000, 2_000_000),
        name="rims",
    )(inc, near, jacobian, prev, later)
    yprev2 = lax.ppermute(yhi2, "dom", shifted("dom", 1))
    ynext2 = lax.ppermute(ylo2, "dom", shifted("dom", -1))

    new_state = pl.pallas_call(
        final_kernel,
        grid=(elements_x // group,),
        in_specs=[
            pl.BlockSpec((4 * group, fields, levels, width), lambda g: (g, 0, 0, 0)),
            whole((elements, 4 * features)),
            whole((4 * elements_y, features)),
            whole((elements_x, elements_y)),
            whole((packet, width)),
            whole((packet, width)),
            whole((width, features)),
            whole((width, features)),
            whole((width, features)),
            whole((width, features)),
            whole((2, width_x, features)),
            whole((2, width_x, features)),
            whole((2, features, width)),
            whole((2, 8, width)),
        ],
        out_specs=pl.BlockSpec((fields, levels, 4 * group, width), lambda g: (0, 0, g, 0)),
        out_shape=shape_of((fields, levels, width_x, width)),
        scratch_shapes=[
            pltpu.VMEM((elements_x, width), F32),
            pltpu.VMEM((elements_x, width), F32),
            pltpu.VMEM((elements_x + 8, width), F32),
            pltpu.VMEM((2, width_x, features), F32),
            pltpu.VMEM((2, features, width), F32),
        ],
        compiler_params=params(20),
        cost_estimate=cost(1_000_000_000, 14_000_000),
        name="final",
    )(
        adv, inc, near, jacobian, prev, later, ylo2, yhi2, yprev2, ynext2, fy, ry, fx, rx
    )

    span_state = pl.pallas_call(
        lambda *refs: arrange_kernel(capacity, *refs),
        in_specs=[vmem],
        out_specs=vmem,
        out_shape=shape_of((4 * elements, features), BF16),
        scratch_shapes=[
            pltpu.VMEM((4, slots, features), F32),
            pltpu.VMEM((4 * (elements + capacity), features), F32),
            pltpu.VMEM((devices, features), jnp.int32),
            pltpu.SMEM((devices, features), jnp.int32),
            pltpu.SemaphoreType.DMA,
        ],
        compiler_params=params(24),
        cost_estimate=cost(1_000_000, 3_000_000),
        name="arrange",
    )(arrived)
    return (new_state, span_state)


def solution(mesh):
    return jax.shard_map(
        on_device,
        mesh=mesh,
        in_specs=(
            P(None, None, "face", "dom"),
            P(None, None, "face", "dom"),
            P("face", "dom"),
            P("face", "dom"),
            P("face", "dom"),
        )
        + (P(),) * 14,
        out_specs=(P(None, None, "face", "dom"), P(("face", "dom"), None)),
        check_vma=False,
    )
```

```python
import jax
import jax.numpy as jnp
import numpy as np
from jax import lax
from jax.experimental import pallas as pl
from jax.experimental.pallas import tpu as pltpu
from jax.sharding import PartitionSpec as P

TIME_STEP = 0.1
LEAK_SLOPE = 0.15
F32 = jnp.float32
BF16 = jnp.bfloat16
HIGHEST = lax.Precision.HIGHEST
CELL_WEIGHTS = (1.0 / 6.0, 5.0 / 6.0, 5.0 / 6.0, 1.0 / 6.0)
MIB = 1024 * 1024
EMPTY = 1e30


def derivative_matrix():
    points = np.array([-1.0, -1.0 / np.sqrt(5.0), 1.0 / np.sqrt(5.0), 1.0])
    legendre = (5.0 * points**3 - 3.0 * points) / 2.0
    derivative = np.zeros((4, 4))
    for i in range(4):
        for k in range(4):
            if i != k:
                derivative[i, k] = legendre[i] / (legendre[k] * (points[i] - points[k]))
    derivative[0, 0] = -3.0
    derivative[3, 3] = 3.0
    return derivative


D = derivative_matrix()


def y_derivative_operand(width):
    full = np.kron(np.eye(width // 4), D.T).astype(np.float32)
    high = full.astype(jnp.bfloat16)
    low = (full - high.astype(np.float32)).astype(jnp.bfloat16)
    return np.concatenate([high, high, low], axis=0)


def iota(shape, dim):
    return lax.broadcasted_iota(jnp.int32, shape, dim)


def split(values):
    high = values.astype(BF16)
    return high, (values - high.astype(F32)).astype(BF16)


def copies_along_y(values):
    width = values.shape[-1]
    lane = iota((1, width), 1)
    up = ((lane & 3) == 3) & (lane < width - 1)
    down = ((lane & 3) == 0) & (lane > 0)
    return jnp.where(
        up, pltpu.roll(values, width - 1, 1), jnp.where(down, pltpu.roll(values, 1, 1), 0.0)
    )


def along_lanes(jac, width):
    expand = (iota((jac.shape[1], width), 1) >> 2) == iota((jac.shape[1], width), 0)
    return jnp.dot(jac, expand.astype(F32), precision=HIGHEST, preferred_element_type=F32)


def inner_reciprocals(mass):
    width = mass.shape[1]
    lane = iota(mass.shape, 1)
    row = iota(mass.shape, 0)
    inner = (lane > 0) & (lane < width - 1)
    inside = jnp.where(inner, 1.0 / mass, 0.0)
    shared = jnp.where(inner & (row > 0), 1.0 / (mass + pltpu.roll(mass, 1, 0)), 0.0)
    return inside, shared


def element_slopes(f):
    outer_gap, inner_gap = f[0] - f[3], f[1] - f[2]
    bend = (f[1] + f[2]) - (f[0] + f[3])
    odd = (D[0, 0] - D[0, 3]) / 2 * outer_gap + (D[0, 1] - D[0, 2]) / 2 * inner_gap
    even = (D[0, 1] + D[0, 2]) / 2 * bend
    odd_in = (D[1, 0] - D[1, 3]) / 2 * outer_gap - D[1, 2] / 2 * inner_gap
    even_in = D[1, 2] / 2 * bend
    return [odd + even, odd_in + even_in, odd_in - even_in, odd - even]


def edges_kernel(
    lit_ref, proglo_ref, proghi_ref, vello_ref, velhi_ref, jac_ref, dcat_ref, xlo_ref, xhi_ref,
    vf_ref,
):
    elements_x, elements_y = jac_ref.shape
    fields, levels, _, width = proglo_ref.shape
    features = fields * levels
    jac = jac_ref[...]
    mass = along_lanes(jac, width)
    joined = mass + copies_along_y(mass)
    inside, _ = inner_reciprocals(joined)
    lit = lit_ref[0, 0].astype(F32)
    sides = ((proglo_ref, vello_ref, xlo_ref), (proghi_ref, velhi_ref, xhi_ref))
    for side, (prog_ref, vel_ref, out_ref) in enumerate(sides):
        p = side * (elements_x - 1)
        lines = prog_ref.shape[2]
        prog = prog_ref.reshape(features * lines, width)
        first = side * (lines - 4)
        f = [prog[pl.ds(first + k, features, stride=lines), :] for k in range(4)]
        vlines = vel_ref.shape[2]
        vf_ref[...] = vel_ref[...].astype(F32).reshape(2 * levels * vlines, width)
        slopes = element_slopes(f)
        turned, moved = [], []
        for node in (3 * side, 1 + side):
            row = node + side * (vlines - 4)
            vx = vf_ref[pl.ds(row, levels, stride=vlines), :]
            vy = vf_ref[pl.ds(levels * vlines + row, levels, stride=vlines), :]
            high, low = split(f[node])
            sy = jnp.dot(
                jnp.concatenate([high, low, high], axis=1), dcat_ref[...],
                preferred_element_type=F32,
            )
            vx = jnp.concatenate([vx] * fields, axis=0)
            vy = jnp.concatenate([vy] * fields, axis=0)
            line = (vx * slopes[node] + vy * sy) * (-TIME_STEP * jnp.sqrt(mass[p : p + 1]))
            line = line + copies_along_y(line)
            moved.append(line)
            turned.append(line.T)
        out_ref[0:features, :] = moved[0]
        out_ref[features : 2 * features, :] = CELL_WEIGHTS[0] * f[3 * side] + CELL_WEIGHTS[1] * (
            f[1 + side] + moved[1] * inside[p : p + 1]
        )
        out_ref[2 * features : 2 * features + 16, :] = jnp.concatenate(
            [
                turned[0][0:1],
                turned[0][width - 1 : width],
                joined[p : p + 1],
                jnp.broadcast_to(jac[p : p + 1, 0:1], (1, width)),
                jnp.broadcast_to(jac[p : p + 1, elements_y - 1 : elements_y], (1, width)),
                turned[1][0:1],
                turned[1][width - 1 : width],
                jnp.broadcast_to(lit, (1, width)),
                mass[p : p + 1],
                jnp.zeros((7, width), F32),
            ],
            axis=0,
        )


def dynamics_kernel(
    prog_hbm, vel_hbm, jac_ref, dcat_ref, adv_ref, ylo_ref, yhi_ref, prog_ref, vel_ref,
    sy3_ref, vf3_ref, pf3_ref, scale_ref, inside_ref, shared_ref, zlo_ref, zhi_ref, sems,
):
    _, levels, width_x, width = prog_ref.shape
    tile = sy3_ref.shape[0] // 2
    steps = levels // tile
    elements_x, elements_y = jac_ref.shape
    features = zlo_ref.shape[0]
    planes = 2 * tile
    pitch = sy3_ref.shape[1]
    sy_ref = sy3_ref.reshape(planes * pitch, width)
    vf_ref = vf3_ref.reshape(planes * pitch, width)
    pf_ref = pf3_ref.reshape(planes * pitch, width)

    def copies(step):
        at = pl.ds(step * tile, tile)
        return (
            pltpu.make_async_copy(prog_hbm.at[:, at], prog_ref.at[:, at], sems.at[0, step]),
            pltpu.make_async_copy(vel_hbm.at[:, at], vel_ref.at[:, at], sems.at[1, step]),
        )

    for step in range(steps):
        for copy in copies(step):
            copy.start()

    mass = along_lanes(jac_ref[...], width)
    scale_ref[...] = -TIME_STEP * jnp.sqrt(mass)
    inside, shared = inner_reciprocals(mass + copies_along_y(mass))
    inside_ref[...] = inside
    shared_ref[...] = shared

    def one_tile(step):
        level = pl.ds(pl.multiple_of(step * tile, tile), tile)
        vf3_ref[:, 0:width_x, :] = vel_ref[:, pl.ds(step * tile, tile)].astype(F32).reshape(
            planes, width_x, width
        )
        piece = planes // 4
        for at in range(4):
            first = at * piece
            values = prog_ref[first // tile, pl.ds(step * tile + first % tile, piece)]
            pf3_ref[first : first + piece, 0:width_x, :] = values
            high, low = split(values.reshape(piece * width_x, width))
            sy3_ref[first : first + piece, 0:width_x, :] = jnp.dot(
                jnp.concatenate([high, low, high], axis=1), dcat_ref[...], preferred_element_type=F32
            ).reshape(piece, width_x, width)

        lane = iota((tile, width), 1)

        def rims(lines):
            first, second, third = lines
            a = pltpu.roll(first, 1, 1)
            b = pltpu.roll(second, 2, 1)
            c = pltpu.roll(third, 3, 1)

            def pick(base):
                return jnp.where(
                    lane == base, first,
                    jnp.where(
                        lane == (base + 1) % width, a,
                        jnp.where(
                            lane == (base + 2) % width, b, jnp.where(lane == (base + 3) % width, c, 0.0)
                        ),
                    ),
                )

            return pick(0), pick(width - 1)

        def element(p, carry):
            scale = scale_ref[p : p + 1, :]
            inside = inside_ref[p : p + 1, :]
            shared = shared_ref[p : p + 1, :]
            shift = (4 * p + width - 1) % width
            vx = [vf_ref[pl.ds(4 * p + k, tile, stride=pitch), :] for k in range(4)]
            vy = [
                vf_ref[pl.ds(tile * pitch + 4 * p + k, tile, stride=pitch), :] for k in range(4)
            ]
            out = []
            for v in range(2):
                last_e, last_f, z_low, z_high = carry[4 * v : 4 * v + 4]
                base = v * tile * pitch + 4 * p
                f = [pf_ref[pl.ds(base + k, tile, stride=pitch), :] for k in range(4)]
                sy = [sy_ref[pl.ds(base + k, tile, stride=pitch), :] for k in range(4)]
                sx = element_slopes(f)
                e = []
                for k in range(4):
                    moved = (vx[k] * sx[k] + vy[k] * sy[k]) * scale
                    e.append(moved + copies_along_y(moved))
                joined = last_e + e[0]
                gain = joined * shared
                adv_ref[4 * p, v, level, :] = f[0] + gain
                adv_ref[4 * p + 1, v, level, :] = f[1] + e[1] * inside
                adv_ref[4 * p + 2, v, level, :] = f[2] + e[2] * inside

                if p > 0:
                    adv_ref[4 * p - 1, v, level, :] = last_f + gain

                low, high = rims((joined, e[1], e[2]))
                out += [
                    e[3], f[3],
                    z_low + pltpu.roll(low, shift, 1), z_high + pltpu.roll(high, shift, 1),
                ]
            return tuple(out)

        zero = jnp.zeros((tile, width), F32)
        final = (zero,) * 8
        for p in range(elements_x):
            final = element(p, final)
        for v in range(2):
            last_e, last_f, z_low, z_high = final[4 * v : 4 * v + 4]
            at = pl.ds(pl.multiple_of(v * levels + tile * step, tile), tile)
            adv_ref[width_x - 1, v, level, :] = last_f
            zlo_ref[at, :] = jnp.where(
                lane == width_x - 1, pltpu.roll(last_e, width_x - 1, 1), z_low
            )
            zhi_ref[at, :] = pltpu.roll(
                jnp.where(lane == width_x - 2, pltpu.roll(last_e, width_x - 1, 1), z_high), 1, 1
            )

    @pl.loop(0, steps)
    def _(step):
        for copy in copies(step):
            copy.wait()
        one_tile(step)

    jac = jac_ref[...]
    ylo_ref[...] = zlo_ref[...].T
    yhi_ref[...] = zhi_ref[...].T
    for ref, q in ((ylo_ref, 0), (yhi_ref, elements_y - 1)):
        ref[width_x : width_x + elements_x, :] = jnp.broadcast_to(
            jac[:, q : q + 1], (elements_x, features)
        )


def cells_kernel(capacity, devices, adv_ref, span_ref, col_ref, slot_ref):
    group = adv_ref.shape[0] // 4
    width = adv_ref.shape[3]
    features = adv_ref.shape[1] * adv_ref.shape[2]
    elements_x, elements_y = span_ref.shape
    elements = elements_x * elements_y

    @pl.when(pl.program_id(0) == 0)
    def _():
        lane = iota((elements_y, elements), 1)
        tiled = lax.rem(lane, elements_y) == iota((elements_y, elements), 0)
        spread = jnp.dot(
            span_ref[...].astype(F32).astype(BF16), tiled.astype(BF16), preferred_element_type=F32
        )
        start = iota((elements_x, elements), 0) * elements_y
        at = iota((elements_x, elements), 1)
        own = (at >= start) & (at < start + elements_y)
        target = jnp.sum(jnp.where(own, spread, 0.0), axis=0, keepdims=True)
        chosen = jnp.where(
            target == iota((devices, elements), 0).astype(F32), 1.0, 0.0
        )
        before = iota((elements, elements), 0) < iota((elements, elements), 1)
        earlier = jnp.dot(
            chosen.astype(BF16), before.astype(BF16), preferred_element_type=F32
        )
        rank = jnp.sum(chosen * earlier, axis=0, keepdims=True)
        slot_ref[...] = (target * capacity + rank).astype(jnp.int32)

    select = select_cells(elements_y, width)
    for p in range(group):
        for a in range(2):
            line = adv_ref[4 * p + 2 * a] * CELL_WEIGHTS[2 * a]
            line += adv_ref[4 * p + 2 * a + 1] * CELL_WEIGHTS[2 * a + 1]
            low, high = cells_of_line(line.reshape(features, width), select)
            at = slice(p * elements_y, (p + 1) * elements_y)
            col_ref[2 * a, at, :] = low
            col_ref[2 * a + 1, at, :] = high


def select_cells(elements_y, width):
    shape = (2 * elements_y, width)
    row, lane = iota(shape, 0), iota(shape, 1)
    wanted = jnp.where(row < elements_y, 4 * row, 4 * (row - elements_y) + 2)
    return (lane == wanted).astype(BF16)


def cells_of_line(line, select):
    features, width = line.shape
    inner = (iota((1, width), 1) & 3)
    line = line * jnp.where((inner == 0) | (inner == 3), 1.0 / 6.0, 5.0 / 6.0)
    line = line + pltpu.roll(line, width - 1, 1)
    high, low = split(line)
    both = lax.dot_general(
        select, jnp.concatenate([high, low], axis=0), (((1,), (1,)), ((), ())),
        preferred_element_type=F32,
    )
    cells = both[:, :features] + both[:, features:]
    half = select.shape[0] // 2
    return cells[:half], cells[half:]


def corners_kernel(width_x, elements_x, ylo_ref, yhi_ref, prev_ref, next_ref, ylo_out, yhi_out):
    tail = prev_ref.shape[0] - 16
    spare = width_x + elements_x
    for side, (ref, out) in enumerate(((ylo_ref, ylo_out), (yhi_ref, yhi_out))):
        row = iota(ref.shape, 0)
        values = ref[...]
        for k, (packet, x) in enumerate(((prev_ref, 0), (next_ref, width_x - 1))):
            rim = packet[tail + side : tail + side + 1, :]
            mass = packet[tail + 3 + side : tail + 4 + side, :]
            inner = packet[tail + 5 + side : tail + 6 + side, :]
            values = values + jnp.where(row == x, rim, 0.0)
            values = jnp.where(row == spare + k, mass, values)
            values = jnp.where(row == spare + 2 + k, inner, values)
        out[...] = values


def complete_kernel(
    width_x, elements_x,
    col_ref, xlo_ref, xhi_ref, prev_ref, next_ref, ylo_ref, yhi_ref, yprev_ref,
    ynext_ref, colbf_ref, fy_ref, ry_ref, fx_ref, rx_ref, ghost_ref, work_ref, cell_ref,
):
    _, elements, features = col_ref.shape
    tail = 2 * features
    ghost_fixes = []
    elements_y = elements // elements_x
    width = xlo_ref.shape[1]
    work_ref[...] = col_ref[...]
    select = select_cells(elements_y, width)
    lane = iota((1, width), 1)
    inner = (lane > 0) & (lane < width - 1)
    for side, (own, other) in enumerate(((ylo_ref, yprev_ref), (yhi_ref, ynext_ref))):
        total = own[...] + other[...]
        mass = total[width_x : width_x + elements_x]
        row = iota(mass.shape, 0)
        spare = width_x + elements_x
        before = jnp.where(row == 0, total[spare : spare + 1], pltpu.roll(mass, 1, 0))
        after = jnp.where(
            row == elements_x - 1, total[spare + 1 : spare + 2], pltpu.roll(mass, elements_x - 1, 0)
        )
        inside = 1.0 / mass
        ry_ref[side, pl.ds(0, elements_x, stride=4), :] = 1.0 / (mass + before)
        ry_ref[side, pl.ds(1, elements_x, stride=4), :] = inside
        ry_ref[side, pl.ds(2, elements_x, stride=4), :] = inside
        ry_ref[side, pl.ds(3, elements_x, stride=4), :] = 1.0 / (mass + after)
        fy_ref[side] = total[:width_x] * ry_ref[side]
        ghost_fixes.append(total[spare + 2 : spare + 4] / total[spare : spare + 2])
        fixes = [fy_ref[side, pl.ds(k, elements_x, stride=4), :] for k in range(4)]
        at = pl.ds(side * (elements_y - 1), elements_x, stride=elements_y)
        for a in range(2):
            added = CELL_WEIGHTS[2 * a] * fixes[2 * a] + CELL_WEIGHTS[2 * a + 1] * fixes[2 * a + 1]
            k = 2 * a + side
            work_ref[k, at, :] = work_ref[k, at, :] + CELL_WEIGHTS[0] * added
    for side, (own, other) in enumerate(((xlo_ref, prev_ref), (xhi_ref, next_ref))):
        mass = own[tail + 2 : tail + 3, :] + other[tail + 2 : tail + 3, :]
        reciprocal = jnp.where(inner, 1.0 / mass, 0.0)
        rx_ref[side] = jnp.broadcast_to(reciprocal, (8, width))
        fix = (own[:features] + other[:features]) * reciprocal
        fx_ref[side] = fix
        low, high = cells_of_line(CELL_WEIGHTS[0] * fix, select)
        at = slice(side * (elements_x - 1) * elements_y, (side * (elements_x - 1) + 1) * elements_y)
        work_ref[2 * side, at, :] = work_ref[2 * side, at, :] + low
        work_ref[2 * side + 1, at, :] = work_ref[2 * side + 1, at, :] + high
        line = other[features : 2 * features] + CELL_WEIGHTS[0] * fix
        cell_ref[2 * side], cell_ref[2 * side + 1] = cells_of_line(line, select)
        for end in range(2):
            x = side * (width_x - 1)
            added = CELL_WEIGHTS[0] * fy_ref[end, x : x + 1, :]
            added = added + CELL_WEIGHTS[1] * ghost_fixes[end][side : side + 1]
            q = end * (elements_y - 1)
            cell_ref[2 * side + end, q : q + 1, :] = (
                cell_ref[2 * side + end, q : q + 1, :] + CELL_WEIGHTS[0] * added
            )
    for k in range(4):
        ghost_ref[k * elements_y : (k + 1) * elements_y, :] = cell_ref[k].astype(BF16)
    for k in range(4):
        colbf_ref[:, k * features : (k + 1) * features] = work_ref[k].astype(BF16)


def send_kernel(colbf_ref, slot_ref, out_hbm, out_ref, sems):
    elements = colbf_ref.shape[0]
    slots = out_ref.shape[0]
    pieces = sems.shape[0]
    piece = slots // pieces
    copies = []
    for part in range(pieces):
        at = pl.ds(part * piece, piece)
        chosen = (iota((piece, elements), 0) + part * piece) == slot_ref[...]
        chosen = jnp.where(chosen, 1.0, 0.0)
        filled = jnp.max(chosen, axis=1, keepdims=True)
        moved = jnp.dot(chosen.astype(BF16), colbf_ref[...], preferred_element_type=F32)
        out_ref[at, :] = jnp.where(filled > 0.0, moved, EMPTY).astype(BF16)
        copies.append(pltpu.make_async_copy(out_ref.at[at], out_hbm.at[at], sems.at[part]))
        copies[-1].start()
    for copy in copies:
        copy.wait()


def dense(inputs, weight_ref, bias_ref):
    return jnp.dot(inputs, weight_ref[...], preferred_element_type=F32) + bias_ref[...]


def leaky(values):
    return jnp.maximum(values, LEAK_SLOPE * values).astype(BF16)


def network_kernel(
    lit_ref, col_ref, ghost_ref, prev_ref, next_ref, w1, b1, w2, b2, w3, b3, w4, b4, s1, c1, s2,
    c2, s3, c3, inc_ref, ghost_inc_ref, total_ref,
):
    rows = col_ref.shape[0]
    features = col_ref.shape[1] // 4
    inputs = jnp.concatenate(
        [col_ref[:, k * features : (k + 1) * features] for k in range(4)], axis=0
    )
    total_ref[...] = primary(inputs, w1, b1, w2, b2, w3, b3, w4, b4)

    @pl.when(lit_ref[0, 0] != 0)
    def _():
        total_ref[...] += lit_ref[0, 0].astype(F32) * solar(inputs, s1, c1, s2, c2, s3, c3)

    for k in range(4):
        inc_ref[:, k * features : (k + 1) * features] = total_ref[
            k * rows : (k + 1) * rows, :
        ].astype(BF16)

    @pl.when(pl.program_id(0) == 0)
    def _():
        near = ghost_ref[...]
        tail = 2 * features + 7
        row = iota(near.shape, 0)
        lit = jnp.where(
            row < near.shape[0] // 2, prev_ref[tail : tail + 1, :], next_ref[tail : tail + 1, :]
        )
        near_inc = primary(near, w1, b1, w2, b2, w3, b3, w4, b4)
        near_inc = near_inc + lit * solar(near, s1, c1, s2, c2, s3, c3)
        ghost_inc_ref[...] = near_inc.astype(BF16)


def primary(inputs, w1, b1, w2, b2, w3, b3, w4, b4):
    hidden = leaky(dense(inputs, w1, b1))
    hidden = leaky(dense(hidden, w2, b2))
    hidden = leaky(dense(hidden, w3, b3))
    return dense(hidden, w4, b4)


def solar(inputs, s1, c1, s2, c2, s3, c3):
    hidden = leaky(dense(inputs, s1, c1))
    hidden = leaky(dense(hidden, s2, c2))
    return dense(hidden, s3, c3)


def spread_operand(mass_line, elements_y):
    width = mass_line.shape[1]
    shape = (2 * elements_y, width)
    row, lane = iota(shape, 0), iota(shape, 1)
    upper = row >= elements_y
    q = jnp.where(upper, row - elements_y, row)
    b = jnp.where(upper, 1, 0)
    own = (lane >> 1) == 2 * q + b
    copy = lane == jnp.where(upper, 4 * q + 4, 4 * q - 1)
    weights = jnp.where(
        own, mass_line, jnp.where(copy, copies_along_y(mass_line), 0.0)
    )
    high, low = split(weights)
    return jnp.concatenate([high, low], axis=0)


def spread_line(inc_ref, p, a, operand, elements_y):
    features = inc_ref.shape[1] // 4
    start = p * elements_y
    if not isinstance(p, int):
        start = pl.multiple_of(start, elements_y)
    at = pl.ds(start, elements_y)
    cells = [
        inc_ref[at, (2 * a + b) * features : (2 * a + b + 1) * features] for b in range(2)
    ]
    return spread_cells(cells, operand)


def spread_cells(cells, operand):
    return lax.dot_general(
        jnp.concatenate(cells + cells, axis=0), operand, (((0,), (0,)), ((), ())),
        preferred_element_type=F32,
    )


def rims_kernel(inc_ref, near_ref, jac_ref, prev_ref, next_ref, ylo_ref, yhi_ref, wide_ref):
    elements_x, elements_y = jac_ref.shape
    features = near_ref.shape[1]
    width_x = 4 * elements_x
    tail = 2 * features
    for k in range(4):
        wide_ref[k] = inc_ref[:, k * features : (k + 1) * features].astype(F32)
    near = near_ref[...].astype(F32)
    for side, ref in enumerate((ylo_ref, yhi_ref)):
        q = side * (elements_y - 1)
        column = jac_ref[:, q : q + 1]
        at = pl.ds(q, elements_x, stride=elements_y)
        first = column * wide_ref[side, at, :]
        second = column * wide_ref[2 + side, at, :]
        ghosts = []
        for k, packet in enumerate((prev_ref, next_ref)):
            cell = (2 * k + side) * elements_y + q
            mass = packet[tail + 3 + side : tail + 4 + side, :]
            ghosts.append(mass * near[cell : cell + 1])
        row = iota(first.shape, 0)
        ref[pl.ds(0, elements_x, stride=4), :] = first + jnp.where(
            row == 0, ghosts[0], pltpu.roll(second, 1, 0)
        )
        ref[pl.ds(1, elements_x, stride=4), :] = first
        ref[pl.ds(2, elements_x, stride=4), :] = second
        ref[pl.ds(3, elements_x, stride=4), :] = second + jnp.where(
            row == elements_x - 1, ghosts[1], pltpu.roll(first, elements_x - 1, 0)
        )
        ref[width_x:, :] = jnp.zeros((ref.shape[0] - width_x, features), F32)


def final_kernel(
    adv_ref, inc_ref, near_ref, jac_ref, prev_ref, next_ref, ylo_ref, yhi_ref, yprev_ref,
    ynext_ref, fy_ref, ry_ref, fx_ref, rx_ref, out_ref, mass_ref, inside_ref, shared_ref,
    rim_ref, edge_ref,
):
    step = pl.program_id(0)
    elements_x, elements_y = jac_ref.shape
    width_x = 4 * elements_x
    lines = adv_ref.shape[0]
    group = lines // 4
    width = adv_ref.shape[3]
    features = adv_ref.shape[1] * adv_ref.shape[2]

    @pl.when(step == 0)
    def _():
        mass = along_lanes(jac_ref[...], width)
        mass_ref[...] = mass
        inside, shared = inner_reciprocals(mass + copies_along_y(mass))
        inside_ref[...] = inside
        shared_ref[0:elements_x, :] = shared
        shared_ref[elements_x:, :] = jnp.zeros((8, width), F32)
        for side, (own, other) in enumerate(((ylo_ref, yprev_ref), (yhi_ref, ynext_ref))):
            rim_ref[side] = fy_ref[side] + (own[0:width_x, :] + other[0:width_x, :]) * ry_ref[side]
        for side, packet in enumerate((prev_ref, next_ref)):
            p = side * (elements_x - 1)
            own = spread_line(
                inc_ref, p, side, spread_operand(mass[p : p + 1], elements_y), elements_y
            )
            tail = 2 * features + 8
            at = 2 * side * elements_y
            other = spread_cells(
                [near_ref[at : at + 2 * elements_y, :]],
                spread_operand(packet[tail : tail + 1, :], elements_y),
            )
            edge_ref[side] = fx_ref[side] + (own + other) * rx_ref[side, 0:1, :]

    out = out_ref.reshape(features * lines, width)
    row = iota((16, width), 0)
    lane = iota((16, width), 1)
    place = (((row < 2) & (lane == 0)) | ((row >= 2) & (row < 4) & (lane == width - 1))).astype(BF16)

    def rim_of(x):
        low = rim_ref[0, pl.ds(x, 1), :]
        high = rim_ref[1, pl.ds(x, 1), :]
        parts = jnp.where(row < 2, low, high)
        rough = parts.astype(BF16).astype(F32)
        rest = parts - rough
        stacked = jnp.where((row == 0) | (row == 2), rough, jnp.where(row < 4, rest, 0.0))
        return lax.dot_general(
            stacked.astype(BF16), place, (((0,), (0,)), ((), ())), preferred_element_type=F32
        )

    def line_of(p, a):
        operand = spread_operand(mass_ref[pl.ds(p, 1), :], elements_y)
        return spread_line(inc_ref, p, a, operand, elements_y)

    def store(at, values):
        out[pl.ds(at, features, stride=lines), :] = adv_ref[at].reshape(features, width) + values

    first = step * group
    before = line_of(jnp.maximum(first - 1, 0), 1)
    here = line_of(first, 0)
    joint = (before + here) * shared_ref[pl.ds(first, 1), :] + rim_of(4 * first)
    for k in range(group):
        p = first + k
        inside = inside_ref[pl.ds(p, 1), :]
        store(4 * k, joint)
        store(4 * k + 1, here * inside + rim_of(4 * p + 1))
        there = line_of(p, 1)
        store(4 * k + 2, there * inside + rim_of(4 * p + 2))
        here = line_of(jnp.minimum(p + 1, elements_x - 1), 0)
        joint = (there + here) * shared_ref[pl.ds(p + 1, 1), :] + rim_of(4 * p + 3)
        store(4 * k + 3, joint)

    @pl.when(step == 0)
    def _():
        at = pl.ds(0, features, stride=lines)
        out[at, :] = out[at, :] + edge_ref[0]

    @pl.when(step == pl.num_programs(0) - 1)
    def _():
        at = pl.ds(lines - 1, features, stride=lines)
        out[at, :] = out[at, :] + edge_ref[1]


def arrange_kernel(
    capacity, data_ref, out_hbm, wide_ref, rows_ref, out_ref, vector_ref, start_ref, sem, sems
):
    devices = vector_ref.shape[0]
    slots = data_ref.shape[0]
    features = data_ref.shape[1] // 4
    elements = out_ref.shape[0] // 4
    filled = jnp.where(data_ref[:, 0:features].astype(F32) < 0.5 * EMPTY, 1.0, 0.0).astype(BF16)
    before = iota((devices, slots), 1) < iota((devices, slots), 0) * capacity
    starts = jnp.dot(
        jnp.where(before, 1.0, 0.0).astype(BF16), filled, preferred_element_type=F32
    )
    vector_ref[...] = jnp.clip(starts, 0.0, float(elements)).astype(jnp.int32)
    copy = pltpu.make_async_copy(vector_ref, start_ref, sem)
    copy.start()
    for k in range(4):
        wide_ref[k] = data_ref[:, k * features : (k + 1) * features].astype(F32)
    copy.wait()

    def one(s, carry):
        start = start_ref[s, 0]
        for k in range(4):
            rows_ref[pl.ds(4 * start + k, capacity, stride=4), :] = wide_ref[
                k, pl.ds(s * capacity, capacity), :
            ]
        return carry

    lax.fori_loop(0, devices, one, 0, unroll=4)
    pieces = sems.shape[0]
    piece = 4 * elements // pieces
    copies = []
    for part in range(pieces):
        at = pl.ds(part * piece, piece)
        out_ref[at, :] = rows_ref[at, :].astype(BF16)
        copies.append(pltpu.make_async_copy(out_ref.at[at], out_hbm.at[at], sems.at[part]))
        copies[-1].start()
    for copy in copies:
        copy.wait()


def params(mib):
    return pltpu.CompilerParams(vmem_limit_bytes=mib * MIB)


def whole(shape):
    return pl.BlockSpec(shape, lambda *_: (0,) * len(shape))


def cost(flops, bytes_accessed):
    return pl.CostEstimate(flops=flops, bytes_accessed=bytes_accessed, transcendentals=0)


def shape_of(shape, dtype=F32):
    return jax.ShapeDtypeStruct(shape, dtype)


def shifted(axis, by):
    count = lax.axis_size(axis)
    return [(i, (i + by) % count) for i in range(count)]


def edges_call(sunlit, prognostic, velocity, jacobian):
    fields, levels, width_x, width = prognostic.shape
    features = fields * levels
    last = width_x // 8 - 1, width_x // 16 - 1
    dcat = jnp.asarray(y_derivative_operand(width))
    return pl.pallas_call(
        edges_kernel,
        grid=(1,),
        in_specs=[
            pl.BlockSpec(memory_space=pltpu.SMEM),
            pl.BlockSpec((fields, levels, 8, width), lambda g: (0, 0, 0, 0)),
            pl.BlockSpec((fields, levels, 8, width), lambda g: (0, 0, last[0], 0)),
            pl.BlockSpec((2, levels, 16, width), lambda g: (0, 0, 0, 0)),
            pl.BlockSpec((2, levels, 16, width), lambda g: (0, 0, last[1], 0)),
            whole(jacobian.shape),
            whole((3 * width, width)),
        ],
        out_specs=[whole((2 * features + 16, width))] * 2,
        out_shape=[shape_of((2 * features + 16, width))] * 2,
        scratch_shapes=[pltpu.VMEM((2 * levels * 16, width), F32)],
        compiler_params=params(58),
        cost_estimate=cost(50_000_000, 2_000_000),
        name="edges",
    )(sunlit, prognostic, prognostic, velocity, velocity, jacobian, dcat)


def dynamics_call(prognostic, velocity, jacobian):
    fields, levels, width_x, width = prognostic.shape
    elements_x, elements_y = jacobian.shape
    features = fields * levels
    tile = 8
    dcat = jnp.asarray(y_derivative_operand(width))
    hbm = pl.BlockSpec(memory_space=pltpu.HBM)
    vmem = pl.BlockSpec(memory_space=pltpu.VMEM)
    return pl.pallas_call(
        dynamics_kernel,
        in_specs=[hbm, hbm, vmem, vmem],
        out_specs=[vmem] * 3,
        out_shape=[
            shape_of((width_x, fields, levels, width)),
            shape_of((width, features)),
            shape_of((width, features)),
        ],
        scratch_shapes=[
            pltpu.VMEM(prognostic.shape, F32),
            pltpu.VMEM(velocity.shape, BF16),
            pltpu.VMEM((2 * tile, width_x + 8, width), F32),
            pltpu.VMEM((2 * tile, width_x + 8, width), F32),
            pltpu.VMEM((2 * tile, width_x + 8, width), F32),
            pltpu.VMEM((elements_x, width), F32),
            pltpu.VMEM((elements_x, width), F32),
            pltpu.VMEM((elements_x, width), F32),
            pltpu.VMEM((features, width), F32),
            pltpu.VMEM((features, width), F32),
            pltpu.SemaphoreType.DMA((2, levels // tile)),
        ],
        compiler_params=params(42),
        cost_estimate=cost(2_000_000_000, 16_000_000),
        name="dynamics",
    )(prognostic, velocity, jacobian, dcat)


def on_device(
    prognostic,
    velocity,
    jacobian,
    element_span,
    sunlit,
    *weights,
):
    fields, levels, width_x, width = prognostic.shape
    elements_x, elements_y = jacobian.shape
    features = fields * levels
    elements = elements_x * elements_y
    devices = lax.axis_size("face") * lax.axis_size("dom")
    capacity = max(2, 2 * elements // devices)
    slots = devices * capacity
    packet = 2 * features + 16
    vmem = pl.BlockSpec(memory_space=pltpu.VMEM)
    hbm = pl.BlockSpec(memory_space=pltpu.HBM)
    smem = pl.BlockSpec(memory_space=pltpu.SMEM)

    xlo, xhi = edges_call(sunlit, prognostic, velocity, jacobian)
    adv, ylo, yhi = dynamics_call(prognostic, velocity, jacobian)

    group = 4
    col, slot_ids = pl.pallas_call(
        lambda *refs: cells_kernel(capacity, devices, *refs),
        grid=(elements_x // group,),
        in_specs=[
            pl.BlockSpec((4 * group, fields, levels, width), lambda g: (g, 0, 0, 0)),
            whole((elements_x, elements_y)),
        ],
        out_specs=[
            pl.BlockSpec((4, group * elements_y, features), lambda g: (0, g, 0)),
            whole((1, elements)),
        ],
        out_shape=[
            shape_of((4, elements, features)),
            shape_of((1, elements), jnp.int32),
        ],
        compiler_params=params(20),
        cost_estimate=cost(1_000_000_000, 8_000_000),
        name="cells",
    )(adv, element_span)

    prev = lax.ppermute(xhi, "face", shifted("face", 1))
    later = lax.ppermute(xlo, "face", shifted("face", -1))
    ylo, yhi = pl.pallas_call(
        lambda *refs: corners_kernel(width_x, elements_x, *refs),
        in_specs=[vmem] * 4,
        out_specs=[vmem] * 2,
        out_shape=[shape_of((width, features))] * 2,
        compiler_params=params(12),
        name="corners",
    )(ylo, yhi, prev, later)
    yprev = lax.ppermute(yhi, "dom", shifted("dom", 1))
    ynext = lax.ppermute(ylo, "dom", shifted("dom", -1))

    colbf, fy, ry, fx, rx, ghosts = pl.pallas_call(
        lambda *refs: complete_kernel(width_x, elements_x, *refs),
        in_specs=[vmem] * 9,
        out_specs=[vmem] * 6,
        out_shape=[
            shape_of((elements, 4 * features), BF16),
            shape_of((2, width_x, features)),
            shape_of((2, width_x, features)),
            shape_of((2, features, width)),
            shape_of((2, 8, width)),
            shape_of((4 * elements_y, features), BF16),
        ],
        scratch_shapes=[
            pltpu.VMEM((4, elements, features), F32),
            pltpu.VMEM((4, elements_y, features), F32),
        ],
        compiler_params=params(16),
        cost_estimate=cost(10_000_000, 3_000_000),
        name="complete",
    )(col, xlo, xhi, prev, later, ylo, yhi, yprev, ynext)

    chunk = elements // 3
    hidden = weights[0].shape[1]
    operands, operand_specs = [], []
    for item in weights:
        item = item if item.ndim == 2 else item.reshape(1, -1)
        operands.append(item)
        operand_specs.append(whole(item.shape))
    outgoing = pl.pallas_call(
        send_kernel,
        in_specs=[vmem] * 2,
        out_specs=hbm,
        out_shape=shape_of((slots, 4 * features), BF16),
        scratch_shapes=[
            pltpu.VMEM((slots, 4 * features), BF16),
            pltpu.SemaphoreType.DMA((4,)),
        ],
        compiler_params=params(16),
        cost_estimate=cost(2_000_000_000, 3_000_000),
        name="send",
    )(colbf, slot_ids)

    arrived = lax.all_to_all(
        outgoing.reshape(devices, capacity, 4 * features), ("face", "dom"),
        split_axis=0, concat_axis=0, tiled=True,
    ).reshape(slots, 4 * features)

    inc, near = pl.pallas_call(
        network_kernel,
        grid=(3,),
        in_specs=[
            smem,
            pl.BlockSpec((chunk, 4 * features), lambda g: (g, 0)),
            whole((4 * elements_y, features)),
            whole((packet, width)),
            whole((packet, width)),
        ]
        + operand_specs,
        out_specs=[
            pl.BlockSpec((chunk, 4 * features), lambda g: (g, 0)),
            whole((4 * elements_y, features)),
        ],
        out_shape=[
            shape_of((elements, 4 * features), BF16),
            shape_of((4 * elements_y, features), BF16),
        ],
        scratch_shapes=[pltpu.VMEM((4 * chunk, features), F32)],
        compiler_params=params(24),
        cost_estimate=cost(8 * elements * (4 * features * hidden + 3 * hidden * hidden), 4_000_000),
        name="network",
    )(sunlit, colbf, ghosts, prev, later, *operands)

    ylo2, yhi2 = pl.pallas_call(
        rims_kernel,
        in_specs=[vmem] * 5,
        out_specs=[vmem] * 2,
        out_shape=[shape_of((width, features))] * 2,
        scratch_shapes=[pltpu.VMEM((4, elements, features), F32)],
        compiler_params=params(16),
        cost_estimate=cost(10_000_000, 2_000_000),
        name="rims",
    )(inc, near, jacobian, prev, later)
    yprev2 = lax.ppermute(yhi2, "dom", shifted("dom", 1))
    ynext2 = lax.ppermute(ylo2, "dom", shifted("dom", -1))

    new_state = pl.pallas_call(
        final_kernel,
        grid=(elements_x // group,),
        in_specs=[
            pl.BlockSpec((4 * group, fields, levels, width), lambda g: (g, 0, 0, 0)),
            whole((elements, 4 * features)),
            whole((4 * elements_y, features)),
            whole((elements_x, elements_y)),
            whole((packet, width)),
            whole((packet, width)),
            whole((width, features)),
            whole((width, features)),
            whole((width, features)),
            whole((width, features)),
            whole((2, width_x, features)),
            whole((2, width_x, features)),
            whole((2, features, width)),
            whole((2, 8, width)),
        ],
        out_specs=pl.BlockSpec((fields, levels, 4 * group, width), lambda g: (0, 0, g, 0)),
        out_shape=shape_of((fields, levels, width_x, width)),
        scratch_shapes=[
            pltpu.VMEM((elements_x, width), F32),
            pltpu.VMEM((elements_x, width), F32),
            pltpu.VMEM((elements_x + 8, width), F32),
            pltpu.VMEM((2, width_x, features), F32),
            pltpu.VMEM((2, features, width), F32),
        ],
        compiler_params=params(20),
        cost_estimate=cost(1_000_000_000, 14_000_000),
        name="final",
    )(
        adv, inc, near, jacobian, prev, later, ylo2, yhi2, yprev2, ynext2, fy, ry, fx, rx
    )

    span_state = pl.pallas_call(
        lambda *refs: arrange_kernel(capacity, *refs),
        in_specs=[vmem],
        out_specs=hbm,
        out_shape=shape_of((4 * elements, features), BF16),
        scratch_shapes=[
            pltpu.VMEM((4, slots, features), F32),
            pltpu.VMEM((4 * (elements + capacity), features), F32),
            pltpu.VMEM((4 * elements, features), BF16),
            pltpu.VMEM((devices, features), jnp.int32),
            pltpu.SMEM((devices, features), jnp.int32),
            pltpu.SemaphoreType.DMA,
            pltpu.SemaphoreType.DMA((4,)),
        ],
        compiler_params=params(24),
        cost_estimate=cost(1_000_000, 3_000_000),
        name="arrange",
    )(arrived)
    return (new_state, span_state)


def solution(mesh):
    return jax.shard_map(
        on_device,
        mesh=mesh,
        in_specs=(
            P(None, None, "face", "dom"),
            P(None, None, "face", "dom"),
            P("face", "dom"),
            P("face", "dom"),
            P("face", "dom"),
        )
        + (P(),) * 14,
        out_specs=(P(None, None, "face", "dom"), P(("face", "dom"), None)),
        check_vma=False,
    )
```

```python
import jax
import jax.numpy as jnp
import numpy as np
from jax import lax
from jax.experimental import pallas as pl
from jax.experimental.pallas import tpu as pltpu
from jax.sharding import PartitionSpec as P

TIME_STEP = 0.1
LEAK_SLOPE = 0.15
F32 = jnp.float32
BF16 = jnp.bfloat16
HIGHEST = lax.Precision.HIGHEST
CELL_WEIGHTS = (1.0 / 6.0, 5.0 / 6.0, 5.0 / 6.0, 1.0 / 6.0)
MIB = 1024 * 1024
EMPTY = 1e30


def derivative_matrix():
    points = np.array([-1.0, -1.0 / np.sqrt(5.0), 1.0 / np.sqrt(5.0), 1.0])
    legendre = (5.0 * points**3 - 3.0 * points) / 2.0
    derivative = np.zeros((4, 4))
    for i in range(4):
        for k in range(4):
            if i != k:
                derivative[i, k] = legendre[i] / (legendre[k] * (points[i] - points[k]))
    derivative[0, 0] = -3.0
    derivative[3, 3] = 3.0
    return derivative


D = derivative_matrix()


def y_derivative_operand(width):
    full = np.kron(np.eye(width // 4), D.T).astype(np.float32)
    high = full.astype(jnp.bfloat16)
    low = (full - high.astype(np.float32)).astype(jnp.bfloat16)
    return np.concatenate([high, high, low], axis=0)


def iota(shape, dim):
    return lax.broadcasted_iota(jnp.int32, shape, dim)


def split(values):
    high = values.astype(BF16)
    return high, (values - high.astype(F32)).astype(BF16)


def copies_along_y(values):
    width = values.shape[-1]
    lane = iota((1, width), 1)
    up = ((lane & 3) == 3) & (lane < width - 1)
    down = ((lane & 3) == 0) & (lane > 0)
    return jnp.where(
        up, pltpu.roll(values, width - 1, 1), jnp.where(down, pltpu.roll(values, 1, 1), 0.0)
    )


def along_lanes(jac, width):
    expand = (iota((jac.shape[1], width), 1) >> 2) == iota((jac.shape[1], width), 0)
    return jnp.dot(jac, expand.astype(F32), precision=HIGHEST, preferred_element_type=F32)


def inner_reciprocals(mass):
    width = mass.shape[1]
    lane = iota(mass.shape, 1)
    row = iota(mass.shape, 0)
    inner = (lane > 0) & (lane < width - 1)
    inside = jnp.where(inner, 1.0 / mass, 0.0)
    shared = jnp.where(inner & (row > 0), 1.0 / (mass + pltpu.roll(mass, 1, 0)), 0.0)
    return inside, shared


def element_slopes(f):
    outer_gap, inner_gap = f[0] - f[3], f[1] - f[2]
    bend = (f[1] + f[2]) - (f[0] + f[3])
    odd = (D[0, 0] - D[0, 3]) / 2 * outer_gap + (D[0, 1] - D[0, 2]) / 2 * inner_gap
    even = (D[0, 1] + D[0, 2]) / 2 * bend
    odd_in = (D[1, 0] - D[1, 3]) / 2 * outer_gap - D[1, 2] / 2 * inner_gap
    even_in = D[1, 2] / 2 * bend
    return [odd + even, odd_in + even_in, odd_in - even_in, odd - even]


def edges_kernel(
    lit_ref, proglo_ref, proghi_ref, vello_ref, velhi_ref, jac_ref, dcat_ref, xlo_ref, xhi_ref,
    vf_ref,
):
    elements_x, elements_y = jac_ref.shape
    fields, levels, _, width = proglo_ref.shape
    features = fields * levels
    jac = jac_ref[...]
    mass = along_lanes(jac, width)
    joined = mass + copies_along_y(mass)
    inside, _ = inner_reciprocals(joined)
    lit = lit_ref[0, 0].astype(F32)
    sides = ((proglo_ref, vello_ref, xlo_ref), (proghi_ref, velhi_ref, xhi_ref))
    for side, (prog_ref, vel_ref, out_ref) in enumerate(sides):
        p = side * (elements_x - 1)
        lines = prog_ref.shape[2]
        prog = prog_ref.reshape(features * lines, width)
        first = side * (lines - 4)
        f = [prog[pl.ds(first + k, features, stride=lines), :] for k in range(4)]
        vlines = vel_ref.shape[2]
        vf_ref[...] = vel_ref[...].astype(F32).reshape(2 * levels * vlines, width)
        slopes = element_slopes(f)
        turned, moved = [], []
        for node in (3 * side, 1 + side):
            row = node + side * (vlines - 4)
            vx = vf_ref[pl.ds(row, levels, stride=vlines), :]
            vy = vf_ref[pl.ds(levels * vlines + row, levels, stride=vlines), :]
            high, low = split(f[node])
            sy = jnp.dot(
                jnp.concatenate([high, low, high], axis=1), dcat_ref[...],
                preferred_element_type=F32,
            )
            vx = jnp.concatenate([vx] * fields, axis=0)
            vy = jnp.concatenate([vy] * fields, axis=0)
            line = (vx * slopes[node] + vy * sy) * (-TIME_STEP * jnp.sqrt(mass[p : p + 1]))
            line = line + copies_along_y(line)
            moved.append(line)
            turned.append(line.T)
        out_ref[0:features, :] = moved[0]
        out_ref[features : 2 * features, :] = CELL_WEIGHTS[0] * f[3 * side] + CELL_WEIGHTS[1] * (
            f[1 + side] + moved[1] * inside[p : p + 1]
        )
        out_ref[2 * features : 2 * features + 16, :] = jnp.concatenate(
            [
                turned[0][0:1],
                turned[0][width - 1 : width],
                joined[p : p + 1],
                jnp.broadcast_to(jac[p : p + 1, 0:1], (1, width)),
                jnp.broadcast_to(jac[p : p + 1, elements_y - 1 : elements_y], (1, width)),
                turned[1][0:1],
                turned[1][width - 1 : width],
                jnp.broadcast_to(lit, (1, width)),
                mass[p : p + 1],
                jnp.zeros((7, width), F32),
            ],
            axis=0,
        )


def dynamics_kernel(
    prog_hbm, vel_ref, jac_ref, dcat_ref, adv_ref, ylo_ref, yhi_ref, prog_ref,
    sy3_ref, vf3_ref, pf3_ref, scale_ref, inside_ref, shared_ref, zlo_ref, zhi_ref, sems,
):
    _, levels, width_x, width = prog_ref.shape
    tile = sy3_ref.shape[0] // 2
    steps = levels // tile
    elements_x, elements_y = jac_ref.shape
    features = zlo_ref.shape[0]
    planes = 2 * tile
    pitch = sy3_ref.shape[1]
    sy_ref = sy3_ref.reshape(planes * pitch, width)
    vf_ref = vf3_ref.reshape(planes * pitch, width)
    pf_ref = pf3_ref.reshape(planes * pitch, width)

    def arrival(step):
        at = pl.ds(step * tile, tile)
        return pltpu.make_async_copy(prog_hbm.at[:, at], prog_ref.at[:, at], sems.at[step])

    for step in range(steps):
        arrival(step).start()

    mass = along_lanes(jac_ref[...], width)
    scale_ref[...] = -TIME_STEP * jnp.sqrt(mass)
    inside, shared = inner_reciprocals(mass + copies_along_y(mass))
    inside_ref[...] = inside
    shared_ref[...] = shared

    def one_tile(step):
        level = pl.ds(pl.multiple_of(step * tile, tile), tile)
        vf3_ref[:, 0:width_x, :] = vel_ref[:, pl.ds(step * tile, tile)].astype(F32).reshape(
            planes, width_x, width
        )
        piece = planes // 4
        for at in range(4):
            first = at * piece
            values = prog_ref[first // tile, pl.ds(step * tile + first % tile, piece)]
            pf3_ref[first : first + piece, 0:width_x, :] = values
            high, low = split(values.reshape(piece * width_x, width))
            sy3_ref[first : first + piece, 0:width_x, :] = jnp.dot(
                jnp.concatenate([high, low, high], axis=1), dcat_ref[...], preferred_element_type=F32
            ).reshape(piece, width_x, width)

        lane = iota((tile, width), 1)

        def rims(lines):
            first, second, third = lines
            a = pltpu.roll(first, 1, 1)
            b = pltpu.roll(second, 2, 1)
            c = pltpu.roll(third, 3, 1)

            def pick(base):
                return jnp.where(
                    lane == base, first,
                    jnp.where(
                        lane == (base + 1) % width, a,
                        jnp.where(
                            lane == (base + 2) % width, b, jnp.where(lane == (base + 3) % width, c, 0.0)
                        ),
                    ),
                )

            return pick(0), pick(width - 1)

        def element(p, carry):
            scale = scale_ref[p : p + 1, :]
            inside = inside_ref[p : p + 1, :]
            shared = shared_ref[p : p + 1, :]
            shift = (4 * p + width - 1) % width
            vx = [vf_ref[pl.ds(4 * p + k, tile, stride=pitch), :] for k in range(4)]
            vy = [
                vf_ref[pl.ds(tile * pitch + 4 * p + k, tile, stride=pitch), :] for k in range(4)
            ]
            out = []
            for v in range(2):
                last_e, last_f, z_low, z_high = carry[4 * v : 4 * v + 4]
                base = v * tile * pitch + 4 * p
                f = [pf_ref[pl.ds(base + k, tile, stride=pitch), :] for k in range(4)]
                sy = [sy_ref[pl.ds(base + k, tile, stride=pitch), :] for k in range(4)]
                sx = element_slopes(f)
                e = []
                for k in range(4):
                    moved = (vx[k] * sx[k] + vy[k] * sy[k]) * scale
                    e.append(moved + copies_along_y(moved))
                joined = last_e + e[0]
                gain = joined * shared
                adv_ref[4 * p, v, level, :] = f[0] + gain
                adv_ref[4 * p + 1, v, level, :] = f[1] + e[1] * inside
                adv_ref[4 * p + 2, v, level, :] = f[2] + e[2] * inside

                if p > 0:
                    adv_ref[4 * p - 1, v, level, :] = last_f + gain

                low, high = rims((joined, e[1], e[2]))
                out += [
                    e[3], f[3],
                    z_low + pltpu.roll(low, shift, 1), z_high + pltpu.roll(high, shift, 1),
                ]
            return tuple(out)

        zero = jnp.zeros((tile, width), F32)
        final = (zero,) * 8
        for p in range(elements_x):
            final = element(p, final)
        for v in range(2):
            last_e, last_f, z_low, z_high = final[4 * v : 4 * v + 4]
            at = pl.ds(pl.multiple_of(v * levels + tile * step, tile), tile)
            adv_ref[width_x - 1, v, level, :] = last_f
            zlo_ref[at, :] = jnp.where(
                lane == width_x - 1, pltpu.roll(last_e, width_x - 1, 1), z_low
            )
            zhi_ref[at, :] = pltpu.roll(
                jnp.where(lane == width_x - 2, pltpu.roll(last_e, width_x - 1, 1), z_high), 1, 1
            )

    @pl.loop(0, steps)
    def _(step):
        arrival(step).wait()
        one_tile(step)

    jac = jac_ref[...]
    ylo_ref[...] = zlo_ref[...].T
    yhi_ref[...] = zhi_ref[...].T
    for ref, q in ((ylo_ref, 0), (yhi_ref, elements_y - 1)):
        ref[width_x : width_x + elements_x, :] = jnp.broadcast_to(
            jac[:, q : q + 1], (elements_x, features)
        )


def cells_kernel(capacity, devices, adv_ref, span_ref, col_ref, slot_ref):
    group = adv_ref.shape[0] // 4
    width = adv_ref.shape[3]
    features = adv_ref.shape[1] * adv_ref.shape[2]
    elements_x, elements_y = span_ref.shape
    elements = elements_x * elements_y

    @pl.when(pl.program_id(0) == 0)
    def _():
        lane = iota((elements_y, elements), 1)
        tiled = lax.rem(lane, elements_y) == iota((elements_y, elements), 0)
        spread = jnp.dot(
            span_ref[...].astype(F32).astype(BF16), tiled.astype(BF16), preferred_element_type=F32
        )
        start = iota((elements_x, elements), 0) * elements_y
        at = iota((elements_x, elements), 1)
        own = (at >= start) & (at < start + elements_y)
        target = jnp.sum(jnp.where(own, spread, 0.0), axis=0, keepdims=True)
        chosen = jnp.where(
            target == iota((devices, elements), 0).astype(F32), 1.0, 0.0
        )
        before = iota((elements, elements), 0) < iota((elements, elements), 1)
        earlier = jnp.dot(
            chosen.astype(BF16), before.astype(BF16), preferred_element_type=F32
        )
        rank = jnp.sum(chosen * earlier, axis=0, keepdims=True)
        slot_ref[...] = (target * capacity + rank).astype(jnp.int32)

    select = select_cells(elements_y, width)
    for p in range(group):
        for a in range(2):
            line = adv_ref[4 * p + 2 * a] * CELL_WEIGHTS[2 * a]
            line += adv_ref[4 * p + 2 * a + 1] * CELL_WEIGHTS[2 * a + 1]
            low, high = cells_of_line(line.reshape(features, width), select)
            at = slice(p * elements_y, (p + 1) * elements_y)
            col_ref[2 * a, at, :] = low
            col_ref[2 * a + 1, at, :] = high


def select_cells(elements_y, width):
    shape = (2 * elements_y, width)
    row, lane = iota(shape, 0), iota(shape, 1)
    wanted = jnp.where(row < elements_y, 4 * row, 4 * (row - elements_y) + 2)
    return (lane == wanted).astype(BF16)


def cells_of_line(line, select):
    features, width = line.shape
    inner = (iota((1, width), 1) & 3)
    line = line * jnp.where((inner == 0) | (inner == 3), 1.0 / 6.0, 5.0 / 6.0)
    line = line + pltpu.roll(line, width - 1, 1)
    high, low = split(line)
    both = lax.dot_general(
        select, jnp.concatenate([high, low], axis=0), (((1,), (1,)), ((), ())),
        preferred_element_type=F32,
    )
    cells = both[:, :features] + both[:, features:]
    half = select.shape[0] // 2
    return cells[:half], cells[half:]


def corners_kernel(width_x, elements_x, ylo_ref, yhi_ref, prev_ref, next_ref, ylo_out, yhi_out):
    tail = prev_ref.shape[0] - 16
    spare = width_x + elements_x
    for side, (ref, out) in enumerate(((ylo_ref, ylo_out), (yhi_ref, yhi_out))):
        row = iota(ref.shape, 0)
        values = ref[...]
        for k, (packet, x) in enumerate(((prev_ref, 0), (next_ref, width_x - 1))):
            rim = packet[tail + side : tail + side + 1, :]
            mass = packet[tail + 3 + side : tail + 4 + side, :]
            inner = packet[tail + 5 + side : tail + 6 + side, :]
            values = values + jnp.where(row == x, rim, 0.0)
            values = jnp.where(row == spare + k, mass, values)
            values = jnp.where(row == spare + 2 + k, inner, values)
        out[...] = values


def complete_kernel(
    width_x, elements_x,
    col_ref, xlo_ref, xhi_ref, prev_ref, next_ref, ylo_ref, yhi_ref, yprev_ref,
    ynext_ref, colbf_ref, fy_ref, ry_ref, fx_ref, rx_ref, ghost_ref, work_ref, cell_ref,
):
    _, elements, features = col_ref.shape
    tail = 2 * features
    ghost_fixes = []
    elements_y = elements // elements_x
    width = xlo_ref.shape[1]
    work_ref[...] = col_ref[...]
    select = select_cells(elements_y, width)
    lane = iota((1, width), 1)
    inner = (lane > 0) & (lane < width - 1)
    for side, (own, other) in enumerate(((ylo_ref, yprev_ref), (yhi_ref, ynext_ref))):
        total = own[...] + other[...]
        mass = total[width_x : width_x + elements_x]
        row = iota(mass.shape, 0)
        spare = width_x + elements_x
        before = jnp.where(row == 0, total[spare : spare + 1], pltpu.roll(mass, 1, 0))
        after = jnp.where(
            row == elements_x - 1, total[spare + 1 : spare + 2], pltpu.roll(mass, elements_x - 1, 0)
        )
        inside = 1.0 / mass
        ry_ref[side, pl.ds(0, elements_x, stride=4), :] = 1.0 / (mass + before)
        ry_ref[side, pl.ds(1, elements_x, stride=4), :] = inside
        ry_ref[side, pl.ds(2, elements_x, stride=4), :] = inside
        ry_ref[side, pl.ds(3, elements_x, stride=4), :] = 1.0 / (mass + after)
        fy_ref[side] = total[:width_x] * ry_ref[side]
        ghost_fixes.append(total[spare + 2 : spare + 4] / total[spare : spare + 2])
        fixes = [fy_ref[side, pl.ds(k, elements_x, stride=4), :] for k in range(4)]
        at = pl.ds(side * (elements_y - 1), elements_x, stride=elements_y)
        for a in range(2):
            added = CELL_WEIGHTS[2 * a] * fixes[2 * a] + CELL_WEIGHTS[2 * a + 1] * fixes[2 * a + 1]
            k = 2 * a + side
            work_ref[k, at, :] = work_ref[k, at, :] + CELL_WEIGHTS[0] * added
    for side, (own, other) in enumerate(((xlo_ref, prev_ref), (xhi_ref, next_ref))):
        mass = own[tail + 2 : tail + 3, :] + other[tail + 2 : tail + 3, :]
        reciprocal = jnp.where(inner, 1.0 / mass, 0.0)
        rx_ref[side] = jnp.broadcast_to(reciprocal, (8, width))
        fix = (own[:features] + other[:features]) * reciprocal
        fx_ref[side] = fix
        low, high = cells_of_line(CELL_WEIGHTS[0] * fix, select)
        at = slice(side * (elements_x - 1) * elements_y, (side * (elements_x - 1) + 1) * elements_y)
        work_ref[2 * side, at, :] = work_ref[2 * side, at, :] + low
        work_ref[2 * side + 1, at, :] = work_ref[2 * side + 1, at, :] + high
        line = other[features : 2 * features] + CELL_WEIGHTS[0] * fix
        cell_ref[2 * side], cell_ref[2 * side + 1] = cells_of_line(line, select)
        for end in range(2):
            x = side * (width_x - 1)
            added = CELL_WEIGHTS[0] * fy_ref[end, x : x + 1, :]
            added = added + CELL_WEIGHTS[1] * ghost_fixes[end][side : side + 1]
            q = end * (elements_y - 1)
            cell_ref[2 * side + end, q : q + 1, :] = (
                cell_ref[2 * side + end, q : q + 1, :] + CELL_WEIGHTS[0] * added
            )
    for k in range(4):
        ghost_ref[k * elements_y : (k + 1) * elements_y, :] = cell_ref[k].astype(BF16)
    for k in range(4):
        colbf_ref[:, k * features : (k + 1) * features] = work_ref[k].astype(BF16)


def send_kernel(colbf_ref, slot_ref, out_hbm, out_ref, sems):
    elements = colbf_ref.shape[0]
    slots = out_ref.shape[0]
    pieces = sems.shape[0]
    piece = slots // pieces
    copies = []
    for part in range(pieces):
        at = pl.ds(part * piece, piece)
        chosen = (iota((piece, elements), 0) + part * piece) == slot_ref[...]
        chosen = jnp.where(chosen, 1.0, 0.0)
        filled = jnp.max(chosen, axis=1, keepdims=True)
        moved = jnp.dot(chosen.astype(BF16), colbf_ref[...], preferred_element_type=F32)
        out_ref[at, :] = jnp.where(filled > 0.0, moved, EMPTY).astype(BF16)
        copies.append(pltpu.make_async_copy(out_ref.at[at], out_hbm.at[at], sems.at[part]))
        copies[-1].start()
    for copy in copies:
        copy.wait()


def dense(inputs, weight_ref, bias_ref):
    return jnp.dot(inputs, weight_ref[...], preferred_element_type=F32) + bias_ref[...]


def leaky(values):
    return jnp.maximum(values, LEAK_SLOPE * values).astype(BF16)


def network_kernel(
    lit_ref, col_ref, ghost_ref, prev_ref, next_ref, w1, b1, w2, b2, w3, b3, w4, b4, s1, c1, s2,
    c2, s3, c3, inc_ref, ghost_inc_ref, total_ref,
):
    rows = col_ref.shape[0]
    features = col_ref.shape[1] // 4
    inputs = jnp.concatenate(
        [col_ref[:, k * features : (k + 1) * features] for k in range(4)], axis=0
    )
    total_ref[...] = primary(inputs, w1, b1, w2, b2, w3, b3, w4, b4)

    @pl.when(lit_ref[0, 0] != 0)
    def _():
        total_ref[...] += lit_ref[0, 0].astype(F32) * solar(inputs, s1, c1, s2, c2, s3, c3)

    for k in range(4):
        inc_ref[:, k * features : (k + 1) * features] = total_ref[
            k * rows : (k + 1) * rows, :
        ].astype(BF16)

    @pl.when(pl.program_id(0) == 0)
    def _():
        near = ghost_ref[...]
        tail = 2 * features + 7
        row = iota(near.shape, 0)
        lit = jnp.where(
            row < near.shape[0] // 2, prev_ref[tail : tail + 1, :], next_ref[tail : tail + 1, :]
        )
        near_inc = primary(near, w1, b1, w2, b2, w3, b3, w4, b4)
        near_inc = near_inc + lit * solar(near, s1, c1, s2, c2, s3, c3)
        ghost_inc_ref[...] = near_inc.astype(BF16)


def primary(inputs, w1, b1, w2, b2, w3, b3, w4, b4):
    hidden = leaky(dense(inputs, w1, b1))
    hidden = leaky(dense(hidden, w2, b2))
    hidden = leaky(dense(hidden, w3, b3))
    return dense(hidden, w4, b4)


def solar(inputs, s1, c1, s2, c2, s3, c3):
    hidden = leaky(dense(inputs, s1, c1))
    hidden = leaky(dense(hidden, s2, c2))
    return dense(hidden, s3, c3)


def spread_operand(mass_line, elements_y):
    width = mass_line.shape[1]
    shape = (2 * elements_y, width)
    row, lane = iota(shape, 0), iota(shape, 1)
    upper = row >= elements_y
    q = jnp.where(upper, row - elements_y, row)
    b = jnp.where(upper, 1, 0)
    own = (lane >> 1) == 2 * q + b
    copy = lane == jnp.where(upper, 4 * q + 4, 4 * q - 1)
    weights = jnp.where(
        own, mass_line, jnp.where(copy, copies_along_y(mass_line), 0.0)
    )
    high, low = split(weights)
    return jnp.concatenate([high, low], axis=0)


def spread_line(inc_ref, p, a, operand, elements_y):
    features = inc_ref.shape[1] // 4
    start = p * elements_y
    if not isinstance(p, int):
        start = pl.multiple_of(start, elements_y)
    at = pl.ds(start, elements_y)
    cells = [
        inc_ref[at, (2 * a + b) * features : (2 * a + b + 1) * features] for b in range(2)
    ]
    return spread_cells(cells, operand)


def spread_cells(cells, operand):
    return lax.dot_general(
        jnp.concatenate(cells + cells, axis=0), operand, (((0,), (0,)), ((), ())),
        preferred_element_type=F32,
    )


def rims_kernel(inc_ref, near_ref, jac_ref, prev_ref, next_ref, ylo_ref, yhi_ref, wide_ref):
    elements_x, elements_y = jac_ref.shape
    features = near_ref.shape[1]
    width_x = 4 * elements_x
    tail = 2 * features
    for k in range(4):
        wide_ref[k] = inc_ref[:, k * features : (k + 1) * features].astype(F32)
    near = near_ref[...].astype(F32)
    for side, ref in enumerate((ylo_ref, yhi_ref)):
        q = side * (elements_y - 1)
        column = jac_ref[:, q : q + 1]
        at = pl.ds(q, elements_x, stride=elements_y)
        first = column * wide_ref[side, at, :]
        second = column * wide_ref[2 + side, at, :]
        ghosts = []
        for k, packet in enumerate((prev_ref, next_ref)):
            cell = (2 * k + side) * elements_y + q
            mass = packet[tail + 3 + side : tail + 4 + side, :]
            ghosts.append(mass * near[cell : cell + 1])
        row = iota(first.shape, 0)
        ref[pl.ds(0, elements_x, stride=4), :] = first + jnp.where(
            row == 0, ghosts[0], pltpu.roll(second, 1, 0)
        )
        ref[pl.ds(1, elements_x, stride=4), :] = first
        ref[pl.ds(2, elements_x, stride=4), :] = second
        ref[pl.ds(3, elements_x, stride=4), :] = second + jnp.where(
            row == elements_x - 1, ghosts[1], pltpu.roll(first, elements_x - 1, 0)
        )
        ref[width_x:, :] = jnp.zeros((ref.shape[0] - width_x, features), F32)


def final_kernel(
    adv_ref, inc_ref, near_ref, jac_ref, prev_ref, next_ref, ylo_ref, yhi_ref, yprev_ref,
    ynext_ref, fy_ref, ry_ref, fx_ref, rx_ref, out_ref, mass_ref, inside_ref, shared_ref,
    rim_ref, edge_ref,
):
    step = pl.program_id(0)
    elements_x, elements_y = jac_ref.shape
    width_x = 4 * elements_x
    lines = adv_ref.shape[0]
    group = lines // 4
    width = adv_ref.shape[3]
    features = adv_ref.shape[1] * adv_ref.shape[2]

    @pl.when(step == 0)
    def _():
        mass = along_lanes(jac_ref[...], width)
        mass_ref[...] = mass
        inside, shared = inner_reciprocals(mass + copies_along_y(mass))
        inside_ref[...] = inside
        shared_ref[0:elements_x, :] = shared
        shared_ref[elements_x:, :] = jnp.zeros((8, width), F32)
        for side, (own, other) in enumerate(((ylo_ref, yprev_ref), (yhi_ref, ynext_ref))):
            rim_ref[side] = fy_ref[side] + (own[0:width_x, :] + other[0:width_x, :]) * ry_ref[side]
        for side, packet in enumerate((prev_ref, next_ref)):
            p = side * (elements_x - 1)
            own = spread_line(
                inc_ref, p, side, spread_operand(mass[p : p + 1], elements_y), elements_y
            )
            tail = 2 * features + 8
            at = 2 * side * elements_y
            other = spread_cells(
                [near_ref[at : at + 2 * elements_y, :]],
                spread_operand(packet[tail : tail + 1, :], elements_y),
            )
            edge_ref[side] = fx_ref[side] + (own + other) * rx_ref[side, 0:1, :]

    out = out_ref.reshape(features * lines, width)
    row = iota((16, width), 0)
    lane = iota((16, width), 1)
    place = (((row < 2) & (lane == 0)) | ((row >= 2) & (row < 4) & (lane == width - 1))).astype(BF16)

    def rim_of(x):
        low = rim_ref[0, pl.ds(x, 1), :]
        high = rim_ref[1, pl.ds(x, 1), :]
        parts = jnp.where(row < 2, low, high)
        rough = parts.astype(BF16).astype(F32)
        rest = parts - rough
        stacked = jnp.where((row == 0) | (row == 2), rough, jnp.where(row < 4, rest, 0.0))
        return lax.dot_general(
            stacked.astype(BF16), place, (((0,), (0,)), ((), ())), preferred_element_type=F32
        )

    def line_of(p, a):
        operand = spread_operand(mass_ref[pl.ds(p, 1), :], elements_y)
        return spread_line(inc_ref, p, a, operand, elements_y)

    def store(at, values):
        out[pl.ds(at, features, stride=lines), :] = adv_ref[at].reshape(features, width) + values

    first = step * group
    before = line_of(jnp.maximum(first - 1, 0), 1)
    here = line_of(first, 0)
    joint = (before + here) * shared_ref[pl.ds(first, 1), :] + rim_of(4 * first)
    for k in range(group):
        p = first + k
        inside = inside_ref[pl.ds(p, 1), :]
        store(4 * k, joint)
        store(4 * k + 1, here * inside + rim_of(4 * p + 1))
        there = line_of(p, 1)
        store(4 * k + 2, there * inside + rim_of(4 * p + 2))
        here = line_of(jnp.minimum(p + 1, elements_x - 1), 0)
        joint = (there + here) * shared_ref[pl.ds(p + 1, 1), :] + rim_of(4 * p + 3)
        store(4 * k + 3, joint)

    @pl.when(step == 0)
    def _():
        at = pl.ds(0, features, stride=lines)
        out[at, :] = out[at, :] + edge_ref[0]

    @pl.when(step == pl.num_programs(0) - 1)
    def _():
        at = pl.ds(lines - 1, features, stride=lines)
        out[at, :] = out[at, :] + edge_ref[1]


def arrange_kernel(
    capacity, data_ref, out_hbm, wide_ref, rows_ref, out_ref, vector_ref, start_ref, sem, sems
):
    devices = vector_ref.shape[0]
    slots = data_ref.shape[0]
    features = data_ref.shape[1] // 4
    elements = out_ref.shape[0] // 4
    filled = jnp.where(data_ref[:, 0:features].astype(F32) < 0.5 * EMPTY, 1.0, 0.0).astype(BF16)
    before = iota((devices, slots), 1) < iota((devices, slots), 0) * capacity
    starts = jnp.dot(
        jnp.where(before, 1.0, 0.0).astype(BF16), filled, preferred_element_type=F32
    )
    vector_ref[...] = jnp.clip(starts, 0.0, float(elements)).astype(jnp.int32)
    copy = pltpu.make_async_copy(vector_ref, start_ref, sem)
    copy.start()
    for k in range(4):
        wide_ref[k] = data_ref[:, k * features : (k + 1) * features].astype(F32)
    copy.wait()

    def one(s, carry):
        start = start_ref[s, 0]
        for k in range(4):
            rows_ref[pl.ds(4 * start + k, capacity, stride=4), :] = wide_ref[
                k, pl.ds(s * capacity, capacity), :
            ]
        return carry

    lax.fori_loop(0, devices, one, 0, unroll=4)
    pieces = sems.shape[0]
    piece = 4 * elements // pieces
    copies = []
    for part in range(pieces):
        at = pl.ds(part * piece, piece)
        out_ref[at, :] = rows_ref[at, :].astype(BF16)
        copies.append(pltpu.make_async_copy(out_ref.at[at], out_hbm.at[at], sems.at[part]))
        copies[-1].start()
    for copy in copies:
        copy.wait()


def params(mib):
    return pltpu.CompilerParams(vmem_limit_bytes=mib * MIB)


def whole(shape):
    return pl.BlockSpec(shape, lambda *_: (0,) * len(shape))


def cost(flops, bytes_accessed):
    return pl.CostEstimate(flops=flops, bytes_accessed=bytes_accessed, transcendentals=0)


def shape_of(shape, dtype=F32):
    return jax.ShapeDtypeStruct(shape, dtype)


def shifted(axis, by):
    count = lax.axis_size(axis)
    return [(i, (i + by) % count) for i in range(count)]


def edges_call(sunlit, prognostic, velocity, jacobian):
    fields, levels, width_x, width = prognostic.shape
    features = fields * levels
    last = width_x // 8 - 1, width_x // 16 - 1
    dcat = jnp.asarray(y_derivative_operand(width))
    return pl.pallas_call(
        edges_kernel,
        grid=(1,),
        in_specs=[
            pl.BlockSpec(memory_space=pltpu.SMEM),
            pl.BlockSpec((fields, levels, 8, width), lambda g: (0, 0, 0, 0)),
            pl.BlockSpec((fields, levels, 8, width), lambda g: (0, 0, last[0], 0)),
            pl.BlockSpec((2, levels, 16, width), lambda g: (0, 0, 0, 0)),
            pl.BlockSpec((2, levels, 16, width), lambda g: (0, 0, last[1], 0)),
            whole(jacobian.shape),
            whole((3 * width, width)),
        ],
        out_specs=[whole((2 * features + 16, width))] * 2,
        out_shape=[shape_of((2 * features + 16, width))] * 2,
        scratch_shapes=[pltpu.VMEM((2 * levels * 16, width), F32)],
        compiler_params=params(58),
        cost_estimate=cost(50_000_000, 2_000_000),
        name="edges",
    )(sunlit, prognostic, prognostic, velocity, velocity, jacobian, dcat)


def dynamics_call(prognostic, velocity, jacobian):
    fields, levels, width_x, width = prognostic.shape
    elements_x, elements_y = jacobian.shape
    features = fields * levels
    tile = 8
    dcat = jnp.asarray(y_derivative_operand(width))
    hbm = pl.BlockSpec(memory_space=pltpu.HBM)
    vmem = pl.BlockSpec(memory_space=pltpu.VMEM)
    return pl.pallas_call(
        dynamics_kernel,
        in_specs=[hbm, vmem, vmem, vmem],
        out_specs=[vmem] * 3,
        out_shape=[
            shape_of((width_x, fields, levels, width)),
            shape_of((width, features)),
            shape_of((width, features)),
        ],
        scratch_shapes=[
            pltpu.VMEM(prognostic.shape, F32),
            pltpu.VMEM((2 * tile, width_x + 8, width), F32),
            pltpu.VMEM((2 * tile, width_x + 8, width), F32),
            pltpu.VMEM((2 * tile, width_x + 8, width), F32),
            pltpu.VMEM((elements_x, width), F32),
            pltpu.VMEM((elements_x, width), F32),
            pltpu.VMEM((elements_x, width), F32),
            pltpu.VMEM((features, width), F32),
            pltpu.VMEM((features, width), F32),
            pltpu.SemaphoreType.DMA((levels // tile,)),
        ],
        compiler_params=params(42),
        cost_estimate=cost(2_000_000_000, 16_000_000),
        name="dynamics",
    )(prognostic, velocity, jacobian, dcat)


def on_device(
    prognostic,
    velocity,
    jacobian,
    element_span,
    sunlit,
    *weights,
):
    fields, levels, width_x, width = prognostic.shape
    elements_x, elements_y = jacobian.shape
    features = fields * levels
    elements = elements_x * elements_y
    devices = lax.axis_size("face") * lax.axis_size("dom")
    capacity = max(2, 2 * elements // devices)
    slots = devices * capacity
    packet = 2 * features + 16
    vmem = pl.BlockSpec(memory_space=pltpu.VMEM)
    hbm = pl.BlockSpec(memory_space=pltpu.HBM)
    smem = pl.BlockSpec(memory_space=pltpu.SMEM)

    xlo, xhi = edges_call(sunlit, prognostic, velocity, jacobian)
    adv, ylo, yhi = dynamics_call(prognostic, velocity, jacobian)

    group = 4
    col, slot_ids = pl.pallas_call(
        lambda *refs: cells_kernel(capacity, devices, *refs),
        grid=(elements_x // group,),
        in_specs=[
            pl.BlockSpec((4 * group, fields, levels, width), lambda g: (g, 0, 0, 0)),
            whole((elements_x, elements_y)),
        ],
        out_specs=[
            pl.BlockSpec((4, group * elements_y, features), lambda g: (0, g, 0)),
            whole((1, elements)),
        ],
        out_shape=[
            shape_of((4, elements, features)),
            shape_of((1, elements), jnp.int32),
        ],
        compiler_params=params(20),
        cost_estimate=cost(1_000_000_000, 8_000_000),
        name="cells",
    )(adv, element_span)

    prev = lax.ppermute(xhi, "face", shifted("face", 1))
    later = lax.ppermute(xlo, "face", shifted("face", -1))
    ylo, yhi = pl.pallas_call(
        lambda *refs: corners_kernel(width_x, elements_x, *refs),
        in_specs=[vmem] * 4,
        out_specs=[vmem] * 2,
        out_shape=[shape_of((width, features))] * 2,
        compiler_params=params(12),
        name="corners",
    )(ylo, yhi, prev, later)
    yprev = lax.ppermute(yhi, "dom", shifted("dom", 1))
    ynext = lax.ppermute(ylo, "dom", shifted("dom", -1))

    colbf, fy, ry, fx, rx, ghosts = pl.pallas_call(
        lambda *refs: complete_kernel(width_x, elements_x, *refs),
        in_specs=[vmem] * 9,
        out_specs=[vmem] * 6,
        out_shape=[
            shape_of((elements, 4 * features), BF16),
            shape_of((2, width_x, features)),
            shape_of((2, width_x, features)),
            shape_of((2, features, width)),
            shape_of((2, 8, width)),
            shape_of((4 * elements_y, features), BF16),
        ],
        scratch_shapes=[
            pltpu.VMEM((4, elements, features), F32),
            pltpu.VMEM((4, elements_y, features), F32),
        ],
        compiler_params=params(16),
        cost_estimate=cost(10_000_000, 3_000_000),
        name="complete",
    )(col, xlo, xhi, prev, later, ylo, yhi, yprev, ynext)

    chunk = elements // 3
    hidden = weights[0].shape[1]
    operands, operand_specs = [], []
    for item in weights:
        item = item if item.ndim == 2 else item.reshape(1, -1)
        operands.append(item)
        operand_specs.append(whole(item.shape))
    outgoing = pl.pallas_call(
        send_kernel,
        in_specs=[vmem] * 2,
        out_specs=hbm,
        out_shape=shape_of((slots, 4 * features), BF16),
        scratch_shapes=[
            pltpu.VMEM((slots, 4 * features), BF16),
            pltpu.SemaphoreType.DMA((4,)),
        ],
        compiler_params=params(16),
        cost_estimate=cost(2_000_000_000, 3_000_000),
        name="send",
    )(colbf, slot_ids)

    arrived = lax.all_to_all(
        outgoing.reshape(devices, capacity, 4 * features), ("face", "dom"),
        split_axis=0, concat_axis=0, tiled=True,
    ).reshape(slots, 4 * features)

    inc, near = pl.pallas_call(
        network_kernel,
        grid=(3,),
        in_specs=[
            smem,
            pl.BlockSpec((chunk, 4 * features), lambda g: (g, 0)),
            whole((4 * elements_y, features)),
            whole((packet, width)),
            whole((packet, width)),
        ]
        + operand_specs,
        out_specs=[
            pl.BlockSpec((chunk, 4 * features), lambda g: (g, 0)),
            whole((4 * elements_y, features)),
        ],
        out_shape=[
            shape_of((elements, 4 * features), BF16),
            shape_of((4 * elements_y, features), BF16),
        ],
        scratch_shapes=[pltpu.VMEM((4 * chunk, features), F32)],
        compiler_params=params(24),
        cost_estimate=cost(8 * elements * (4 * features * hidden + 3 * hidden * hidden), 4_000_000),
        name="network",
    )(sunlit, colbf, ghosts, prev, later, *operands)

    ylo2, yhi2 = pl.pallas_call(
        rims_kernel,
        in_specs=[vmem] * 5,
        out_specs=[vmem] * 2,
        out_shape=[shape_of((width, features))] * 2,
        scratch_shapes=[pltpu.VMEM((4, elements, features), F32)],
        compiler_params=params(16),
        cost_estimate=cost(10_000_000, 2_000_000),
        name="rims",
    )(inc, near, jacobian, prev, later)
    yprev2 = lax.ppermute(yhi2, "dom", shifted("dom", 1))
    ynext2 = lax.ppermute(ylo2, "dom", shifted("dom", -1))

    new_state = pl.pallas_call(
        final_kernel,
        grid=(elements_x // group,),
        in_specs=[
            pl.BlockSpec((4 * group, fields, levels, width), lambda g: (g, 0, 0, 0)),
            whole((elements, 4 * features)),
            whole((4 * elements_y, features)),
            whole((elements_x, elements_y)),
            whole((packet, width)),
            whole((packet, width)),
            whole((width, features)),
            whole((width, features)),
            whole((width, features)),
            whole((width, features)),
            whole((2, width_x, features)),
            whole((2, width_x, features)),
            whole((2, features, width)),
            whole((2, 8, width)),
        ],
        out_specs=pl.BlockSpec((fields, levels, 4 * group, width), lambda g: (0, 0, g, 0)),
        out_shape=shape_of((fields, levels, width_x, width)),
        scratch_shapes=[
            pltpu.VMEM((elements_x, width), F32),
            pltpu.VMEM((elements_x, width), F32),
            pltpu.VMEM((elements_x + 8, width), F32),
            pltpu.VMEM((2, width_x, features), F32),
            pltpu.VMEM((2, features, width), F32),
        ],
        compiler_params=params(20),
        cost_estimate=cost(1_000_000_000, 14_000_000),
        name="final",
    )(
        adv, inc, near, jacobian, prev, later, ylo2, yhi2, yprev2, ynext2, fy, ry, fx, rx
    )

    span_state = pl.pallas_call(
        lambda *refs: arrange_kernel(capacity, *refs),
        in_specs=[vmem],
        out_specs=hbm,
        out_shape=shape_of((4 * elements, features), BF16),
        scratch_shapes=[
            pltpu.VMEM((4, slots, features), F32),
            pltpu.VMEM((4 * (elements + capacity) + 8, features), F32),
            pltpu.VMEM((4 * elements, features), BF16),
            pltpu.VMEM((devices, features), jnp.int32),
            pltpu.SMEM((devices, features), jnp.int32),
            pltpu.SemaphoreType.DMA,
            pltpu.SemaphoreType.DMA((4,)),
        ],
        compiler_params=params(24),
        cost_estimate=cost(1_000_000, 3_000_000),
        name="arrange",
    )(arrived)
    return (new_state, span_state)


def solution(mesh):
    return jax.shard_map(
        on_device,
        mesh=mesh,
        in_specs=(
            P(None, None, "face", "dom"),
            P(None, None, "face", "dom"),
            P("face", "dom"),
            P("face", "dom"),
            P("face", "dom"),
        )
        + (P(),) * 14,
        out_specs=(P(None, None, "face", "dom"), P(("face", "dom"), None)),
        check_vma=False,
    )
```
